32 devices in a mesh: row: 8 (over y, x, core), col: 4 (over z).
Axes of the slice: x: 2, y: 2, z: 4, core: 2. Of those that a mesh axis runs over, the one named last changes fastest.
Arguments:
- mask_logits: float32 [1024, 512], P('row', 'col'), may hold values from -6 to 6
- target: float32 [1024, 512], P('row', 'col'), may hold values from 0 to 1
- weight: float32 [1024, 512], P('row', 'col'), may hold values from 0.004 to 10, as said below
- kernels: float32 [2, 12288], P(None, ('row', 'col')), may hold values from -3 to 3
Outputs:
- new_logits: float32 [1024, 512], P('row', 'col')
- loss_value: float32 [], replicated
The draws below stay inside these ranges and needn't reach their ends.
Inputs may be any that keep to these rules, and one draw needn't show every extreme that they name: `weight`: positive loss weights.
All inputs are finite; a program needn't handle non-finite values.
Results may differ from the reference program's by a relative error of at most 0.0003.
Values sent between devices are 32-bit elements; how exact they have to be, the bound alone decides.
No kernel may reach another device: no remote copies, remote signals or barrier semaphores. Data moves between devices by JAX's collectives and lax.ppermute only.
A program may use at most 64 MiB of HBM per device.

```python
import math
import jax
import jax.numpy as jnp
from jax import lax

PAD = 256
HALO = 64
KERNELS = 6
BAND = 32
CONDITIONS = 2
CORE = 128
ROWS = 1024
COLUMNS = 512
BANK_SIZE = 12288


def draw_weight(key, part):
    key_rows, key_cols, key_cells = jax.random.split(key, 3)
    row_ramp = jnp.exp(math.log(3.0) * jnp.arange(ROWS, dtype=jnp.float32) / ROWS)
    col_ramp = jnp.exp(math.log(3.0) * jnp.arange(COLUMNS, dtype=jnp.float32) / COLUMNS)
    spread = math.log(3.5)
    floor_value = 0.5
    row_scale = row_ramp * jnp.exp(jax.random.uniform(key_rows, (ROWS,), jnp.float32, 0.0, spread))
    col_scale = col_ramp * jnp.exp(jax.random.uniform(key_cols, (COLUMNS,), jnp.float32, 0.0, spread))
    cell_scale = jax.random.uniform(key_cells, (ROWS, COLUMNS), jnp.float32, floor_value, 1.0)
    return row_scale[:, None] * col_scale[None, :] * cell_scale / 40.0


def steps_of(own_key, dims, shards, least, top_value):
    factor_of = 1.0
    for dim, parts in shards:
        heights = jax.random.uniform(jax.random.fold_in(jax.random.fold_in(own_key, 6), dim), (parts,), jnp.float32, least / len(shards), top_value / len(shards))
        factor_of = factor_of * jnp.repeat(jnp.exp(heights), dims[dim] // parts).reshape((-1,) + (1,) * (len(dims) - 1 - dim))
    return factor_of


def normal_values(own_key, dims, scale, reach, cuts=(), kind=jnp.bfloat16):
    array = scale * jax.random.normal(own_key, dims, jnp.float32)
    if cuts:
        array = array * steps_of(own_key, dims, cuts, -0.22, 0.18)
    return jnp.clip(array, -reach, reach).astype(kind)


def setup_inputs(seed: int = 0) -> dict:
    key_of = jax.random.split(jax.random.key(seed), 5)
    return {
        "mask_logits": normal_values(key_of[0], (ROWS, COLUMNS), 1.5, 6.0, ((0, 8), (1, 4)), jnp.float32),
        "target": jnp.clip(1.0 * jax.random.uniform(key_of[1], (ROWS, COLUMNS), jnp.float32) ** steps_of(key_of[1], (ROWS, COLUMNS), ((0, 8), (1, 4)), -0.2, 0.2), 0.0, 1.0),
        "weight": draw_weight(jax.random.fold_in(key_of[4], 71), 0),
        "kernels": normal_values(key_of[3], (CONDITIONS, BANK_SIZE), 0.5, 3.0, ((1, 32),), jnp.float32),
    }


SHARPNESS = 6.0
THRESHOLD = 0.75
STEP = 0.5
EPSILON = 1e-06
DOSES = (1.0, 1.15)

def matmul(first, second):
    return jnp.matmul(first, second, precision=lax.Precision.HIGHEST, preferred_element_type=jnp.float32)

def cmatmul(first_re, first_im, second_re, second_im):
    return (matmul(first_re, second_re) - matmul(first_im, second_im), matmul(first_re, second_im) + matmul(first_im, second_re))

def dft_rows(band, pad_width):
    freq = jnp.arange(band, dtype=jnp.int32) - band // 2
    place = jnp.arange(pad_width, dtype=jnp.int32)
    turns = (freq[:, None] * place[None, :] % pad_width).astype(jnp.float32) * (2.0 * math.pi / pad_width)
    factor = 1.0 / math.sqrt(pad_width)
    return (jnp.cos(turns) * factor, -jnp.sin(turns) * factor)

def synthesize(spec_re, spec_im, wave_re, wave_im):
    left_re, left_im = cmatmul(wave_re.T, -wave_im.T, spec_re, spec_im)
    return cmatmul(left_re, left_im, wave_re, -wave_im)

def analyse(cell_re, cell_im, wave_re, wave_im):
    left_re, left_im = cmatmul(wave_re, wave_im, cell_re, cell_im)
    return cmatmul(left_re, left_im, wave_re.T, wave_im.T)

def tile_terms(padded_tile, kernel_re, kernel_im, wave_re, wave_im, dose, margin):
    mask_tile, target_tile, weight_tile = (padded_tile[0], padded_tile[1], padded_tile[2])
    pad_width = mask_tile.shape[0]
    core_width = pad_width - 2 * margin
    four_re, four_im = cmatmul(matmul(wave_re, mask_tile), matmul(wave_im, mask_tile), wave_re.T, wave_im.T)
    prod_re = four_re[None] * kernel_re - four_im[None] * kernel_im
    prod_im = four_re[None] * kernel_im + four_im[None] * kernel_re
    fields_re, fields_im = synthesize(prod_re, prod_im, wave_re, wave_im)
    intensity = lax.optimization_barrier(jnp.sum(fields_re * fields_re + fields_im * fields_im, axis=0))
    resist = jax.nn.sigmoid(SHARPNESS * (dose * intensity - THRESHOLD))
    error_map = resist - target_tile
    inner = (weight_tile * error_map * error_map)[margin:margin + core_width, margin:margin + core_width]
    tile_loss = jnp.sum(inner)
    slope_map = 2.0 * SHARPNESS * dose * weight_tile * error_map * resist * (1.0 - resist)
    back_re, back_im = analyse(slope_map[None] * fields_re, slope_map[None] * fields_im, wave_re, wave_im)
    sum_re = lax.optimization_barrier(jnp.sum(kernel_re * back_re + kernel_im * back_im, axis=0))
    sum_im = lax.optimization_barrier(jnp.sum(kernel_re * back_im - kernel_im * back_re, axis=0))
    core_re = wave_re[:, margin:margin + core_width]
    core_im = wave_im[:, margin:margin + core_width]
    left_re, left_im = cmatmul(core_re.T, -core_im.T, sum_re, sum_im)
    real_part = matmul(left_re, core_re) + matmul(left_im, core_im)
    return (2.0 * real_part, tile_loss)

def reference(mask_logits, target, weight, kernels):
    mask_cells = jax.nn.sigmoid(mask_logits)
    stacked = jnp.pad(jnp.stack([mask_cells, target, weight]), ((0, 0), (HALO, HALO), (HALO, HALO)))
    wave_re, wave_im = dft_rows(BAND, PAD)
    banks = kernels.reshape(CONDITIONS, 2, KERNELS, BAND, BAND)
    tile_rows = ROWS // CORE
    tile_cols = COLUMNS // CORE

    def one_tile(tile_index):
        row_start = tile_index // tile_cols * CORE
        col_start = tile_index % tile_cols * CORE
        padded_tile = lax.dynamic_slice(stacked, (jnp.int32(0), row_start.astype(jnp.int32), col_start.astype(jnp.int32)), (3, PAD, PAD))
        grad_tile = jnp.zeros((CORE, CORE), jnp.float32)
        loss_tile = jnp.float32(0.0)
        for condition in range(CONDITIONS):
            part_grad, part_loss = tile_terms(padded_tile, banks[condition, 0], banks[condition, 1], wave_re, wave_im, DOSES[condition], HALO)
            grad_tile = grad_tile + part_grad
            loss_tile = loss_tile + part_loss
        return (grad_tile, loss_tile)
    tile_grads, tile_losses = lax.map(one_tile, jnp.arange(tile_rows * tile_cols, dtype=jnp.int32))
    grad_cells = tile_grads.reshape(tile_rows, tile_cols, CORE, CORE).transpose(0, 2, 1, 3).reshape(ROWS, COLUMNS)
    grad_cells = grad_cells * mask_cells * (1.0 - mask_cells)
    cell_count = ROWS * COLUMNS
    loss_value = jnp.sum(tile_losses) / cell_count
    norm_value = jnp.sqrt(jnp.sum(grad_cells * grad_cells) / cell_count + EPSILON)
    return (mask_logits - STEP * grad_cells / norm_value, loss_value)
```

```python
import math

import jax
import jax.numpy as jnp
import numpy as np
from jax import lax
from jax.experimental import pallas as pl
from jax.experimental.pallas import tpu as pltpu
from jax.sharding import PartitionSpec as P

HALO = 64
KERNELS = 6
BAND = 32
CONDITIONS = 2

SHARPNESS = 6.0
THRESHOLD = 0.75
STEP = 0.5
EPSILON = 1e-06
DOSES = (1.0, 1.15)

LANES = 128
VMEM = pl.BlockSpec(memory_space=pltpu.VMEM)


def dot(first, second):
    return lax.dot_general(
        first,
        second,
        (((1,), (0,)), ((), ())),
        precision=lax.Precision.HIGHEST,
        preferred_element_type=jnp.float32,
    )


def tables(pad_width, margin):
    freq = np.arange(BAND) - BAND // 2
    place = np.arange(pad_width)
    turns = (freq[:, None] * place[None, :] % pad_width) * (2.0 * math.pi / pad_width)
    wave_re = np.cos(turns) / math.sqrt(pad_width)
    wave_im = -np.sin(turns) / math.sqrt(pad_width)
    grid = 2 * BAND
    stride = pad_width // grid
    fold = LANES // BAND
    rows = np.arange(BAND).reshape(BAND // fold, fold).T.reshape(-1)
    row_re, row_im = wave_re[rows], wave_im[rows]
    coarse_re, coarse_im = wave_re[:, ::stride], wave_im[:, ::stride]
    crow_re, crow_im = row_re[:, ::stride], row_im[:, ::stride]
    core = slice(margin, pad_width - margin)
    steps = (place[:, None] - stride * np.arange(grid)[None, :]) % pad_width
    diffs = np.arange(1, BAND)
    between = (
        1.0
        + 2.0
        * np.cos(2.0 * math.pi / pad_width * (steps[..., None] * diffs % pad_width)).sum(-1)
    ) / grid

    def cat(*blocks):
        return np.concatenate(blocks, axis=1)

    analyse_cols = cat(wave_re.T, wave_im.T, -wave_im.T, wave_re.T)
    analyse_rows = np.concatenate([row_re, row_im], axis=0)
    field_cols = np.concatenate(
        [
            cat(coarse_re, -coarse_im, -coarse_im, -coarse_re),
            cat(coarse_im, coarse_re, coarse_re, -coarse_im),
        ]
        * 2,
        axis=0,
    )
    field_rows = cat(crow_re.T, crow_im.T)
    up_rows = between
    up_cols = np.concatenate([between.T, between.T], axis=0)
    down_cols = cat(between, between)
    down_rows = between.T
    c_re, c_im = coarse_re.T, coarse_im.T
    back_cols = np.concatenate(
        [
            cat(c_re, c_im, c_im, -c_re, -c_im, c_re, c_re, c_im),
            cat(-c_im, c_re, c_re, c_im, -c_re, -c_im, -c_im, c_re),
        ],
        axis=0,
    )
    back_rows = cat(crow_re, crow_im)
    core_re, core_im = wave_re[:, core], wave_im[:, core]
    core_cols = np.concatenate([cat(core_re, -core_im), cat(core_im, core_re)] * 2, axis=0)
    core_rows = 2.0 * cat(row_re[:, core].T, row_im[:, core].T)
    return [
        jnp.asarray(t, jnp.float32)
        for t in (
            analyse_cols,
            analyse_rows,
            field_cols,
            field_rows,
            up_rows,
            up_cols,
            down_cols,
            down_rows,
            back_cols,
            back_rows,
            core_cols,
            core_rows,
        )
    ]


def pack_columns(logits_ref, target_ref, weight_ref, a_ref, b_ref):
    half = HALO
    odd = lax.rem(lax.axis_index("col"), 2) == 1
    values = [ref[...] for ref in (logits_ref, target_ref, weight_ref)]
    turned = [pltpu.roll(value, half, 1) for value in values]
    low = lax.broadcasted_iota(jnp.int32, values[0].shape, 1) < half
    rows = values[0].shape[0]
    to_right = [
        jnp.where(low, turned[0], values[1]),
        jnp.where(low[: rows // 2], turned[2][: rows // 2], values[2][rows // 2 :]),
    ]
    to_left = [
        jnp.where(low, values[0], turned[1]),
        jnp.where(low[: rows // 2], values[2][: rows // 2], turned[2][rows // 2 :]),
    ]
    a_ref[:rows] = jnp.where(odd, to_left[0], to_right[0])
    a_ref[rows:] = jnp.where(odd, to_left[1], to_right[1])
    b_ref[:rows] = jnp.where(odd, to_right[0], to_left[0])
    b_ref[rows:] = jnp.where(odd, to_right[1], to_left[1])


def widen(logits_ref, target_ref, weight_ref, a_ref, b_ref, centre_ref, up_ref, down_ref):
    half = HALO
    odd = lax.rem(lax.axis_index("col"), 2) == 1
    odd_row = lax.rem(lax.axis_index("row"), 2) == 1
    values = [ref[...] for ref in (logits_ref, target_ref, weight_ref)]
    rows = values[0].shape[0]
    low = lax.broadcasted_iota(jnp.int32, values[0].shape, 1) < half
    got_a, got_b = a_ref[...], b_ref[...]
    left = jnp.where(odd, got_a, got_b)
    right = jnp.where(odd, got_b, got_a)
    left_turned, right_turned = pltpu.roll(left, half, 1), pltpu.roll(right, half, 1)

    def two(first, second):
        return jnp.concatenate([first, second], axis=0)

    lefts = [left[:rows], left_turned[:rows], two(left[rows:], left_turned[rows:])]
    rights = [right_turned[:rows], right[:rows], two(right_turned[rows:], right[rows:])]
    for index, value in enumerate(values):
        turned = pltpu.roll(value, half, 1)
        wide = jnp.concatenate(
            [jnp.where(low, lefts[index], turned), jnp.where(low, turned, rights[index])], axis=1
        )
        centre_ref[index] = wide
        up_ref[index] = jnp.where(odd_row, wide[:half], wide[half:])
        down_ref[index] = jnp.where(odd_row, wide[half:], wide[:half])


def step_kernel(
    order,
    bank_ref,
    centre_ref,
    up_ref,
    down_ref,
    analyse_cols,
    analyse_rows,
    field_cols,
    field_rows,
    up_rows,
    up_cols,
    down_cols,
    down_rows,
    back_cols,
    back_rows,
    core_cols,
    core_rows,
    grad_ref,
    sums_ref,
    flat_ref,
):
    odd_row = lax.rem(lax.axis_index("row"), 2) == 1
    grid = 2 * BAND
    fold = LANES // BAND
    per = BAND // fold

    def padded(index):
        first, second = up_ref[index], down_ref[index]
        return jnp.concatenate(
            [
                jnp.where(odd_row, first, second),
                centre_ref[index],
                jnp.where(odd_row, second, first),
            ],
            axis=0,
        )

    weight = padded(2)
    mask = jnp.where(weight > 0.0, jax.nn.sigmoid(padded(0)), 0.0)
    target = padded(1)
    pad_width = mask.shape[0]
    core = slice(HALO, pad_width - HALO)

    for row, (device, piece) in enumerate(order):
        both = bank_ref[device, :, piece * LANES : (piece + 1) * LANES]
        for condition in range(CONDITIONS):
            flat_ref[condition, row : row + 1, :] = both[condition : condition + 1]

    lane = lax.broadcasted_iota(jnp.int32, (per, LANES), 1)

    def spread(condition, kernel):
        real = flat_ref[condition, pl.ds(kernel * per, per), :]
        imag = flat_ref[condition, pl.ds((KERNELS + kernel) * per, per), :]
        reals = [real] + [pltpu.roll(real, BAND * s, 1) for s in range(1, fold)]
        imags = [imag] + [pltpu.roll(imag, BAND * s, 1) for s in range(1, fold)]
        rows = []
        for j in range(fold):
            first, second = reals[-j % fold], reals[(1 - j) % fold]
            third, fourth = imags[(2 - j) % fold], imags[(3 - j) % fold]
            rows.append(
                jnp.where(
                    lane < 2 * BAND,
                    jnp.where(lane < BAND, first, second),
                    jnp.where(lane < 3 * BAND, third, fourth),
                )
            )
        return jnp.concatenate(rows, axis=0)

    pairs = [(c, k) for c in range(CONDITIONS) for k in range(KERNELS)]
    spectra = [spread(c, k) for c, k in pairs]

    half = dot(mask, analyse_cols[...])
    both = dot(analyse_rows[...], half)
    wide_lane = lax.broadcasted_iota(jnp.int32, (BAND, LANES), 1)
    turned = pltpu.roll(both[BAND:], LANES // 2, 1)
    spectrum = both[:BAND] + jnp.where(wide_lane < LANES // 2, turned, -turned)

    products = jnp.concatenate([s * spectrum for s in spectra], axis=0)
    halves = dot(products, field_cols[...])
    fields = []
    squares = [0.0] * CONDITIONS
    for index, (condition, _) in enumerate(pairs):
        rows = halves[index * BAND : (index + 1) * BAND]
        stacked = jnp.concatenate([rows[:, :LANES], rows[:, LANES:]], axis=0)
        field = dot(field_rows[...], stacked)
        fields.append(field)
        squares[condition] = squares[condition] + field * field

    tall = dot(up_rows[...], jnp.concatenate(squares, axis=1))
    tall = jnp.concatenate(
        [tall[:, c * LANES : (c + 1) * LANES] for c in range(CONDITIONS)], axis=0
    )
    intensities = dot(tall, up_cols[...])

    slopes = []
    loss = 0.0
    for condition, dose in enumerate(DOSES):
        intensity = intensities[condition * pad_width : (condition + 1) * pad_width]
        resist = jax.nn.sigmoid(SHARPNESS * (dose * intensity - THRESHOLD))
        error = resist - target
        scaled = weight * error
        loss = loss + (scaled * error)[core, core]
        slopes.append((2.0 * SHARPNESS * dose) * scaled * (resist * (1.0 - resist)))
    narrow = dot(jnp.concatenate(slopes, axis=0), down_cols[...])
    narrow = jnp.concatenate(
        [narrow[c * pad_width : (c + 1) * pad_width] for c in range(CONDITIONS)], axis=1
    )
    coarse = dot(down_rows[...], narrow)

    weighted = jnp.concatenate(
        [
            field * coarse[:, condition * LANES : (condition + 1) * LANES]
            for field, (condition, _) in zip(fields, pairs, strict=True)
        ],
        axis=0,
    )
    backs = dot(weighted, back_cols[...])
    total = 0.0
    for index in range(len(pairs)):
        rows = backs[index * grid : (index + 1) * grid]
        stacked = jnp.concatenate([rows[:, :LANES], rows[:, LANES:]], axis=0)
        total = total + spectra[index] * dot(back_rows[...], stacked)

    across = dot(total, core_cols[...])
    core_width = across.shape[1] // 2
    stacked = jnp.concatenate([across[:, :core_width], across[:, core_width:]], axis=0)
    gradient = dot(core_rows[...], stacked)
    own = mask[core, core]
    cells = gradient * own * (1.0 - own)
    grad_ref[...] = cells
    square = jnp.sum(jnp.sum(cells * cells, axis=0, keepdims=True), axis=1, keepdims=True)
    loss = jnp.sum(jnp.sum(loss, axis=0, keepdims=True), axis=1, keepdims=True)
    sums_ref[0:1, :] = jnp.broadcast_to(square, (1, LANES))
    sums_ref[1:2, :] = jnp.broadcast_to(loss, (1, LANES))


def axis_rounds(axis):
    count = lax.axis_size(axis)
    bits = [1 << b for b in range(count.bit_length() - 1)]
    return bits[1:] + bits[:1] if axis == "row" else bits


def swap(value, axis, bit):
    count = lax.axis_size(axis)
    return lax.ppermute(value, axis, [(i, i ^ bit) for i in range(count)])


def gather_bank(kernels):
    held = kernels[None]
    crossed = []
    for axis in ("col", "row"):
        for bit in axis_rounds(axis):
            got = swap(held, axis, bit)
            high = (lax.axis_index(axis) & bit) != 0
            held = jnp.concatenate(
                [jnp.where(high, got, held), jnp.where(high, held, got)], axis=0
            )
            crossed.append((axis, bit))
    rows, cols = lax.axis_size("row"), lax.axis_size("col")
    place = {}
    for row in range(rows):
        for col in range(cols):
            index = 0
            for level, (axis, bit) in enumerate(crossed):
                own = row if axis == "row" else col
                index += (1 << level) * ((own & bit) != 0)
            place[row * cols + col] = index
    return held, place


def pair_swap(value, axis, first):
    count = lax.axis_size(axis)
    pairs = []
    for low in range(first, count - 1, 2):
        pairs += [(low, low + 1), (low + 1, low)]
    return lax.ppermute(value, axis, pairs)


def total_sum(value):
    for axis in ("row", "col"):
        for bit in axis_rounds(axis):
            value = value + swap(value, axis, bit)
    return value


def shards(mask_logits, target, weight, kernels):
    core_width = mask_logits.shape[0]
    pad_width = core_width + 2 * HALO
    rows, cols = lax.axis_size("row"), lax.axis_size("col")
    f32 = jnp.float32

    bank, place = gather_bank(kernels)
    pieces = kernels.shape[1] // LANES
    if kernels.shape[1] % LANES:
        whole = bank[np.array([place[device] for device in range(rows * cols)])]
        bank = jnp.swapaxes(whole, 0, 1).reshape(1, CONDITIONS, -1)
        place, pieces = {0: 0}, bank.shape[2] // LANES
    order = [(place[device], piece) for device in sorted(place) for piece in range(pieces)]

    packed = jax.ShapeDtypeStruct((core_width * 3 // 2, core_width), f32)
    slab_a, slab_b = pl.pallas_call(
        pack_columns, out_shape=(packed, packed), in_specs=[VMEM] * 3, out_specs=(VMEM,) * 2
    )(mask_logits, target, weight)
    got_a, got_b = pair_swap(slab_a, "col", 0), pair_swap(slab_b, "col", 1)
    slab = jax.ShapeDtypeStruct((3, HALO, pad_width), f32)
    centre, up, down = pl.pallas_call(
        widen,
        out_shape=(jax.ShapeDtypeStruct((3, core_width, pad_width), f32), slab, slab),
        in_specs=[VMEM] * 5,
        out_specs=(VMEM,) * 3,
    )(mask_logits, target, weight, got_a, got_b)
    up, down = pair_swap(up, "row", 0), pair_swap(down, "row", 1)

    consts = tables(pad_width, HALO)
    grad_cells, sums = pl.pallas_call(
        lambda *refs: step_kernel(order, *refs),
        out_shape=(
            jax.ShapeDtypeStruct((core_width, core_width), f32),
            jax.ShapeDtypeStruct((2, LANES), f32),
        ),
        in_specs=[VMEM] * (4 + len(consts)),
        out_specs=(VMEM,) * 2,
        scratch_shapes=[pltpu.VMEM((CONDITIONS, len(order), LANES), f32)],
        compiler_params=pltpu.CompilerParams(vmem_limit_bytes=32 * 1024 * 1024),
    )(bank, centre, up, down, *consts)

    sums = total_sum(sums)
    cell_count = rows * cols * core_width * core_width
    norm = jnp.sqrt(sums[0:1] / cell_count + EPSILON)
    return (mask_logits - STEP * grad_cells / norm, sums[1, 0] / cell_count)


def solution(mesh):
    placed = (P("row", "col"), P("row", "col"), P("row", "col"), P(None, ("row", "col")))
    return jax.shard_map(
        shards, mesh=mesh, in_specs=placed, out_specs=(P("row", "col"), P()), check_vma=False
    )
```

```python
import functools
import math

import jax
import jax.numpy as jnp
import numpy as np
from jax import lax
from jax.experimental import pallas as pl
from jax.experimental.pallas import tpu as pltpu
from jax.sharding import PartitionSpec as P

HALO = 64
KERNELS = 6
BAND = 32
CONDITIONS = 2

SHARPNESS = 6.0
THRESHOLD = 0.75
STEP = 0.5
EPSILON = 1e-06
DOSES = (1.0, 1.15)

LANES = 128
VMEM = pl.BlockSpec(memory_space=pltpu.VMEM)


def dot(first, second):
    return lax.dot_general(
        first,
        second,
        (((1,), (0,)), ((), ())),
        precision=lax.Precision.HIGHEST,
        preferred_element_type=jnp.float32,
    )


def tables(pad_width, margin):
    freq = np.arange(BAND) - BAND // 2
    place = np.arange(pad_width)
    turns = (freq[:, None] * place[None, :] % pad_width) * (2.0 * math.pi / pad_width)
    wave_re = np.cos(turns) / math.sqrt(pad_width)
    wave_im = -np.sin(turns) / math.sqrt(pad_width)
    grid = 2 * BAND
    stride = pad_width // grid
    fold = LANES // BAND
    rows = np.arange(BAND).reshape(BAND // fold, fold).T.reshape(-1)
    row_re, row_im = wave_re[rows], wave_im[rows]
    coarse_re, coarse_im = wave_re[:, ::stride], wave_im[:, ::stride]
    crow_re, crow_im = row_re[:, ::stride], row_im[:, ::stride]
    core = slice(margin, pad_width - margin)
    steps = (place[:, None] - stride * np.arange(grid)[None, :]) % pad_width
    diffs = np.arange(1, BAND)
    between = (
        1.0
        + 2.0
        * np.cos(2.0 * math.pi / pad_width * (steps[..., None] * diffs % pad_width)).sum(-1)
    ) / grid

    def cat(*blocks):
        return np.concatenate(blocks, axis=1)

    analyse_cols = cat(wave_re.T, wave_im.T, -wave_im.T, wave_re.T)
    analyse_rows = np.concatenate([row_re, row_im], axis=0)
    field_cols = np.concatenate(
        [
            cat(coarse_re, -coarse_im, -coarse_im, -coarse_re),
            cat(coarse_im, coarse_re, coarse_re, -coarse_im),
        ]
        * 2,
        axis=0,
    )
    field_rows = cat(crow_re.T, crow_im.T)
    up_rows = between
    up_cols = np.concatenate([between.T, between.T], axis=0)
    down_cols = cat(between, between)
    down_rows = between.T
    c_re, c_im = coarse_re.T, coarse_im.T
    back_cols = np.concatenate(
        [
            cat(c_re, c_im, c_im, -c_re, -c_im, c_re, c_re, c_im),
            cat(-c_im, c_re, c_re, c_im, -c_re, -c_im, -c_im, c_re),
        ],
        axis=0,
    )
    back_rows = cat(crow_re, crow_im)
    core_re, core_im = wave_re[:, core], wave_im[:, core]
    core_cols = np.concatenate([cat(core_re, -core_im), cat(core_im, core_re)] * 2, axis=0)
    core_rows = 2.0 * cat(row_re[:, core].T, row_im[:, core].T)
    parts = [
        ("field_cols", field_cols),
        ("up_cols", up_cols),
        ("back_cols", back_cols),
        ("core_cols", core_cols),
        ("analyse_rows", analyse_rows),
        ("down_rows", down_rows),
    ]
    side = [
        [("analyse_cols", analyse_cols), ("up_rows", up_rows)],
        [
            ("down_cols", down_cols),
            ("core_rows", core_rows),
            ("field_rows", field_rows),
            ("back_rows", back_rows),
        ],
    ]
    place, rows = {}, []
    start = 0
    for name, part in parts:
        place[name] = (start, 0, part.shape)
        rows.append(part)
        start += part.shape[0]
    columns = []
    for left, stack in zip((0, LANES), side, strict=True):
        top = start
        column = []
        for name, part in stack:
            place[name] = (top, left, part.shape)
            column.append(np.pad(part, ((0, 0), (0, LANES - part.shape[1]))))
            top += part.shape[0]
        columns.append(np.concatenate(column, axis=0))
    height = max(column.shape[0] for column in columns)
    columns = [np.pad(c, ((0, height - c.shape[0]), (0, 0))) for c in columns]
    rows.append(np.concatenate(columns, axis=1))
    return jnp.asarray(np.concatenate(rows, axis=0), jnp.float32), place


def pack_columns(own_ref, a_ref, b_ref):
    half = HALO
    odd = lax.rem(lax.axis_index("col"), 2) == 1
    values = [own_ref[index] for index in range(3)]
    turned = [pltpu.roll(value, half, 1) for value in values]
    low = lax.broadcasted_iota(jnp.int32, values[0].shape, 1) < half
    rows = values[0].shape[0]
    to_right = [
        jnp.where(low, turned[0], values[1]),
        jnp.where(low[: rows // 2], turned[2][: rows // 2], values[2][rows // 2 :]),
    ]
    to_left = [
        jnp.where(low, values[0], turned[1]),
        jnp.where(low[: rows // 2], values[2][: rows // 2], turned[2][rows // 2 :]),
    ]
    a_ref[:rows] = jnp.where(odd, to_left[0], to_right[0])
    a_ref[rows:] = jnp.where(odd, to_left[1], to_right[1])
    b_ref[:rows] = jnp.where(odd, to_right[0], to_left[0])
    b_ref[rows:] = jnp.where(odd, to_right[1], to_left[1])


def widen(own_ref, a_ref, b_ref, shards_ref, centre_ref, up_ref, down_ref, bank_ref):
    bank_ref[...] = shards_ref[...]
    half = HALO
    odd = lax.rem(lax.axis_index("col"), 2) == 1
    odd_row = lax.rem(lax.axis_index("row"), 2) == 1
    values = [own_ref[index] for index in range(3)]
    rows = values[0].shape[0]
    low = lax.broadcasted_iota(jnp.int32, values[0].shape, 1) < half
    got_a, got_b = a_ref[...], b_ref[...]
    left = jnp.where(odd, got_a, got_b)
    right = jnp.where(odd, got_b, got_a)
    left_turned, right_turned = pltpu.roll(left, half, 1), pltpu.roll(right, half, 1)

    def two(first, second):
        return jnp.concatenate([first, second], axis=0)

    lefts = [left[:rows], left_turned[:rows], two(left[rows:], left_turned[rows:])]
    rights = [right_turned[:rows], right[:rows], two(right_turned[rows:], right[rows:])]
    for index, value in enumerate(values):
        turned = pltpu.roll(value, half, 1)
        wide = jnp.concatenate(
            [jnp.where(low, lefts[index], turned), jnp.where(low, turned, rights[index])], axis=1
        )
        centre_ref[index] = wide
        up_ref[index] = jnp.where(odd_row, wide[:half], wide[half:])
        down_ref[index] = jnp.where(odd_row, wide[half:], wide[:half])


def step_kernel(
    order,
    place,
    bank_ref,
    centre_ref,
    up_ref,
    down_ref,
    table_ref,
    grad_ref,
    sums_ref,
    flat_ref,
):
    row_place = lax.axis_index("row")
    odd_row = lax.rem(row_place, 2) == 1
    at_top, at_bottom = row_place == 0, row_place == lax.axis_size("row") - 1
    grid = 2 * BAND
    fold = LANES // BAND
    per = BAND // fold

    def table(name):
        top, left, shape = place[name]
        return table_ref[top : top + shape[0], left : left + shape[1]]

    def padded(index):
        first, second = up_ref[index], down_ref[index]
        above = jnp.where(odd_row, first, second)
        below = jnp.where(odd_row, second, first)
        return jnp.concatenate([above, centre_ref[index], below], axis=0)

    cell_row = lax.broadcasted_iota(jnp.int32, (centre_ref.shape[1] + 2 * HALO, 1), 0)
    first_row = jnp.where(at_top, HALO, 0)
    last_row = jnp.where(at_bottom, cell_row.shape[0] - HALO, cell_row.shape[0])
    inside = jnp.logical_and(cell_row >= first_row, cell_row < last_row)
    weight = jnp.where(inside, padded(2), 0.0)
    mask = jnp.where(weight > 0.0, jax.nn.sigmoid(padded(0)), 0.0)
    target = jnp.where(inside, padded(1), 0.0)
    pad_width = mask.shape[0]
    core = slice(HALO, pad_width - HALO)

    for row, (device, piece) in enumerate(order):
        both = bank_ref[device, :, piece * LANES : (piece + 1) * LANES]
        for condition in range(CONDITIONS):
            flat_ref[condition, row : row + 1, :] = both[condition : condition + 1]

    lane = lax.broadcasted_iota(jnp.int32, (per, LANES), 1)

    def spread(condition, kernel):
        real = flat_ref[condition, pl.ds(kernel * per, per), :]
        imag = flat_ref[condition, pl.ds((KERNELS + kernel) * per, per), :]
        reals = [real] + [pltpu.roll(real, BAND * s, 1) for s in range(1, fold)]
        imags = [imag] + [pltpu.roll(imag, BAND * s, 1) for s in range(1, fold)]
        rows = []
        for j in range(fold):
            first, second = reals[-j % fold], reals[(1 - j) % fold]
            third, fourth = imags[(2 - j) % fold], imags[(3 - j) % fold]
            rows.append(
                jnp.where(
                    lane < 2 * BAND,
                    jnp.where(lane < BAND, first, second),
                    jnp.where(lane < 3 * BAND, third, fourth),
                )
            )
        return jnp.concatenate(rows, axis=0)

    pairs = [(c, k) for c in range(CONDITIONS) for k in range(KERNELS)]
    spectra = [spread(c, k) for c, k in pairs]

    half = dot(mask, table("analyse_cols"))
    both = dot(table("analyse_rows"), half)
    wide_lane = lax.broadcasted_iota(jnp.int32, (BAND, LANES), 1)
    turned = pltpu.roll(both[BAND:], LANES // 2, 1)
    spectrum = both[:BAND] + jnp.where(wide_lane < LANES // 2, turned, -turned)

    products = jnp.concatenate([s * spectrum for s in spectra], axis=0)
    halves = dot(products, table("field_cols"))
    fields = []
    squares = [0.0] * CONDITIONS
    for index, (condition, _) in enumerate(pairs):
        rows = halves[index * BAND : (index + 1) * BAND]
        stacked = jnp.concatenate([rows[:, :LANES], rows[:, LANES:]], axis=0)
        field = dot(table("field_rows"), stacked)
        fields.append(field)
        squares[condition] = squares[condition] + field * field

    tall = dot(table("up_rows"), jnp.concatenate(squares, axis=1))
    tall = jnp.concatenate(
        [tall[:, c * LANES : (c + 1) * LANES] for c in range(CONDITIONS)], axis=0
    )
    intensities = dot(tall, table("up_cols"))

    slopes = []
    loss = 0.0
    for condition, dose in enumerate(DOSES):
        intensity = intensities[condition * pad_width : (condition + 1) * pad_width]
        resist = jax.nn.sigmoid(SHARPNESS * (dose * intensity - THRESHOLD))
        error = resist - target
        scaled = weight * error
        loss = loss + (scaled * error)[core, core]
        slopes.append((2.0 * SHARPNESS * dose) * scaled * (resist * (1.0 - resist)))
    narrow = dot(jnp.concatenate(slopes, axis=0), table("down_cols"))
    narrow = jnp.concatenate(
        [narrow[c * pad_width : (c + 1) * pad_width] for c in range(CONDITIONS)], axis=1
    )
    coarse = dot(table("down_rows"), narrow)

    weighted = jnp.concatenate(
        [
            field * coarse[:, condition * LANES : (condition + 1) * LANES]
            for field, (condition, _) in zip(fields, pairs, strict=True)
        ],
        axis=0,
    )
    backs = dot(weighted, table("back_cols"))
    total = 0.0
    for index in range(len(pairs)):
        rows = backs[index * grid : (index + 1) * grid]
        stacked = jnp.concatenate([rows[:, :LANES], rows[:, LANES:]], axis=0)
        total = total + spectra[index] * dot(table("back_rows"), stacked)

    across = dot(total, table("core_cols"))
    core_width = across.shape[1] // 2
    stacked = jnp.concatenate([across[:, :core_width], across[:, core_width:]], axis=0)
    gradient = dot(table("core_rows"), stacked)
    own = mask[core, core]
    cells = gradient * own * (1.0 - own)
    grad_ref[...] = cells
    square = jnp.sum(jnp.sum(cells * cells, axis=0, keepdims=True), axis=1, keepdims=True)
    loss = jnp.sum(jnp.sum(loss, axis=0, keepdims=True), axis=1, keepdims=True)
    sums = jnp.concatenate([square, loss], axis=0)
    sums_ref[...] = jnp.broadcast_to(sums[None], sums_ref.shape)


def rounds():
    row = [("row", 1 << b) for b in range(lax.axis_size("row").bit_length() - 1)]
    col = [("col", 1 << b) for b in range(lax.axis_size("col").bit_length() - 1)]
    return col[:1] + row[1:2] + col[1:] + row[2:] + row[:1]


def swap(value, axis, bit):
    count = lax.axis_size(axis)
    return lax.ppermute(value, axis, [(i, i ^ bit) for i in range(count)])


def small(megabytes):
    return pltpu.CompilerParams(vmem_limit_bytes=megabytes * 1024 * 1024)


def to_all(value):
    return lax.all_to_all(value, ("row", "col"), 0, 0)


def pair_swap(value, axis, first, wrap=False):
    count = lax.axis_size(axis)
    pairs = []
    for low in range(first, count - 1, 2):
        pairs += [(low, low + 1), (low + 1, low)]
    if wrap and first and count % 2 == 0:
        pairs += [(0, count - 1), (count - 1, 0)]
    return lax.ppermute(value, axis, pairs)


def finish(cell_count, own_ref, cells_ref, sums_ref, logits_ref, loss_ref):
    total = jnp.sum(sums_ref[...], axis=0) / cell_count
    scale = STEP / jnp.sqrt(total[0:1] + EPSILON)
    logits_ref[...] = own_ref[0] - cells_ref[...] * scale
    loss_ref[...] = total[1:2, 0:1]


def shards(mask_logits, target, weight, kernels):
    core_width = mask_logits.shape[0]
    pad_width = core_width + 2 * HALO
    rows, cols = lax.axis_size("row"), lax.axis_size("col")
    f32 = jnp.float32

    def struct(*shape):
        return jax.ShapeDtypeStruct(shape, f32)

    packed = struct(core_width * 3 // 2, core_width)
    own = jnp.stack([mask_logits, target, weight])
    slab_a, slab_b = pl.pallas_call(
        pack_columns,
        out_shape=(packed, packed),
        in_specs=[VMEM],
        out_specs=(VMEM,) * 2,
        compiler_params=small(4),
    )(own)
    bank = jnp.broadcast_to(kernels[None], (rows * cols,) + kernels.shape)
    got_a, got_b = pair_swap(slab_a, "col", 0), pair_swap(slab_b, "col", 1)
    slab = struct(3, HALO, pad_width)
    centre, up, down, bank = pl.pallas_call(
        widen,
        out_shape=(struct(3, core_width, pad_width), slab, slab, struct(*bank.shape)),
        in_specs=[VMEM] * 4,
        out_specs=(VMEM,) * 4,
        compiler_params=small(8),
    )(own, got_a, got_b, bank)
    up, down = pair_swap(up, "row", 0), pair_swap(down, "row", 1, wrap=True)
    bank = to_all(bank)
    pieces = kernels.shape[1] // LANES
    if kernels.shape[1] % LANES:
        bank = jnp.swapaxes(bank, 0, 1).reshape(1, CONDITIONS, -1)
        pieces = bank.shape[2] // LANES
    order = [(device, piece) for device in range(bank.shape[0]) for piece in range(pieces)]

    consts, place = tables(pad_width, HALO)
    grad_cells, sums = pl.pallas_call(
        functools.partial(step_kernel, order, place),
        out_shape=(
            struct(core_width, core_width),
            struct(rows * cols, 2, LANES),
        ),
        in_specs=[VMEM] * 5,
        out_specs=(VMEM,) * 2,
        scratch_shapes=[pltpu.VMEM((CONDITIONS, len(order), LANES), f32)],
        compiler_params=pltpu.CompilerParams(vmem_limit_bytes=16 * 1024 * 1024),
    )(bank, centre, up, down, consts)

    sums = to_all(sums)
    cell_count = rows * cols * core_width * core_width
    new_logits, loss = pl.pallas_call(
        functools.partial(finish, cell_count),
        out_shape=(struct(core_width, core_width), struct(1, 1)),
        in_specs=[VMEM] * 3,
        out_specs=(VMEM,) * 2,
        compiler_params=small(4),
    )(own, grad_cells, sums)
    return (new_logits, loss[0, 0])


def solution(mesh):
    placed = (P("row", "col"), P("row", "col"), P("row", "col"), P(None, ("row", "col")))
    return jax.shard_map(
        shards, mesh=mesh, in_specs=placed, out_specs=(P("row", "col"), P()), check_vma=False
    )
```

```python
import functools
import math

import jax
import jax.numpy as jnp
import numpy as np
from jax import lax
from jax.experimental import pallas as pl
from jax.experimental.pallas import tpu as pltpu
from jax.sharding import PartitionSpec as P

HALO = 64
KERNELS = 6
BAND = 32
CONDITIONS = 2

SHARPNESS = 6.0
THRESHOLD = 0.75
STEP = 0.5
EPSILON = 1e-06
DOSES = (1.0, 1.15)

LANES = 128
VMEM = pl.BlockSpec(memory_space=pltpu.VMEM)


def dot(first, second):
    return lax.dot_general(
        first, second, (((1,), (0,)), ((), ())), preferred_element_type=jnp.float32
    )


def split(value, count):
    parts = []
    for index in range(count):
        part = value.astype(jnp.bfloat16)
        parts.append(part)
        if index + 1 < count:
            value = value - part.astype(jnp.float32)
    return parts


def split_table(table, count):
    parts = []
    for _ in range(count):
        part = table.astype(np.float32).astype(jnp.bfloat16)
        parts.append(part)
        table = table - part.astype(np.float64)
    return parts


def tables(pad_width, margin):
    freq = np.arange(BAND) - BAND // 2
    place = np.arange(pad_width)
    turns = (freq[:, None] * place[None, :] % pad_width) * (2.0 * math.pi / pad_width)
    wave_re = np.cos(turns) / math.sqrt(pad_width)
    wave_im = -np.sin(turns) / math.sqrt(pad_width)
    grid = 2 * BAND
    stride = pad_width // grid
    fold = LANES // BAND
    rows = np.arange(BAND).reshape(BAND // fold, fold).T.reshape(-1)
    row_re, row_im = wave_re[rows], wave_im[rows]
    coarse_re, coarse_im = wave_re[:, ::stride], wave_im[:, ::stride]
    crow_re, crow_im = row_re[:, ::stride], row_im[:, ::stride]
    core = slice(margin, pad_width - margin)
    core_re, core_im = wave_re[:, core], wave_im[:, core]
    steps = (place[:, None] - stride * np.arange(grid)[None, :]) % pad_width
    diffs = np.arange(1, BAND)
    phases = (steps[..., None] * diffs % pad_width) * (2.0 * math.pi / pad_width)
    between = (1.0 + 2.0 * np.cos(phases).sum(-1)) / grid

    def beside(*blocks):
        return np.concatenate(blocks, axis=1)

    def below(*blocks):
        return np.concatenate(blocks, axis=0)

    found = {}
    h, l = split_table(beside(wave_re.T, wave_im.T, -wave_im.T, wave_re.T), 2)
    found["analyse_cols"] = beside(h, l)
    found["analyse_rows"] = below(*split_table(below(row_re, row_im), 3))
    from_re = beside(coarse_re, -coarse_im, -coarse_im, -coarse_re)
    from_im = beside(coarse_im, coarse_re, coarse_re, -coarse_im)
    h, m, l = split_table(below(from_re, from_im, from_re, from_im), 3)
    found["field_cols"] = below(h, h, m, m, h, l)
    h, m, l = split_table(beside(crow_re.T, crow_im.T), 3)
    found["field_rows"] = beside(h, h, h, m, m, l)
    h, m, l = split_table(between, 3)
    found["up_rows"] = beside(h, h, h, m, m, l)
    found["up_cols"] = below(h.T, h.T, h.T, m.T, m.T, l.T)
    found["down_cols"] = beside(h, h, m, m)
    found["down_rows"] = below(h.T, m.T)
    h, l = split_table(below(crow_re, crow_im), 2)
    found["back_rows"] = beside(h, h, l)
    c_re, c_im = coarse_re.T, coarse_im.T
    h, l = split_table(
        below(beside(c_re, c_im, c_im, -c_re), beside(-c_im, c_re, c_re, c_im)), 2
    )
    found["back_cols"] = below(h, h, l)
    from_re, from_im = beside(core_re, -core_im), beside(core_im, core_re)
    h, l = split_table(below(from_re, from_im, from_re, from_im), 2)
    found["core_cols"] = below(h, h, l)
    h, l = split_table(2.0 * beside(row_re[:, core].T, row_im[:, core].T), 2)
    found["core_rows"] = beside(h, h, l)

    arrays, where = [], {}
    for index, width in enumerate((2 * LANES, 3 * LANES)):
        start, stack = 0, []
        for name, table in found.items():
            if (table.shape[1] > 2 * LANES) == (index == 1):
                where[name] = (index, start, table.shape)
                stack.append(np.pad(table, ((0, 0), (0, width - table.shape[1]))))
                start += table.shape[0]
        arrays.append(jnp.asarray(np.concatenate(stack, axis=0)))
    return arrays, where


def pack_columns(own_ref, a_ref, b_ref):
    half = HALO
    odd = lax.rem(lax.axis_index("col"), 2) == 1
    values = [own_ref[index] for index in range(3)]
    turned = [pltpu.roll(value, half, 1) for value in values]
    low = lax.broadcasted_iota(jnp.int32, values[0].shape, 1) < half
    rows = values[0].shape[0]
    to_right = [
        jnp.where(low, turned[0], values[1]),
        jnp.where(low[: rows // 2], turned[2][: rows // 2], values[2][rows // 2 :]),
    ]
    to_left = [
        jnp.where(low, values[0], turned[1]),
        jnp.where(low[: rows // 2], values[2][: rows // 2], turned[2][rows // 2 :]),
    ]
    a_ref[:rows] = jnp.where(odd, to_left[0], to_right[0])
    a_ref[rows:] = jnp.where(odd, to_left[1], to_right[1])
    b_ref[:rows] = jnp.where(odd, to_right[0], to_left[0])
    b_ref[rows:] = jnp.where(odd, to_right[1], to_left[1])


def widen(own_ref, a_ref, b_ref, shards_ref, centre_ref, up_ref, down_ref, bank_ref):
    bank_ref[...] = shards_ref[...]
    half = HALO
    odd = lax.rem(lax.axis_index("col"), 2) == 1
    odd_row = lax.rem(lax.axis_index("row"), 2) == 1
    values = [own_ref[index] for index in range(3)]
    rows = values[0].shape[0]
    low = lax.broadcasted_iota(jnp.int32, values[0].shape, 1) < half
    got_a, got_b = a_ref[...], b_ref[...]
    left = jnp.where(odd, got_a, got_b)
    right = jnp.where(odd, got_b, got_a)
    left_turned, right_turned = pltpu.roll(left, half, 1), pltpu.roll(right, half, 1)

    def two(first, second):
        return jnp.concatenate([first, second], axis=0)

    lefts = [left[:rows], left_turned[:rows], two(left[rows:], left_turned[rows:])]
    rights = [right_turned[:rows], right[:rows], two(right_turned[rows:], right[rows:])]
    for index, value in enumerate(values):
        turned = pltpu.roll(value, half, 1)
        wide = jnp.concatenate(
            [jnp.where(low, lefts[index], turned), jnp.where(low, turned, rights[index])], axis=1
        )
        centre_ref[index] = wide
        up_ref[index] = jnp.where(odd_row, wide[:half], wide[half:])
        down_ref[index] = jnp.where(odd_row, wide[half:], wide[:half])


def step_kernel(
    order,
    place,
    bank_ref,
    centre_ref,
    up_ref,
    down_ref,
    narrow_ref,
    wide_ref,
    grad_ref,
    sums_ref,
    flat_ref,
):
    row_place = lax.axis_index("row")
    odd_row = lax.rem(row_place, 2) == 1
    at_top, at_bottom = row_place == 0, row_place == lax.axis_size("row") - 1
    grid = 2 * BAND
    fold = LANES // BAND
    per = BAND // fold

    def table(name, first=0, count=None):
        index, top, shape = place[name]
        top, count = top + first, shape[0] - first if count is None else count
        return (narrow_ref, wide_ref)[index][top : top + count, : shape[1]]

    def beside(*blocks):
        return jnp.concatenate(blocks, axis=1)

    def below(*blocks):
        return jnp.concatenate(blocks, axis=0)

    def padded(index):
        first, second = up_ref[index], down_ref[index]
        above = jnp.where(odd_row, first, second)
        below = jnp.where(odd_row, second, first)
        return jnp.concatenate([above, centre_ref[index], below], axis=0)

    cell_row = lax.broadcasted_iota(jnp.int32, (centre_ref.shape[1] + 2 * HALO, 1), 0)
    first_row = jnp.where(at_top, HALO, 0)
    last_row = jnp.where(at_bottom, cell_row.shape[0] - HALO, cell_row.shape[0])
    inside = jnp.logical_and(cell_row >= first_row, cell_row < last_row)
    weight = jnp.where(inside, padded(2), 0.0)
    mask = jnp.where(weight > 0.0, jax.nn.sigmoid(padded(0)), 0.0)
    target = jnp.where(inside, padded(1), 0.0)
    pad_width = mask.shape[0]
    core = slice(HALO, pad_width - HALO)

    for row, (device, piece) in enumerate(order):
        both = bank_ref[device, :, piece * LANES : (piece + 1) * LANES]
        for condition in range(CONDITIONS):
            flat_ref[condition, row : row + 1, :] = both[condition : condition + 1]

    lane = lax.broadcasted_iota(jnp.int32, (per, LANES), 1)

    def spread(condition, kernel):
        real = flat_ref[condition, pl.ds(kernel * per, per), :]
        imag = flat_ref[condition, pl.ds((KERNELS + kernel) * per, per), :]
        reals = [real] + [pltpu.roll(real, BAND * s, 1) for s in range(1, fold)]
        imags = [imag] + [pltpu.roll(imag, BAND * s, 1) for s in range(1, fold)]
        rows = []
        for j in range(fold):
            first, second = reals[-j % fold], reals[(1 - j) % fold]
            third, fourth = imags[(2 - j) % fold], imags[(3 - j) % fold]
            rows.append(
                jnp.where(
                    lane < 2 * BAND,
                    jnp.where(lane < BAND, first, second),
                    jnp.where(lane < 3 * BAND, third, fourth),
                )
            )
        return jnp.concatenate(rows, axis=0)

    pairs = [(c, k) for c in range(CONDITIONS) for k in range(KERNELS)]
    spectra = [spread(c, k) for c, k in pairs]

    h, l = split(mask, 2)
    both = dot(h, table("analyse_cols"))
    half = both[:, :LANES] + both[:, LANES:] + dot(l, table("analyse_cols")[:, :LANES])
    h, m, l = split(half, 3)
    both = dot(table("analyse_rows", 0, 2 * grid), beside(h, m))
    rest = dot(table("analyse_rows", 2 * grid), h) + dot(table("analyse_rows", 0, grid), l)
    both = both[:grid, :LANES] + (both[:grid, LANES:] + both[grid:, :LANES]) + (both[grid:, LANES:] + rest)
    low = lax.broadcasted_iota(jnp.int32, (1, LANES), 1) < LANES // 2
    turned = pltpu.roll(both[BAND:], LANES // 2, 1)
    spectrum = both[:BAND] + jnp.where(low, turned, -turned)

    products = below(*[s * spectrum for s in spectra])
    h, m, l = split(products, 3)
    size = 2 * LANES
    halves = (
        dot(beside(h, m), table("field_cols", 0, size))
        + dot(beside(h, m), table("field_cols", size, size))
        + dot(beside(l, h), table("field_cols", 2 * size, size))
    )
    halves = split(halves, 3)
    fields = []
    square = 0.0
    for kernel in range(KERNELS):
        parts = []
        for part in halves:
            stacked = []
            for condition in range(CONDITIONS):
                first = (condition * KERNELS + kernel) * BAND
                rows = part[first : first + BAND]
                stacked.append(below(rows[:, :LANES], rows[:, LANES:]))
            parts.append(beside(*stacked))
        h, m, l = parts
        field = dot(table("field_rows"), below(h, m, l, h, m, h))
        fields.append(field)
        square = square + field * field

    square = below(*[square[:, c * LANES : (c + 1) * LANES] for c in range(CONDITIONS)])
    square = square + pltpu.roll(square, LANES // 2, 1)
    h, m, l = [part.astype(jnp.float32) for part in split(square, 3)]
    mixed = [jnp.where(low, h, m), jnp.where(low, l, h), jnp.where(low, m, h)]
    tall = dot(beside(*[part.astype(jnp.bfloat16) for part in mixed]), table("up_cols"))
    tall = split(tall, 3)

    slopes = []
    loss = 0.0
    for condition, dose in enumerate(DOSES):
        h, m, l = [part[condition * grid : (condition + 1) * grid] for part in tall]
        intensity = dot(table("up_rows"), below(h, m, l, h, m, h))
        resist = jax.nn.sigmoid(SHARPNESS * (dose * intensity - THRESHOLD))
        error = resist - target
        scaled = weight * error
        loss = loss + (scaled * error)[core, core]
        slopes.append((2.0 * SHARPNESS * dose) * scaled * (resist * (1.0 - resist)))
    h, l = split(below(*slopes), 2)
    both = dot(h, table("down_cols"))
    narrow = both[:, :LANES] + (both[:, LANES:] + dot(l, table("down_cols")[:, :LANES]))
    narrow = beside(*[narrow[c * pad_width : (c + 1) * pad_width] for c in range(CONDITIONS)])
    h, l = split(narrow, 2)
    both = dot(table("down_rows"), h)
    coarse = both[:grid] + (both[grid:] + dot(table("down_rows", 0, grid), l))

    backs = [[], []]
    for field in fields:
        h, l = split(field * coarse, 2)
        back = dot(table("back_rows"), below(h, l, h))
        for condition in range(CONDITIONS):
            block = back[:, condition * LANES : (condition + 1) * LANES]
            turned = pltpu.roll(block[BAND:], LANES // 2, 1)
            backs[condition].append(block[:BAND] + jnp.where(low, -turned, turned))
    h, l = split(below(*backs[0], *backs[1]), 2)
    backs = dot(beside(h, l), table("back_cols", 0, 2 * LANES)) + dot(
        h, table("back_cols", 2 * LANES)
    )
    total = 0.0
    for index, spectrum in enumerate(spectra):
        total = total + spectrum * backs[index * BAND : (index + 1) * BAND]

    h, l = split(total, 2)
    across = dot(beside(h, l), table("core_cols", 0, 2 * LANES)) + dot(
        h, table("core_cols", 2 * LANES)
    )
    core_width = across.shape[1] // 2
    h, l = split(below(across[:, :core_width], across[:, core_width:]), 2)
    gradient = dot(table("core_rows"), below(h, l, h))
    own = mask[core, core]
    cells = gradient * own * (1.0 - own)
    grad_ref[...] = cells
    square = jnp.sum(jnp.sum(cells * cells, axis=0, keepdims=True), axis=1, keepdims=True)
    loss = jnp.sum(jnp.sum(loss, axis=0, keepdims=True), axis=1, keepdims=True)
    sums = jnp.concatenate([square, loss], axis=0)
    sums_ref[...] = jnp.broadcast_to(sums[None], sums_ref.shape)


def small(megabytes):
    return pltpu.CompilerParams(vmem_limit_bytes=megabytes * 1024 * 1024)


def to_all(value):
    return lax.all_to_all(value, ("row", "col"), 0, 0)


def pair_swap(value, axis, first, wrap=False):
    count = lax.axis_size(axis)
    pairs = []
    for low in range(first, count - 1, 2):
        pairs += [(low, low + 1), (low + 1, low)]
    if wrap and first and count % 2 == 0:
        pairs += [(0, count - 1), (count - 1, 0)]
    return lax.ppermute(value, axis, pairs)


def finish(cell_count, own_ref, cells_ref, sums_ref, logits_ref, loss_ref):
    total = jnp.sum(sums_ref[...], axis=0) / cell_count
    scale = STEP / jnp.sqrt(total[0:1] + EPSILON)
    logits_ref[...] = own_ref[0] - cells_ref[...] * scale
    loss_ref[...] = total[1:2, 0:1]


def shards(mask_logits, target, weight, kernels):
    core_width = mask_logits.shape[0]
    pad_width = core_width + 2 * HALO
    rows, cols = lax.axis_size("row"), lax.axis_size("col")
    f32 = jnp.float32

    def struct(*shape):
        return jax.ShapeDtypeStruct(shape, f32)

    packed = struct(core_width * 3 // 2, core_width)
    own = jnp.stack([mask_logits, target, weight])
    slab_a, slab_b = pl.pallas_call(
        pack_columns,
        out_shape=(packed, packed),
        in_specs=[VMEM],
        out_specs=(VMEM,) * 2,
        compiler_params=small(4),
    )(own)
    bank = jnp.broadcast_to(kernels[None], (rows * cols,) + kernels.shape)
    got_a, got_b = pair_swap(slab_a, "col", 0), pair_swap(slab_b, "col", 1)
    slab = struct(3, HALO, pad_width)
    centre, up, down, bank = pl.pallas_call(
        widen,
        out_shape=(struct(3, core_width, pad_width), slab, slab, struct(*bank.shape)),
        in_specs=[VMEM] * 4,
        out_specs=(VMEM,) * 4,
        compiler_params=small(8),
    )(own, got_a, got_b, bank)
    up, down = pair_swap(up, "row", 0), pair_swap(down, "row", 1, wrap=True)
    bank = to_all(bank)
    pieces = kernels.shape[1] // LANES
    if kernels.shape[1] % LANES:
        bank = jnp.swapaxes(bank, 0, 1).reshape(1, CONDITIONS, -1)
        pieces = bank.shape[2] // LANES
    order = [(device, piece) for device in range(bank.shape[0]) for piece in range(pieces)]

    consts, place = tables(pad_width, HALO)
    grad_cells, sums = pl.pallas_call(
        functools.partial(step_kernel, order, place),
        out_shape=(
            struct(core_width, core_width),
            struct(rows * cols, 2, LANES),
        ),
        in_specs=[VMEM] * 6,
        out_specs=(VMEM,) * 2,
        scratch_shapes=[pltpu.VMEM((CONDITIONS, len(order), LANES), f32)],
        compiler_params=pltpu.CompilerParams(vmem_limit_bytes=16 * 1024 * 1024),
    )(bank, centre, up, down, *consts)

    sums = to_all(sums)
    cell_count = rows * cols * core_width * core_width
    new_logits, loss = pl.pallas_call(
        functools.partial(finish, cell_count),
        out_shape=(struct(core_width, core_width), struct(1, 1)),
        in_specs=[VMEM] * 3,
        out_specs=(VMEM,) * 2,
        compiler_params=small(4),
    )(own, grad_cells, sums)
    return (new_logits, loss[0, 0])


def solution(mesh):
    placed = (P("row", "col"), P("row", "col"), P("row", "col"), P(None, ("row", "col")))
    return jax.shard_map(
        shards, mesh=mesh, in_specs=placed, out_specs=(P("row", "col"), P()), check_vma=False
    )
```

```python
import functools
import math

import jax
import jax.numpy as jnp
import numpy as np
from jax import lax
from jax.experimental import pallas as pl
from jax.experimental.pallas import tpu as pltpu
from jax.sharding import PartitionSpec as P

HALO = 64
KERNELS = 6
BAND = 32
CONDITIONS = 2

SHARPNESS = 6.0
THRESHOLD = 0.75
STEP = 0.5
EPSILON = 1e-06
DOSES = (1.0, 1.15)

LANES = 128
VMEM = pl.BlockSpec(memory_space=pltpu.VMEM)


def dot(first, second):
    return lax.dot_general(
        first, second, (((1,), (0,)), ((), ())), preferred_element_type=jnp.float32
    )


def split(value, count):
    parts = []
    for index in range(count):
        part = value.astype(jnp.bfloat16)
        parts.append(part)
        if index + 1 < count:
            value = value - part.astype(jnp.float32)
    return parts


def split_table(table, count):
    parts = []
    for _ in range(count):
        part = table.astype(np.float32).astype(jnp.bfloat16)
        parts.append(part)
        table = table - part.astype(np.float64)
    return parts


def tables(pad_width, margin):
    freq = np.arange(BAND) - BAND // 2
    place = np.arange(pad_width)
    turns = (freq[:, None] * place[None, :] % pad_width) * (2.0 * math.pi / pad_width)
    wave_re = np.cos(turns) / math.sqrt(pad_width)
    wave_im = -np.sin(turns) / math.sqrt(pad_width)
    grid = 2 * BAND
    stride = pad_width // grid
    fold = LANES // BAND
    rows = np.arange(BAND).reshape(BAND // fold, fold).T.reshape(-1)
    row_re, row_im = wave_re[rows], wave_im[rows]
    coarse_re, coarse_im = wave_re[:, ::stride], wave_im[:, ::stride]
    crow_re, crow_im = row_re[:, ::stride], row_im[:, ::stride]
    core = slice(margin, pad_width - margin)
    core_re, core_im = wave_re[:, core], wave_im[:, core]
    steps = (place[:, None] - stride * np.arange(grid)[None, :]) % pad_width
    diffs = np.arange(1, BAND)
    phases = (steps[..., None] * diffs % pad_width) * (2.0 * math.pi / pad_width)
    between = (1.0 + 2.0 * np.cos(phases).sum(-1)) / grid

    def beside(*blocks):
        return np.concatenate(blocks, axis=1)

    def below(*blocks):
        return np.concatenate(blocks, axis=0)

    found = {}
    h, l = split_table(beside(wave_re.T, wave_im.T, -wave_im.T, wave_re.T), 2)
    found["analyse_cols"] = beside(h, l)
    found["analyse_rows"] = below(*split_table(below(row_re, row_im), 3))
    from_re = beside(coarse_re, -coarse_im, -coarse_im, -coarse_re)
    from_im = beside(coarse_im, coarse_re, coarse_re, -coarse_im)
    h, m, l = split_table(below(from_re, from_im, from_re, from_im), 3)
    found["field_cols"] = below(h, m, l)
    h, m, l = split_table(beside(crow_re.T, crow_im.T), 3)
    found["field_rows"] = beside(h, h, h, m, m, l)
    h, m, l = split_table(between, 3)
    found["up_rows"] = beside(h, h, h, m, m, l)
    found["up_cols"] = below(h.T, m.T, l.T)
    found["down_cols"] = beside(h, h, m, m)
    found["down_rows"] = below(h.T, m.T)
    h, l = split_table(below(crow_re, crow_im), 2)
    found["back_rows"] = beside(h, h, l)
    c_re, c_im = coarse_re.T, coarse_im.T
    h, l = split_table(
        below(beside(c_re, c_im, c_im, -c_re), beside(-c_im, c_re, c_re, c_im)), 2
    )
    found["back_cols"] = below(h, l)
    from_re, from_im = beside(core_re, -core_im), beside(core_im, core_re)
    h, l = split_table(below(from_re, from_im, from_re, from_im), 2)
    found["core_cols"] = below(h, l)
    h, l = split_table(2.0 * beside(row_re[:, core].T, row_im[:, core].T), 2)
    found["core_rows"] = beside(h, h, l)

    pieces = []
    for name, table in found.items():
        for first in range(0, table.shape[1], 2 * LANES):
            pieces.append(((name, first // (2 * LANES)), table[:, first : first + 2 * LANES]))
    where, tops, blocks = {}, [0, 0], []
    for key, piece in sorted(pieces, key=lambda p: (p[1].shape[1] <= LANES, -p[1].shape[0])):
        thin = piece.shape[1] <= LANES
        side = int(thin and tops[1] < tops[0])
        where[key] = (tops[side], side * LANES, piece.shape)
        blocks.append((where[key], piece))
        tops[side] += piece.shape[0]
        if not thin:
            tops[1] = tops[0]
    whole = np.zeros((max(tops), 2 * LANES), jnp.bfloat16)
    for (top, left, shape), piece in blocks:
        whole[top : top + shape[0], left : left + shape[1]] = piece
    return jnp.asarray(whole), where


def pack(own_ref, a_ref, b_ref, up_ref, down_ref):
    odd_row = lax.rem(lax.axis_index("row"), 2) == 1
    for index in range(3):
        first, second = own_ref[index, :HALO], own_ref[index, HALO:]
        up_ref[index] = jnp.where(odd_row, first, second)
        down_ref[index] = jnp.where(odd_row, second, first)
    half = HALO
    odd = lax.rem(lax.axis_index("col"), 2) == 1
    values = [own_ref[index] for index in range(3)]
    turned = [pltpu.roll(value, half, 1) for value in values]
    low = lax.broadcasted_iota(jnp.int32, values[0].shape, 1) < half
    rows = values[0].shape[0]
    to_right = [
        jnp.where(low, turned[0], values[1]),
        jnp.where(low[: rows // 2], turned[2][: rows // 2], values[2][rows // 2 :]),
    ]
    to_left = [
        jnp.where(low, values[0], turned[1]),
        jnp.where(low[: rows // 2], values[2][: rows // 2], turned[2][rows // 2 :]),
    ]
    a_ref[:rows] = jnp.where(odd, to_left[0], to_right[0])
    a_ref[rows:] = jnp.where(odd, to_left[1], to_right[1])
    b_ref[:rows] = jnp.where(odd, to_right[0], to_left[0])
    b_ref[rows:] = jnp.where(odd, to_right[1], to_left[1])


def spread(shard_ref, out_ref):
    out_ref[...] = jnp.broadcast_to(shard_ref[...][None], out_ref.shape)


def widen(own_ref, a_ref, b_ref, _, __, centre_ref, up_ref, down_ref):
    half = HALO
    odd = lax.rem(lax.axis_index("col"), 2) == 1
    odd_row = lax.rem(lax.axis_index("row"), 2) == 1
    values = [own_ref[index] for index in range(3)]
    rows = values[0].shape[0]
    low = lax.broadcasted_iota(jnp.int32, values[0].shape, 1) < half
    got_a, got_b = a_ref[...], b_ref[...]
    col, cols = lax.axis_index("col"), lax.axis_size("col")
    left = jnp.where(col == 0, 0.0, jnp.where(odd, got_a, got_b))
    right = jnp.where(col == cols - 1, 0.0, jnp.where(odd, got_b, got_a))
    left_turned, right_turned = pltpu.roll(left, half, 1), pltpu.roll(right, half, 1)

    def two(first, second):
        return jnp.concatenate([first, second], axis=0)

    lefts = [left[:rows], left_turned[:rows], two(left[rows:], left_turned[rows:])]
    rights = [right_turned[:rows], right[:rows], two(right_turned[rows:], right[rows:])]
    for index, value in enumerate(values):
        turned = pltpu.roll(value, half, 1)
        wide = jnp.concatenate(
            [jnp.where(low, lefts[index], turned), jnp.where(low, turned, rights[index])], axis=1
        )
        centre_ref[index] = wide
        margin = jnp.where(low, wide[:, :LANES], wide[:, LANES:])
        up_ref[index] = jnp.where(odd_row, margin[:half], margin[half:])
        down_ref[index] = jnp.where(odd_row, margin[half:], margin[:half])


def step_kernel(
    order,
    place,
    bank_ref,
    centre_ref,
    up_ref,
    down_ref,
    up_margin_ref,
    down_margin_ref,
    table_ref,
    grad_ref,
    sums_ref,
    flat_ref,
):
    row_place = lax.axis_index("row")
    odd_row = lax.rem(row_place, 2) == 1
    at_top, at_bottom = row_place == 0, row_place == lax.axis_size("row") - 1
    grid = 2 * BAND
    fold = LANES // BAND
    per = BAND // fold

    def table(name, first=0, count=None, part=0):
        top, left, shape = place[name, part]
        top, count = top + first, shape[0] - first if count is None else count
        return table_ref[top : top + count, left : left + shape[1]]

    def three(name, h, l):
        th, tl = table(name, 0, LANES), table(name, LANES)
        return dot(beside(h, l), below(th, th)) + dot(h, tl)

    def six(name, h, m, l):
        return dot(table(name), below(h, m, l, h)) + dot(table(name, part=1), below(m, h))

    def beside(*blocks):
        return jnp.concatenate(blocks, axis=1)

    def below(*blocks):
        return jnp.concatenate(blocks, axis=0)

    low = lax.broadcasted_iota(jnp.int32, (1, LANES), 1) < LANES // 2

    def padded(index):
        wide = []
        for own_ref, margin_ref in ((up_ref, up_margin_ref), (down_ref, down_margin_ref)):
            turned, margin = pltpu.roll(own_ref[index], HALO, 1), margin_ref[index]
            wide.append(beside(jnp.where(low, margin, turned), jnp.where(low, turned, margin)))
        first, second = wide
        return below(
            jnp.where(odd_row, first, second),
            centre_ref[index],
            jnp.where(odd_row, second, first),
        )

    cell_row = lax.broadcasted_iota(jnp.int32, (centre_ref.shape[1] + 2 * HALO, 1), 0)
    first_row = jnp.where(at_top, HALO, 0)
    last_row = jnp.where(at_bottom, cell_row.shape[0] - HALO, cell_row.shape[0])
    inside = jnp.logical_and(cell_row >= first_row, cell_row < last_row)
    weight = jnp.where(inside, padded(2), 0.0)
    mask = jnp.where(weight > 0.0, jax.nn.sigmoid(padded(0)), 0.0)
    target = jnp.where(inside, padded(1), 0.0)
    pad_width = mask.shape[0]
    core = slice(HALO, pad_width - HALO)

    for row, (device, piece) in enumerate(order):
        both = bank_ref[device, :, piece * LANES : (piece + 1) * LANES]
        for condition in range(CONDITIONS):
            flat_ref[condition, row : row + 1, :] = both[condition : condition + 1]

    lane = lax.broadcasted_iota(jnp.int32, (per, LANES), 1)

    def spread(condition, kernel):
        real = flat_ref[condition, pl.ds(kernel * per, per), :]
        imag = flat_ref[condition, pl.ds((KERNELS + kernel) * per, per), :]
        reals = [real] + [pltpu.roll(real, BAND * s, 1) for s in range(1, fold)]
        imags = [imag] + [pltpu.roll(imag, BAND * s, 1) for s in range(1, fold)]
        rows = []
        for j in range(fold):
            first, second = reals[-j % fold], reals[(1 - j) % fold]
            third, fourth = imags[(2 - j) % fold], imags[(3 - j) % fold]
            rows.append(
                jnp.where(
                    lane < 2 * BAND,
                    jnp.where(lane < BAND, first, second),
                    jnp.where(lane < 3 * BAND, third, fourth),
                )
            )
        return jnp.concatenate(rows, axis=0)

    pairs = [(c, k) for c in range(CONDITIONS) for k in range(KERNELS)]
    spectra = [spread(c, k) for c, k in pairs]

    h, l = split(mask, 2)
    both = dot(h, table("analyse_cols"))
    half = both[:, :LANES] + both[:, LANES:] + dot(l, table("analyse_cols")[:, :LANES])
    h, m, l = split(half, 3)
    both = dot(table("analyse_rows", 0, 2 * grid), beside(h, m))
    rest = dot(table("analyse_rows", 2 * grid), h) + dot(table("analyse_rows", 0, grid), l)
    both = both[:grid, :LANES] + (both[:grid, LANES:] + both[grid:, :LANES]) + (both[grid:, LANES:] + rest)
    turned = pltpu.roll(both[BAND:], LANES // 2, 1)
    spectrum = both[:BAND] + jnp.where(low, turned, -turned)

    products = below(*[s * spectrum for s in spectra])
    h, m, l = split(products, 3)
    th, tm, tl = [table("field_cols", LANES * index, LANES) for index in range(3)]
    halves = (
        dot(beside(h, m), below(th, th))
        + dot(beside(h, m), below(tm, tm))
        + dot(beside(l, h), below(th, tl))
    )
    halves = split(halves, 3)
    fields = []
    square = 0.0
    for kernel in range(KERNELS):
        parts = []
        for part in halves:
            stacked = []
            for condition in range(CONDITIONS):
                first = (condition * KERNELS + kernel) * BAND
                rows = part[first : first + BAND]
                stacked.append(below(rows[:, :LANES], rows[:, LANES:]))
            parts.append(beside(*stacked))
        field = six("field_rows", *parts)
        fields.append(field)
        square = square + field * field

    square = below(*[square[:, c * LANES : (c + 1) * LANES] for c in range(CONDITIONS)])
    square = square + pltpu.roll(square, LANES // 2, 1)
    h, m, l = [part.astype(jnp.float32) for part in split(square, 3)]
    mixed = [jnp.where(low, h, m), jnp.where(low, l, h), jnp.where(low, m, h)]
    th, tm, tl = [table("up_cols", grid * index, grid) for index in range(3)]
    mixed = beside(*[part.astype(jnp.bfloat16) for part in mixed])
    tall = dot(mixed, below(th, th, th, tm, tm, tl))
    tall = split(tall, 3)

    slopes = []
    loss = 0.0
    for condition, dose in enumerate(DOSES):
        parts = [part[condition * grid : (condition + 1) * grid] for part in tall]
        intensity = six("up_rows", *parts)
        resist = jax.nn.sigmoid(SHARPNESS * (dose * intensity - THRESHOLD))
        error = resist - target
        scaled = weight * error
        loss = loss + (scaled * error)[core, core]
        slopes.append((2.0 * SHARPNESS * dose) * scaled * (resist * (1.0 - resist)))
    h, l = split(below(*slopes), 2)
    both = dot(h, table("down_cols"))
    narrow = both[:, :LANES] + (both[:, LANES:] + dot(l, table("down_cols")[:, :LANES]))
    narrow = beside(*[narrow[c * pad_width : (c + 1) * pad_width] for c in range(CONDITIONS)])
    h, l = split(narrow, 2)
    both = dot(table("down_rows"), h)
    coarse = both[:grid] + (both[grid:] + dot(table("down_rows", 0, grid), l))

    backs = [[], []]
    for field in fields:
        h, l = split(field * coarse, 2)
        back = dot(table("back_rows"), below(h, l, h))
        for condition in range(CONDITIONS):
            block = back[:, condition * LANES : (condition + 1) * LANES]
            turned = pltpu.roll(block[BAND:], LANES // 2, 1)
            backs[condition].append(block[:BAND] + jnp.where(low, -turned, turned))
    h, l = split(below(*backs[0], *backs[1]), 2)
    backs = three("back_cols", h, l)
    total = 0.0
    for index, spectrum in enumerate(spectra):
        total = total + spectrum * backs[index * BAND : (index + 1) * BAND]

    h, l = split(total, 2)
    across = three("core_cols", h, l)
    core_width = across.shape[1] // 2
    h, l = split(below(across[:, :core_width], across[:, core_width:]), 2)
    gradient = dot(table("core_rows"), below(h, l, h))
    own = mask[core, core]
    cells = gradient * own * (1.0 - own)
    grad_ref[...] = cells
    square = jnp.sum(jnp.sum(cells * cells, axis=0, keepdims=True), axis=1, keepdims=True)
    loss = jnp.sum(jnp.sum(loss, axis=0, keepdims=True), axis=1, keepdims=True)
    sums = jnp.concatenate([square, loss], axis=0)
    sums_ref[...] = jnp.broadcast_to(sums[None], sums_ref.shape)


def small(megabytes):
    return pltpu.CompilerParams(vmem_limit_bytes=megabytes * 1024 * 1024)


def to_all(value):
    return lax.all_to_all(value, ("row", "col"), 0, 0)


def pair_swap(value, axis, first, wrap=False):
    count = lax.axis_size(axis)
    pairs = []
    for low in range(first, count - 1, 2):
        pairs += [(low, low + 1), (low + 1, low)]
    if wrap and first and count % 2 == 0:
        pairs += [(0, count - 1), (count - 1, 0)]
    return lax.ppermute(value, axis, pairs)


def finish(cell_count, own_ref, cells_ref, sums_ref, logits_ref, loss_ref):
    total = jnp.sum(sums_ref[...], axis=0) / cell_count
    scale = STEP / jnp.sqrt(total[0:1] + EPSILON)
    logits_ref[...] = own_ref[0] - cells_ref[...] * scale
    loss_ref[...] = total[1:2, 0:1]


def shards(mask_logits, target, weight, kernels):
    core_width = mask_logits.shape[0]
    pad_width = core_width + 2 * HALO
    rows, cols = lax.axis_size("row"), lax.axis_size("col")
    f32 = jnp.float32

    def struct(*shape):
        return jax.ShapeDtypeStruct(shape, f32)

    packed = struct(core_width * 3 // 2, core_width)
    own = jnp.stack([mask_logits, target, weight])
    slab = struct(3, HALO, core_width)
    slab_a, slab_b, up, down = pl.pallas_call(
        pack,
        out_shape=(packed, packed, slab, slab),
        in_specs=[VMEM],
        out_specs=(VMEM,) * 4,
        compiler_params=small(4),
    )(own)
    bank = pl.pallas_call(
        spread,
        out_shape=struct(rows * cols, *kernels.shape),
        in_specs=[VMEM],
        out_specs=VMEM,
        compiler_params=small(4),
    )(kernels)
    got_a, got_b = pair_swap(slab_a, "col", 0), pair_swap(slab_b, "col", 1, wrap=True)
    up, down = pair_swap(up, "row", 0), pair_swap(down, "row", 1, wrap=True)
    centre, up_margin, down_margin = pl.pallas_call(
        widen,
        out_shape=(struct(3, core_width, pad_width), slab, slab),
        in_specs=[VMEM] * 3 + [pl.BlockSpec(memory_space=pl.ANY)] * 2,
        out_specs=(VMEM,) * 3,
        compiler_params=small(8),
    )(own, got_a, got_b, up, down)
    up_margin, down_margin = (
        pair_swap(up_margin, "row", 0),
        pair_swap(down_margin, "row", 1, wrap=True),
    )
    bank = to_all(bank)
    pieces = kernels.shape[1] // LANES
    if kernels.shape[1] % LANES:
        bank = jnp.swapaxes(bank, 0, 1).reshape(1, CONDITIONS, -1)
        pieces = bank.shape[2] // LANES
    order = [(device, piece) for device in range(bank.shape[0]) for piece in range(pieces)]

    consts, place = tables(pad_width, HALO)
    grad_cells, sums = pl.pallas_call(
        functools.partial(step_kernel, order, place),
        out_shape=(
            struct(core_width, core_width),
            struct(rows * cols, 2, LANES),
        ),
        in_specs=[VMEM] * 7,
        out_specs=(VMEM,) * 2,
        scratch_shapes=[pltpu.VMEM((CONDITIONS, len(order), LANES), f32)],
        compiler_params=pltpu.CompilerParams(vmem_limit_bytes=16 * 1024 * 1024),
    )(bank, centre, up, down, up_margin, down_margin, consts)

    sums = to_all(sums)
    cell_count = rows * cols * core_width * core_width
    new_logits, loss = pl.pallas_call(
        functools.partial(finish, cell_count),
        out_shape=(struct(core_width, core_width), struct(1, 1)),
        in_specs=[VMEM] * 3,
        out_specs=(VMEM,) * 2,
        compiler_params=small(4),
    )(own, grad_cells, sums)
    return (new_logits, loss[0, 0])


def solution(mesh):
    placed = (P("row", "col"), P("row", "col"), P("row", "col"), P(None, ("row", "col")))
    return jax.shard_map(
        shards, mesh=mesh, in_specs=placed, out_specs=(P("row", "col"), P()), check_vma=False
    )
```

```python
import functools
import math

import jax
import jax.numpy as jnp
import numpy as np
from jax import lax
from jax.experimental import pallas as pl
from jax.experimental.pallas import tpu as pltpu
from jax.sharding import PartitionSpec as P

HALO = 64
KERNELS = 6
BAND = 32
CONDITIONS = 2

SHARPNESS = 6.0
THRESHOLD = 0.75
STEP = 0.5
EPSILON = 1e-06
DOSES = (1.0, 1.15)

LANES = 128
VMEM = pl.BlockSpec(memory_space=pltpu.VMEM)


def dot(first, second):
    return lax.dot_general(
        first, second, (((1,), (0,)), ((), ())), preferred_element_type=jnp.float32
    )


def split(value, count):
    parts = []
    for index in range(count):
        part = value.astype(jnp.bfloat16)
        parts.append(part)
        if index + 1 < count:
            value = value - part.astype(jnp.float32)
    return parts


def split_table(table, count):
    parts = []
    for _ in range(count):
        part = table.astype(np.float32).astype(jnp.bfloat16)
        parts.append(part)
        table = table - part.astype(np.float64)
    return parts


def tables(pad_width, margin):
    freq = np.arange(BAND) - BAND // 2
    place = np.arange(pad_width)
    turns = (freq[:, None] * place[None, :] % pad_width) * (2.0 * math.pi / pad_width)
    wave_re = np.cos(turns) / math.sqrt(pad_width)
    wave_im = -np.sin(turns) / math.sqrt(pad_width)
    grid = 2 * BAND
    stride = pad_width // grid
    fold = LANES // BAND
    rows = np.arange(BAND).reshape(BAND // fold, fold).T.reshape(-1)
    row_re, row_im = wave_re[rows], wave_im[rows]
    coarse_re, coarse_im = wave_re[:, ::stride], wave_im[:, ::stride]
    crow_re, crow_im = row_re[:, ::stride], row_im[:, ::stride]
    core = slice(margin, pad_width - margin)
    core_re, core_im = wave_re[:, core], wave_im[:, core]
    steps = (place[:, None] - stride * np.arange(grid)[None, :]) % pad_width
    diffs = np.arange(1, BAND)
    phases = (steps[..., None] * diffs % pad_width) * (2.0 * math.pi / pad_width)
    between = (1.0 + 2.0 * np.cos(phases).sum(-1)) / grid

    def beside(*blocks):
        return np.concatenate(blocks, axis=1)

    def below(*blocks):
        return np.concatenate(blocks, axis=0)

    found = {}
    h, l = split_table(beside(wave_re.T, wave_im.T, -wave_im.T, wave_re.T), 2)
    found["analyse_cols"] = beside(h, l)
    found["analyse_rows"] = below(*split_table(below(row_re, row_im), 3))
    from_re = beside(coarse_re, -coarse_im, -coarse_im, -coarse_re)
    from_im = beside(coarse_im, coarse_re, coarse_re, -coarse_im)
    h, m, l = split_table(below(from_re, from_im, from_re, from_im), 3)
    found["field_cols"] = below(h, m, l)
    h, m, l = split_table(beside(crow_re.T, crow_im.T), 3)
    found["field_rows"] = beside(h, h, h, m, m, l)
    h, m, l = split_table(between, 3)
    found["up_rows"] = beside(h, h, h, m, m, l)
    found["up_cols"] = below(h.T, m.T, l.T)
    found["down_cols"] = beside(h, h, m, m)
    found["down_rows"] = below(h.T, m.T)
    h, l = split_table(below(crow_re, crow_im), 2)
    found["back_rows"] = beside(h, h, l)
    c_re, c_im = coarse_re.T, coarse_im.T
    h, l = split_table(
        below(beside(c_re, c_im, c_im, -c_re), beside(-c_im, c_re, c_re, c_im)), 2
    )
    found["back_cols"] = below(h, l)
    from_re, from_im = beside(core_re, -core_im), beside(core_im, core_re)
    h, l = split_table(below(from_re, from_im, from_re, from_im), 2)
    found["core_cols"] = below(h, l)
    h, l = split_table(2.0 * beside(row_re[:, core].T, row_im[:, core].T), 2)
    found["core_rows"] = beside(h, h, l)

    pieces = []
    for name, table in found.items():
        for first in range(0, table.shape[1], 2 * LANES):
            pieces.append(((name, first // (2 * LANES)), table[:, first : first + 2 * LANES]))
    where, tops, blocks = {}, [0, 0], []
    for key, piece in sorted(pieces, key=lambda p: (p[1].shape[1] <= LANES, -p[1].shape[0])):
        thin = piece.shape[1] <= LANES
        side = int(thin and tops[1] < tops[0])
        where[key] = (tops[side], side * LANES, piece.shape)
        blocks.append((where[key], piece))
        tops[side] += piece.shape[0]
        if not thin:
            tops[1] = tops[0]
    whole = np.zeros((max(tops), 2 * LANES), jnp.bfloat16)
    for (top, left, shape), piece in blocks:
        whole[top : top + shape[0], left : left + shape[1]] = piece
    return jnp.asarray(whole), where


def pack(held_ref, own_ref, a_ref, b_ref, up_ref, down_ref, bank_ref):
    cells, width = own_ref.shape[1:]
    for index in range(3):
        own_ref[index] = held_ref[:cells, index * width : (index + 1) * width]
    shard = held_ref[cells : cells + CONDITIONS, : bank_ref.shape[2]]
    bank_ref[...] = jnp.broadcast_to(shard[None], bank_ref.shape)
    odd_row = lax.rem(lax.axis_index("row"), 2) == 1
    for index in range(3):
        first, second = own_ref[index, :HALO], own_ref[index, HALO:]
        up_ref[index] = jnp.where(odd_row, first, second)
        down_ref[index] = jnp.where(odd_row, second, first)
    half = HALO
    odd = lax.rem(lax.axis_index("col"), 2) == 1
    values = [own_ref[index] for index in range(3)]
    turned = [pltpu.roll(value, half, 1) for value in values]
    low = lax.broadcasted_iota(jnp.int32, values[0].shape, 1) < half
    rows = values[0].shape[0]
    to_right = [
        jnp.where(low, turned[0], values[1]),
        jnp.where(low[: rows // 2], turned[2][: rows // 2], values[2][rows // 2 :]),
    ]
    to_left = [
        jnp.where(low, values[0], turned[1]),
        jnp.where(low[: rows // 2], values[2][: rows // 2], turned[2][rows // 2 :]),
    ]
    a_ref[:rows] = jnp.where(odd, to_left[0], to_right[0])
    a_ref[rows:] = jnp.where(odd, to_left[1], to_right[1])
    b_ref[:rows] = jnp.where(odd, to_right[0], to_left[0])
    b_ref[rows:] = jnp.where(odd, to_right[1], to_left[1])


def widen(own_ref, a_ref, b_ref, _, __, centre_ref, up_ref, down_ref):
    half = HALO
    odd = lax.rem(lax.axis_index("col"), 2) == 1
    odd_row = lax.rem(lax.axis_index("row"), 2) == 1
    values = [own_ref[index] for index in range(3)]
    rows = values[0].shape[0]
    low = lax.broadcasted_iota(jnp.int32, values[0].shape, 1) < half
    got_a, got_b = a_ref[...], b_ref[...]
    col, cols = lax.axis_index("col"), lax.axis_size("col")
    left = jnp.where(col == 0, 0.0, jnp.where(odd, got_a, got_b))
    right = jnp.where(col == cols - 1, 0.0, jnp.where(odd, got_b, got_a))
    left_turned, right_turned = pltpu.roll(left, half, 1), pltpu.roll(right, half, 1)

    def two(first, second):
        return jnp.concatenate([first, second], axis=0)

    lefts = [left[:rows], left_turned[:rows], two(left[rows:], left_turned[rows:])]
    rights = [right_turned[:rows], right[:rows], two(right_turned[rows:], right[rows:])]
    for index, value in enumerate(values):
        turned = pltpu.roll(value, half, 1)
        wide = jnp.concatenate(
            [jnp.where(low, lefts[index], turned), jnp.where(low, turned, rights[index])], axis=1
        )
        centre_ref[index] = wide
        margin = jnp.where(low, wide[:, :LANES], wide[:, LANES:])
        up_ref[index] = jnp.where(odd_row, margin[:half], margin[half:])
        down_ref[index] = jnp.where(odd_row, margin[half:], margin[:half])


def step_kernel(
    order,
    place,
    bank_ref,
    centre_ref,
    up_ref,
    down_ref,
    up_margin_ref,
    down_margin_ref,
    table_ref,
    grad_ref,
    sums_ref,
    flat_ref,
):
    row_place = lax.axis_index("row")
    odd_row = lax.rem(row_place, 2) == 1
    at_top, at_bottom = row_place == 0, row_place == lax.axis_size("row") - 1
    grid = 2 * BAND
    fold = LANES // BAND
    per = BAND // fold

    def table(name, first=0, count=None, part=0):
        top, left, shape = place[name, part]
        top, count = top + first, shape[0] - first if count is None else count
        return table_ref[top : top + count, left : left + shape[1]]

    def three(name, h, l):
        th, tl = table(name, 0, LANES), table(name, LANES)
        return dot(beside(h, l), below(th, th)) + dot(h, tl)

    def six(name, h, m, l):
        return dot(table(name), below(h, m, l, h)) + dot(table(name, part=1), below(m, h))

    def beside(*blocks):
        return jnp.concatenate(blocks, axis=1)

    def below(*blocks):
        return jnp.concatenate(blocks, axis=0)

    low = lax.broadcasted_iota(jnp.int32, (1, LANES), 1) < LANES // 2

    def padded(index):
        wide = []
        for own_ref, margin_ref in ((up_ref, up_margin_ref), (down_ref, down_margin_ref)):
            turned, margin = pltpu.roll(own_ref[index], HALO, 1), margin_ref[index]
            wide.append(beside(jnp.where(low, margin, turned), jnp.where(low, turned, margin)))
        first, second = wide
        return below(
            jnp.where(odd_row, first, second),
            centre_ref[index],
            jnp.where(odd_row, second, first),
        )

    cell_row = lax.broadcasted_iota(jnp.int32, (centre_ref.shape[1] + 2 * HALO, 1), 0)
    first_row = jnp.where(at_top, HALO, 0)
    last_row = jnp.where(at_bottom, cell_row.shape[0] - HALO, cell_row.shape[0])
    inside = jnp.logical_and(cell_row >= first_row, cell_row < last_row)
    weight = jnp.where(inside, padded(2), 0.0)
    mask = jnp.where(weight > 0.0, jax.nn.sigmoid(padded(0)), 0.0)
    target = jnp.where(inside, padded(1), 0.0)
    pad_width = mask.shape[0]
    core = slice(HALO, pad_width - HALO)

    for row, (device, piece) in enumerate(order):
        both = bank_ref[device, :, piece * LANES : (piece + 1) * LANES]
        for condition in range(CONDITIONS):
            flat_ref[condition, row : row + 1, :] = both[condition : condition + 1]

    lane = lax.broadcasted_iota(jnp.int32, (per, LANES), 1)

    def spread(condition, kernel):
        real = flat_ref[condition, pl.ds(kernel * per, per), :]
        imag = flat_ref[condition, pl.ds((KERNELS + kernel) * per, per), :]
        reals = [real] + [pltpu.roll(real, BAND * s, 1) for s in range(1, fold)]
        imags = [imag] + [pltpu.roll(imag, BAND * s, 1) for s in range(1, fold)]
        rows = []
        for j in range(fold):
            first, second = reals[-j % fold], reals[(1 - j) % fold]
            third, fourth = imags[(2 - j) % fold], imags[(3 - j) % fold]
            rows.append(
                jnp.where(
                    lane < 2 * BAND,
                    jnp.where(lane < BAND, first, second),
                    jnp.where(lane < 3 * BAND, third, fourth),
                )
            )
        return jnp.concatenate(rows, axis=0)

    pairs = [(c, k) for c in range(CONDITIONS) for k in range(KERNELS)]
    spectra = [spread(c, k) for c, k in pairs]

    h, l = split(mask, 2)
    both = dot(h, table("analyse_cols"))
    half = both[:, :LANES] + both[:, LANES:] + dot(l, table("analyse_cols")[:, :LANES])
    h, m, l = split(half, 3)
    both = dot(table("analyse_rows", 0, 2 * grid), beside(h, m))
    rest = dot(table("analyse_rows", 2 * grid), h) + dot(table("analyse_rows", 0, grid), l)
    both = both[:grid, :LANES] + (both[:grid, LANES:] + both[grid:, :LANES]) + (both[grid:, LANES:] + rest)
    turned = pltpu.roll(both[BAND:], LANES // 2, 1)
    spectrum = both[:BAND] + jnp.where(low, turned, -turned)

    products = below(*[s * spectrum for s in spectra])
    h, m, l = split(products, 3)
    th, tm, tl = [table("field_cols", LANES * index, LANES) for index in range(3)]
    halves = (
        dot(beside(h, m), below(th, th))
        + dot(beside(h, m), below(tm, tm))
        + dot(beside(l, h), below(th, tl))
    )
    halves = split(halves, 3)
    fields = []
    square = 0.0
    for kernel in range(KERNELS):
        parts = []
        for part in halves:
            stacked = []
            for condition in range(CONDITIONS):
                first = (condition * KERNELS + kernel) * BAND
                rows = part[first : first + BAND]
                stacked.append(below(rows[:, :LANES], rows[:, LANES:]))
            parts.append(beside(*stacked))
        field = six("field_rows", *parts)
        fields.append(field)
        square = square + field * field

    square = below(*[square[:, c * LANES : (c + 1) * LANES] for c in range(CONDITIONS)])
    square = square + pltpu.roll(square, LANES // 2, 1)
    h, m, l = [part.astype(jnp.float32) for part in split(square, 3)]
    mixed = [jnp.where(low, h, m), jnp.where(low, l, h), jnp.where(low, m, h)]
    th, tm, tl = [table("up_cols", grid * index, grid) for index in range(3)]
    mixed = beside(*[part.astype(jnp.bfloat16) for part in mixed])
    tall = dot(mixed, below(th, th, th, tm, tm, tl))
    tall = split(tall, 3)

    slopes = []
    loss = 0.0
    for condition, dose in enumerate(DOSES):
        parts = [part[condition * grid : (condition + 1) * grid] for part in tall]
        intensity = six("up_rows", *parts)
        resist = jax.nn.sigmoid(SHARPNESS * (dose * intensity - THRESHOLD))
        error = resist - target
        scaled = weight * error
        loss = loss + (scaled * error)[core, core]
        slopes.append((2.0 * SHARPNESS * dose) * scaled * (resist * (1.0 - resist)))
    h, l = split(below(*slopes), 2)
    both = dot(h, table("down_cols"))
    narrow = both[:, :LANES] + (both[:, LANES:] + dot(l, table("down_cols")[:, :LANES]))
    narrow = beside(*[narrow[c * pad_width : (c + 1) * pad_width] for c in range(CONDITIONS)])
    h, l = split(narrow, 2)
    both = dot(table("down_rows"), h)
    coarse = both[:grid] + (both[grid:] + dot(table("down_rows", 0, grid), l))

    backs = [[], []]
    for field in fields:
        h, l = split(field * coarse, 2)
        back = dot(table("back_rows"), below(h, l, h))
        for condition in range(CONDITIONS):
            block = back[:, condition * LANES : (condition + 1) * LANES]
            turned = pltpu.roll(block[BAND:], LANES // 2, 1)
            backs[condition].append(block[:BAND] + jnp.where(low, -turned, turned))
    h, l = split(below(*backs[0], *backs[1]), 2)
    backs = three("back_cols", h, l)
    total = 0.0
    for index, spectrum in enumerate(spectra):
        total = total + spectrum * backs[index * BAND : (index + 1) * BAND]

    h, l = split(total, 2)
    across = three("core_cols", h, l)
    core_width = across.shape[1] // 2
    h, l = split(below(across[:, :core_width], across[:, core_width:]), 2)
    gradient = dot(table("core_rows"), below(h, l, h))
    own = mask[core, core]
    cells = gradient * own * (1.0 - own)
    grad_ref[...] = cells
    square = jnp.sum(jnp.sum(cells * cells, axis=0, keepdims=True), axis=1, keepdims=True)
    loss = jnp.sum(jnp.sum(loss, axis=0, keepdims=True), axis=1, keepdims=True)
    sums = jnp.concatenate([square, loss], axis=0)
    sums_ref[...] = jnp.broadcast_to(sums[None], sums_ref.shape)


def small(megabytes):
    return pltpu.CompilerParams(vmem_limit_bytes=megabytes * 1024 * 1024)


def to_all(value):
    return lax.all_to_all(value, ("row", "col"), 0, 0)


def pair_swap(value, axis, first):
    if axis == "row":
        count = lax.axis_size(axis)
        pairs = []
        for low in range(first, count - 1, 2):
            pairs += [(low, low + 1), (low + 1, low)]
        if first and count % 2 == 0:
            pairs += [(0, count - 1), (count - 1, 0)]
        return lax.ppermute(value, axis, pairs)
    sizes = lax.axis_size("row"), lax.axis_size("col")
    along = ("row", "col").index(axis)
    pairs = []
    for place in np.ndindex(*sizes):
        other = list(place)
        step = 1 if (place[along] - first) % 2 == 0 else -1
        if 0 <= place[along] + step < sizes[along]:
            other[along] += step
        elif 0 <= place[1 - along] ^ 1 < sizes[1 - along]:
            other[1 - along] ^= 1
        else:
            continue
        pairs.append(tuple(int(r) * sizes[1] + int(c) for r, c in (place, other)))
    return lax.ppermute(value, ("row", "col"), pairs)


def finish(cell_count, own_ref, cells_ref, sums_ref, logits_ref, loss_ref):
    total = jnp.sum(sums_ref[...], axis=0) / cell_count
    scale = STEP / jnp.sqrt(total[0:1] + EPSILON)
    logits_ref[...] = own_ref[0] - cells_ref[...] * scale
    loss_ref[...] = total[1:2, 0:1]


def shards(mask_logits, target, weight, kernels):
    core_width = mask_logits.shape[0]
    pad_width = core_width + 2 * HALO
    rows, cols = lax.axis_size("row"), lax.axis_size("col")
    f32 = jnp.float32

    def struct(*shape):
        return jax.ShapeDtypeStruct(shape, f32)

    packed = struct(core_width * 3 // 2, core_width)
    slab = struct(3, HALO, core_width)
    cells = jnp.concatenate([mask_logits, target, weight], axis=1)
    shard = jnp.pad(kernels, ((0, 0), (0, cells.shape[1] - kernels.shape[1])))
    own, slab_a, slab_b, up, down, bank = pl.pallas_call(
        pack,
        out_shape=(struct(3, core_width, core_width), packed, packed, slab, slab)
        + (struct(rows * cols, *kernels.shape),),
        in_specs=[VMEM],
        out_specs=(VMEM,) * 6,
        compiler_params=small(4),
    )(jnp.concatenate([cells, shard], axis=0))
    got_a, got_b = pair_swap(slab_a, "col", 0), pair_swap(slab_b, "col", 1)
    up, down = pair_swap(up, "row", 0), pair_swap(down, "row", 1)
    centre, up_margin, down_margin = pl.pallas_call(
        widen,
        out_shape=(struct(3, core_width, pad_width), slab, slab),
        in_specs=[VMEM] * 3 + [pl.BlockSpec(memory_space=pl.ANY)] * 2,
        out_specs=(VMEM,) * 3,
        compiler_params=small(8),
    )(own, got_a, got_b, up, down)
    up_margin, down_margin = (
        pair_swap(up_margin, "row", 0),
        pair_swap(down_margin, "row", 1),
    )
    bank = to_all(bank)
    pieces = kernels.shape[1] // LANES
    if kernels.shape[1] % LANES:
        bank = jnp.swapaxes(bank, 0, 1).reshape(1, CONDITIONS, -1)
        pieces = bank.shape[2] // LANES
    order = [(device, piece) for device in range(bank.shape[0]) for piece in range(pieces)]

    consts, place = tables(pad_width, HALO)
    grad_cells, sums = pl.pallas_call(
        functools.partial(step_kernel, order, place),
        out_shape=(
            struct(core_width, core_width),
            struct(rows * cols, 2, LANES),
        ),
        in_specs=[VMEM] * 7,
        out_specs=(VMEM,) * 2,
        scratch_shapes=[pltpu.VMEM((CONDITIONS, len(order), LANES), f32)],
        compiler_params=pltpu.CompilerParams(vmem_limit_bytes=16 * 1024 * 1024),
    )(bank, centre, up, down, up_margin, down_margin, consts)

    sums = to_all(sums)
    cell_count = rows * cols * core_width * core_width
    new_logits, loss = pl.pallas_call(
        functools.partial(finish, cell_count),
        out_shape=(struct(core_width, core_width), struct(1, 1)),
        in_specs=[VMEM] * 3,
        out_specs=(VMEM,) * 2,
        compiler_params=small(4),
    )(own, grad_cells, sums)
    return (new_logits, loss[0, 0])


def solution(mesh):
    placed = (P("row", "col"), P("row", "col"), P("row", "col"), P(None, ("row", "col")))
    return jax.shard_map(
        shards, mesh=mesh, in_specs=placed, out_specs=(P("row", "col"), P()), check_vma=False
    )
```

```python
import functools
import math

import jax
import jax.numpy as jnp
import numpy as np
from jax import lax
from jax.experimental import pallas as pl
from jax.experimental.pallas import tpu as pltpu
from jax.sharding import PartitionSpec as P

HALO = 64
KERNELS = 6
BAND = 32
CONDITIONS = 2

SHARPNESS = 6.0
THRESHOLD = 0.75
STEP = 0.5
EPSILON = 1e-06
DOSES = (1.0, 1.15)

LANES = 128
VMEM = pl.BlockSpec(memory_space=pltpu.VMEM)


def dot(first, second):
    return lax.dot_general(
        first, second, (((1,), (0,)), ((), ())), preferred_element_type=jnp.float32
    )


def split(value, count):
    parts = []
    for index in range(count):
        part = value.astype(jnp.bfloat16)
        parts.append(part)
        if index + 1 < count:
            value = value - part.astype(jnp.float32)
    return parts


def split_table(table, count):
    parts = []
    for _ in range(count):
        part = table.astype(np.float32).astype(jnp.bfloat16)
        parts.append(part)
        table = table - part.astype(np.float64)
    return parts


def tables(pad_width, margin):
    freq = np.arange(BAND) - BAND // 2
    place = np.arange(pad_width)
    turns = (freq[:, None] * place[None, :] % pad_width) * (2.0 * math.pi / pad_width)
    wave_re = np.cos(turns) / math.sqrt(pad_width)
    wave_im = -np.sin(turns) / math.sqrt(pad_width)
    grid = 2 * BAND
    stride = pad_width // grid
    fold = LANES // BAND
    rows = np.arange(BAND).reshape(BAND // fold, fold).T.reshape(-1)
    row_re, row_im = wave_re[rows], wave_im[rows]
    coarse_re, coarse_im = wave_re[:, ::stride], wave_im[:, ::stride]
    crow_re, crow_im = row_re[:, ::stride], row_im[:, ::stride]
    core = slice(margin, pad_width - margin)
    core_re, core_im = wave_re[:, core], wave_im[:, core]
    steps = (place[:, None] - stride * np.arange(grid)[None, :]) % pad_width
    diffs = np.arange(1, BAND)
    phases = (steps[..., None] * diffs % pad_width) * (2.0 * math.pi / pad_width)
    between = (1.0 + 2.0 * np.cos(phases).sum(-1)) / grid

    def beside(*blocks):
        return np.concatenate(blocks, axis=1)

    def below(*blocks):
        return np.concatenate(blocks, axis=0)

    found = {}
    h, l = split_table(beside(wave_re.T, wave_im.T, -wave_im.T, wave_re.T), 2)
    found["analyse_cols"] = beside(h, l)
    found["analyse_rows"] = below(*split_table(below(row_re, row_im), 3))
    from_re = beside(coarse_re, -coarse_im, -coarse_im, -coarse_re)
    from_im = beside(coarse_im, coarse_re, coarse_re, -coarse_im)
    h, m, l = split_table(below(from_re, from_im, from_re, from_im), 3)
    found["field_cols"] = below(h, m, l)
    h, m, l = split_table(beside(crow_re.T, crow_im.T), 3)
    found["field_rows"] = beside(h, h, h, m, m, l)
    h, m, l = split_table(between, 3)
    found["up_rows"] = beside(h, h, h, m, m, l)
    found["up_cols"] = below(h.T, m.T, l.T)
    found["down_cols"] = beside(h, h, m, m)
    found["down_rows"] = below(h.T, m.T)
    h, l = split_table(below(crow_re, crow_im), 2)
    found["back_rows"] = beside(h, h, l)
    c_re, c_im = coarse_re.T, coarse_im.T
    h, l = split_table(
        below(beside(c_re, c_im, c_im, -c_re), beside(-c_im, c_re, c_re, c_im)), 2
    )
    found["back_cols"] = below(h, l)
    from_re, from_im = beside(core_re, -core_im), beside(core_im, core_re)
    h, l = split_table(below(from_re, from_im, from_re, from_im), 2)
    found["core_cols"] = below(h, l)
    h, l = split_table(2.0 * beside(row_re[:, core].T, row_im[:, core].T), 2)
    found["core_rows"] = beside(h, h, l)

    pieces = []
    for name, table in found.items():
        for first in range(0, table.shape[1], 2 * LANES):
            pieces.append(((name, first // (2 * LANES)), table[:, first : first + 2 * LANES]))
    where, tops, blocks = {}, [0, 0], []
    for key, piece in sorted(pieces, key=lambda p: (p[1].shape[1] <= LANES, -p[1].shape[0])):
        thin = piece.shape[1] <= LANES
        side = int(thin and tops[1] < tops[0])
        where[key] = (tops[side], side * LANES, piece.shape)
        blocks.append((where[key], piece))
        tops[side] += piece.shape[0]
        if not thin:
            tops[1] = tops[0]
    whole = np.zeros((max(tops), 2 * LANES), jnp.bfloat16)
    for (top, left, shape), piece in blocks:
        whole[top : top + shape[0], left : left + shape[1]] = piece
    return jnp.asarray(whole), where


def pack(held_ref, own_ref, a_ref, b_ref, up_ref, down_ref, bank_ref):
    cells, width = own_ref.shape[1:]
    for index in range(3):
        own_ref[index] = held_ref[:cells, index * width : (index + 1) * width]
    shard = held_ref[cells : cells + CONDITIONS, : bank_ref.shape[2]]
    bank_ref[...] = jnp.broadcast_to(shard[None], bank_ref.shape)
    odd_row = lax.rem(lax.axis_index("row"), 2) == 1
    for index in range(3):
        first, second = own_ref[index, :HALO], own_ref[index, HALO:]
        up_ref[index] = jnp.where(odd_row, first, second)
        down_ref[index] = jnp.where(odd_row, second, first)
    half = HALO
    odd = lax.rem(lax.axis_index("col"), 2) == 1
    values = [own_ref[index] for index in range(3)]
    turned = [pltpu.roll(value, half, 1) for value in values]
    low = lax.broadcasted_iota(jnp.int32, values[0].shape, 1) < half
    rows = values[0].shape[0]
    to_right = [
        jnp.where(low, turned[0], values[1]),
        jnp.where(low[: rows // 2], turned[2][: rows // 2], values[2][rows // 2 :]),
    ]
    to_left = [
        jnp.where(low, values[0], turned[1]),
        jnp.where(low[: rows // 2], values[2][: rows // 2], turned[2][rows // 2 :]),
    ]
    a_ref[:rows] = jnp.where(odd, to_left[0], to_right[0])
    a_ref[rows:] = jnp.where(odd, to_left[1], to_right[1])
    b_ref[:rows] = jnp.where(odd, to_right[0], to_left[0])
    b_ref[rows:] = jnp.where(odd, to_right[1], to_left[1])


def widen(
    own_ref, a_ref, b_ref, _, __, centre_ref, up_ref, *down_refs
):
    half = HALO
    odd = lax.rem(lax.axis_index("col"), 2) == 1
    odd_row = lax.rem(lax.axis_index("row"), 2) == 1
    values = [own_ref[index] for index in range(3)]
    rows = values[0].shape[0]
    low = lax.broadcasted_iota(jnp.int32, values[0].shape, 1) < half
    got_a, got_b = a_ref[...], b_ref[...]
    col, cols = lax.axis_index("col"), lax.axis_size("col")
    left = jnp.where(col == 0, 0.0, jnp.where(odd, got_a, got_b))
    right = jnp.where(col == cols - 1, 0.0, jnp.where(odd, got_b, got_a))
    left_turned, right_turned = pltpu.roll(left, half, 1), pltpu.roll(right, half, 1)

    def two(first, second):
        return jnp.concatenate([first, second], axis=0)

    lefts = [left[:rows], left_turned[:rows], two(left[rows:], left_turned[rows:])]
    rights = [right_turned[:rows], right[:rows], two(right_turned[rows:], right[rows:])]
    margins = []
    for index, value in enumerate(values):
        turned = pltpu.roll(value, half, 1)
        wide = jnp.concatenate(
            [jnp.where(low, lefts[index], turned), jnp.where(low, turned, rights[index])], axis=1
        )
        centre_ref[index] = wide
        margins.append(jnp.where(low, wide[:, :LANES], wide[:, LANES:]))
    margins[0] = mask_of(margins[0], margins[2])
    for margin, first_ref, second_ref in zip(
        margins,
        (up_ref.at[0], up_ref.at[1], up_ref.at[2]),
        down_refs,
        strict=True,
    ):
        first_ref[...] = jnp.where(odd_row, margin[:half], margin[half:])
        second_ref[...] = jnp.where(odd_row, margin[half:], margin[:half])


def beside(*blocks):
    return jnp.concatenate(blocks, axis=1)


def below(*blocks):
    return jnp.concatenate(blocks, axis=0)


class Tables:
    def __init__(self, ref, place):
        self.ref, self.place = ref, place

    def __call__(self, name, first=0, count=None, part=0):
        top, left, shape = self.place[name, part]
        top, count = top + first, shape[0] - first if count is None else count
        return self.ref[top : top + count, left : left + shape[1]]

    def three(self, name, h, l):
        th, tl = self(name, 0, LANES), self(name, LANES)
        return dot(beside(h, l), below(th, th)) + dot(h, tl)

    def six(self, name, h, m, l):
        first = dot(self(name), below(h, m, l, h))
        return first + dot(self(name, part=1), below(m, h))


def above_below(first, second):
    row = lax.axis_index("row")
    odd = lax.rem(row, 2) == 1
    above = jnp.where(row == 0, 0.0, jnp.where(odd, first, second))
    last = row == lax.axis_size("row") - 1
    return above, jnp.where(last, 0.0, jnp.where(odd, second, first))


def spectrum_of(mask, cols, rows):
    grid = 2 * BAND
    low = lax.broadcasted_iota(jnp.int32, (1, LANES), 1) < LANES // 2
    h, l = split(mask, 2)
    both = dot(h, cols)
    half = both[:, :LANES] + both[:, LANES:] + dot(l, cols[:, :LANES])
    h, m, l = split(half, 3)
    both = dot(rows[: 2 * grid], beside(h, m))
    rest = dot(rows[2 * grid :], h) + dot(rows[:grid], l)
    middle = both[:grid, LANES:] + both[grid:, :LANES]
    both = both[:grid, :LANES] + middle + (both[grid:, LANES:] + rest)
    turned = pltpu.roll(both[BAND:], LANES // 2, 1)
    return both[:BAND] + jnp.where(low, turned, -turned)


def mask_of(logits, weight):
    return jnp.where(weight > 0.0, jax.nn.sigmoid(logits), 0.0)


def before_margins(
    place, centre_ref, up_ref, down_ref, table_ref, spectrum_ref, cells_ref, factor_ref
):
    table = Tables(table_ref, place)
    low = lax.broadcasted_iota(jnp.int32, (1, LANES), 1) < LANES // 2

    def padded(index):
        ends = []
        for own in above_below(up_ref[index], down_ref[index]):
            turned = pltpu.roll(own, HALO, 1)
            ends.append(beside(jnp.where(low, 0.0, turned), jnp.where(low, turned, 0.0)))
        return below(ends[0], centre_ref[index], ends[1])

    weight = padded(2)
    mask = mask_of(padded(0), weight)
    cells_ref[0] = padded(1)
    cells_ref[1] = weight
    core = slice(HALO, mask.shape[0] - HALO)
    own = mask[core, core]
    factor_ref[...] = own * (1.0 - own)
    spectrum_ref[...] = spectrum_of(mask, table("analyse_cols"), table("analyse_rows"))


def forward_kernel(
    order,
    place,
    bank_ref,
    spectrum_ref,
    up_margin_ref,
    down_margin_ref,
    table_ref,
    spectra_ref,
    fields_ref,
    tall_ref,
    flat_ref,
):
    grid = 2 * BAND
    fold = LANES // BAND
    per = BAND // fold
    table = Tables(table_ref, place)
    low = lax.broadcasted_iota(jnp.int32, (1, LANES), 1) < LANES // 2
    corner_mask = below(*above_below(up_margin_ref[0], down_margin_ref[...]))

    for row, (device, piece) in enumerate(order):
        both = bank_ref[device, :, piece * LANES : (piece + 1) * LANES]
        for condition in range(CONDITIONS):
            flat_ref[condition, row : row + 1, :] = both[condition : condition + 1]

    lane = lax.broadcasted_iota(jnp.int32, (per, LANES), 1)

    def spread(condition, kernel):
        real = flat_ref[condition, pl.ds(kernel * per, per), :]
        imag = flat_ref[condition, pl.ds((KERNELS + kernel) * per, per), :]
        reals = [real] + [pltpu.roll(real, BAND * s, 1) for s in range(1, fold)]
        imags = [imag] + [pltpu.roll(imag, BAND * s, 1) for s in range(1, fold)]
        rows = []
        for j in range(fold):
            first, second = reals[-j % fold], reals[(1 - j) % fold]
            third, fourth = imags[(2 - j) % fold], imags[(3 - j) % fold]
            rows.append(
                jnp.where(
                    lane < 2 * BAND,
                    jnp.where(lane < BAND, first, second),
                    jnp.where(lane < 3 * BAND, third, fourth),
                )
            )
        return jnp.concatenate(rows, axis=0)

    pairs = [(c, k) for c in range(CONDITIONS) for k in range(KERNELS)]
    spectra = [spread(c, k) for c, k in pairs]

    cols = table("analyse_cols")
    cols = below(cols[:HALO], cols[-HALO:])
    rows = table("analyse_rows").astype(jnp.float32)
    rows = jnp.where(low, rows[:, :LANES], rows[:, LANES:]).astype(jnp.bfloat16)
    spectrum = spectrum_ref[...] + spectrum_of(corner_mask, cols, rows)

    products = below(*[s * spectrum for s in spectra])
    h, m, l = split(products, 3)
    th, tm, tl = [table("field_cols", LANES * index, LANES) for index in range(3)]
    halves = (
        dot(beside(h, m), below(th, th))
        + dot(beside(h, m), below(tm, tm))
        + dot(beside(l, h), below(th, tl))
    )
    halves = split(halves, 3)
    fields = []
    square = 0.0
    for kernel in range(KERNELS):
        parts = []
        for part in halves:
            stacked = []
            for condition in range(CONDITIONS):
                first = (condition * KERNELS + kernel) * BAND
                rows = part[first : first + BAND]
                stacked.append(below(rows[:, :LANES], rows[:, LANES:]))
            parts.append(beside(*stacked))
        field = table.six("field_rows", *parts)
        fields.append(field)
        square = square + field * field

    square = below(*[square[:, c * LANES : (c + 1) * LANES] for c in range(CONDITIONS)])
    square = square + pltpu.roll(square, LANES // 2, 1)
    h, m, l = [part.astype(jnp.float32) for part in split(square, 3)]
    mixed = [jnp.where(low, h, m), jnp.where(low, l, h), jnp.where(low, m, h)]
    th, tm, tl = [table("up_cols", grid * index, grid) for index in range(3)]
    mixed = beside(*[part.astype(jnp.bfloat16) for part in mixed])
    tall = dot(mixed, below(th, th, th, tm, tm, tl))
    tall_ref[...] = tall
    for index, value in enumerate(spectra):
        spectra_ref[index] = value
    for index, value in enumerate(fields):
        fields_ref[index] = value


def backward_kernel(
    place,
    spectra_ref,
    fields_ref,
    tall_ref,
    cells_ref,
    factor_ref,
    up_margin_ref,
    down_margin_ref,
    down_weight_ref,
    table_ref,
    grad_ref,
    sums_ref,
):
    grid = 2 * BAND
    table = Tables(table_ref, place)
    low = lax.broadcasted_iota(jnp.int32, (1, LANES), 1) < LANES // 2
    pad_width = cells_ref.shape[1]
    core = slice(HALO, pad_width - HALO)

    def filled(index):
        cells = cells_ref[index]
        other = (down_margin_ref, down_weight_ref)[index][...]
        corners = above_below(up_margin_ref[index + 1], other)
        ends = []
        for corner, rows in zip(corners, (cells[:HALO], cells[-HALO:]), strict=True):
            left, right = rows[:, :LANES], rows[:, LANES:]
            ends.append(beside(jnp.where(low, corner, left), jnp.where(low, right, corner)))
        return below(ends[0], cells[core], ends[1])

    target, weight = filled(0), filled(1)
    spectra = [spectra_ref[index] for index in range(CONDITIONS * KERNELS)]
    fields = [fields_ref[index] for index in range(KERNELS)]
    tall = split(tall_ref[...], 3)
    slopes = []
    loss = 0.0
    for condition, dose in enumerate(DOSES):
        parts = [part[condition * grid : (condition + 1) * grid] for part in tall]
        intensity = table.six("up_rows", *parts)
        resist = jax.nn.sigmoid(SHARPNESS * (dose * intensity - THRESHOLD))
        error = resist - target
        scaled = weight * error
        loss = loss + (scaled * error)[core, core]
        slopes.append((2.0 * SHARPNESS * dose) * scaled * (resist * (1.0 - resist)))
    h, l = split(below(*slopes), 2)
    both = dot(h, table("down_cols"))
    narrow = both[:, :LANES] + (both[:, LANES:] + dot(l, table("down_cols")[:, :LANES]))
    narrow = beside(*[narrow[c * pad_width : (c + 1) * pad_width] for c in range(CONDITIONS)])
    h, l = split(narrow, 2)
    both = dot(table("down_rows"), h)
    coarse = both[:grid] + (both[grid:] + dot(table("down_rows", 0, grid), l))

    backs = [[], []]
    for field in fields:
        h, l = split(field * coarse, 2)
        back = dot(table("back_rows"), below(h, l, h))
        for condition in range(CONDITIONS):
            block = back[:, condition * LANES : (condition + 1) * LANES]
            turned = pltpu.roll(block[BAND:], LANES // 2, 1)
            backs[condition].append(block[:BAND] + jnp.where(low, -turned, turned))
    h, l = split(below(*backs[0], *backs[1]), 2)
    backs = table.three("back_cols", h, l)
    total = 0.0
    for index, spectrum in enumerate(spectra):
        total = total + spectrum * backs[index * BAND : (index + 1) * BAND]

    h, l = split(total, 2)
    across = table.three("core_cols", h, l)
    core_width = across.shape[1] // 2
    h, l = split(below(across[:, :core_width], across[:, core_width:]), 2)
    gradient = dot(table("core_rows"), below(h, l, h))
    cells = gradient * factor_ref[...]
    grad_ref[...] = cells
    square = jnp.sum(jnp.sum(cells * cells, axis=0, keepdims=True), axis=1, keepdims=True)
    loss = jnp.sum(jnp.sum(loss, axis=0, keepdims=True), axis=1, keepdims=True)
    sums = jnp.concatenate([square, loss], axis=0)
    sums_ref[...] = jnp.broadcast_to(sums[None], sums_ref.shape)


def small(megabytes):
    return pltpu.CompilerParams(vmem_limit_bytes=megabytes * 1024 * 1024)


def to_all(value):
    return lax.all_to_all(value, ("row", "col"), 0, 0)


def pair_swap(value, axis, first):
    sizes = lax.axis_size("row"), lax.axis_size("col")
    along = ("row", "col").index(axis)
    pairs = []
    for place in np.ndindex(*sizes):
        other = list(place)
        step = 1 if (place[along] - first) % 2 == 0 else -1
        if 0 <= place[along] + step < sizes[along]:
            other[along] += step
        elif 0 <= place[1 - along] ^ 1 < sizes[1 - along]:
            other[1 - along] ^= 1
        else:
            continue
        pairs.append(tuple(int(r) * sizes[1] + int(c) for r, c in (place, other)))
    return lax.ppermute(value, ("row", "col"), pairs)


def finish(cell_count, own_ref, cells_ref, sums_ref, logits_ref, loss_ref):
    total = jnp.sum(sums_ref[...], axis=0) / cell_count
    scale = STEP / jnp.sqrt(total[0:1] + EPSILON)
    logits_ref[...] = own_ref[0] - cells_ref[...] * scale
    loss_ref[...] = total[1:2, 0:1]


def shards(mask_logits, target, weight, kernels):
    core_width = mask_logits.shape[0]
    pad_width = core_width + 2 * HALO
    rows, cols = lax.axis_size("row"), lax.axis_size("col")
    f32 = jnp.float32

    def struct(*shape):
        return jax.ShapeDtypeStruct(shape, f32)

    packed = struct(core_width * 3 // 2, core_width)
    slab = struct(3, HALO, core_width)
    cells = jnp.concatenate([mask_logits, target, weight], axis=1)
    shard = jnp.pad(kernels, ((0, 0), (0, cells.shape[1] - kernels.shape[1])))
    own, slab_a, slab_b, up, down, bank = pl.pallas_call(
        pack,
        out_shape=(struct(3, core_width, core_width), packed, packed, slab, slab)
        + (struct(rows * cols, *kernels.shape),),
        in_specs=[VMEM],
        out_specs=(VMEM,) * 6,
        compiler_params=small(4),
    )(jnp.concatenate([cells, shard], axis=0))
    got_a, got_b = pair_swap(slab_a, "col", 0), pair_swap(slab_b, "col", 1)
    up, down = pair_swap(up, "row", 0), pair_swap(down, "row", 1)
    centre, up_margin, *down_margins = pl.pallas_call(
        widen,
        out_shape=(struct(3, core_width, pad_width), slab) + (struct(HALO, core_width),) * 3,
        in_specs=[VMEM] * 3 + [pl.BlockSpec(memory_space=pl.ANY)] * 2,
        out_specs=(VMEM,) * 5,
        compiler_params=small(8),
    )(own, got_a, got_b, up, down)
    up_margin = pair_swap(up_margin, "row", 0)
    down_margins = [pair_swap(margin, "row", 1) for margin in down_margins]
    consts, place = tables(pad_width, HALO)
    spectrum, cells, factor = pl.pallas_call(
        functools.partial(before_margins, place),
        out_shape=(
            struct(BAND, LANES),
            struct(2, pad_width, pad_width),
            struct(core_width, core_width),
        ),
        in_specs=[VMEM] * 4,
        out_specs=(VMEM,) * 3,
        compiler_params=small(16),
    )(centre, up, down, consts)
    bank = to_all(bank)
    pieces = kernels.shape[1] // LANES
    if kernels.shape[1] % LANES:
        bank = jnp.swapaxes(bank, 0, 1).reshape(1, CONDITIONS, -1)
        pieces = bank.shape[2] // LANES
    order = [(device, piece) for device in range(bank.shape[0]) for piece in range(pieces)]

    spectra, fields, tall = pl.pallas_call(
        functools.partial(forward_kernel, order, place),
        out_shape=(
            struct(CONDITIONS * KERNELS, BAND, LANES),
            struct(KERNELS, 2 * BAND, 2 * LANES),
            struct(CONDITIONS * 2 * BAND, pad_width),
        ),
        in_specs=[VMEM] * 5,
        out_specs=(VMEM,) * 3,
        scratch_shapes=[pltpu.VMEM((CONDITIONS, len(order), LANES), f32)],
        compiler_params=small(16),
    )(bank, spectrum, up_margin, down_margins[0], consts)
    grad_cells, sums = pl.pallas_call(
        functools.partial(backward_kernel, place),
        out_shape=(struct(core_width, core_width), struct(rows * cols, 2, LANES)),
        in_specs=[VMEM] * 9,
        out_specs=(VMEM,) * 2,
        compiler_params=small(16),
    )(spectra, fields, tall, cells, factor, up_margin, *down_margins[1:], consts)

    sums = to_all(sums)
    cell_count = rows * cols * core_width * core_width
    new_logits, loss = pl.pallas_call(
        functools.partial(finish, cell_count),
        out_shape=(struct(core_width, core_width), struct(1, 1)),
        in_specs=[VMEM] * 3,
        out_specs=(VMEM,) * 2,
        compiler_params=small(4),
    )(own, grad_cells, sums)
    return (new_logits, loss[0, 0])


def solution(mesh):
    placed = (P("row", "col"), P("row", "col"), P("row", "col"), P(None, ("row", "col")))
    return jax.shard_map(
        shards, mesh=mesh, in_specs=placed, out_specs=(P("row", "col"), P()), check_vma=False
    )
```

```python
import functools
import math

import jax
import jax.numpy as jnp
import numpy as np
from jax import lax
from jax.experimental import pallas as pl
from jax.experimental.pallas import tpu as pltpu
from jax.sharding import PartitionSpec as P

HALO = 64
KERNELS = 6
BAND = 32
CONDITIONS = 2

SHARPNESS = 6.0
THRESHOLD = 0.75
STEP = 0.5
EPSILON = 1e-06
DOSES = (1.0, 1.15)

LANES = 128
VMEM = pl.BlockSpec(memory_space=pltpu.VMEM)


def dot(first, second):
    return lax.dot_general(
        first, second, (((1,), (0,)), ((), ())), preferred_element_type=jnp.float32
    )


def split(value, count):
    parts = []
    for index in range(count):
        part = value.astype(jnp.bfloat16)
        parts.append(part)
        if index + 1 < count:
            value = value - part.astype(jnp.float32)
    return parts


def split_table(table, count):
    parts = []
    for _ in range(count):
        part = table.astype(np.float32).astype(jnp.bfloat16)
        parts.append(part)
        table = table - part.astype(np.float64)
    return parts


def tables(pad_width, margin):
    freq = np.arange(BAND) - BAND // 2
    place = np.arange(pad_width)
    turns = (freq[:, None] * place[None, :] % pad_width) * (2.0 * math.pi / pad_width)
    wave_re = np.cos(turns) / math.sqrt(pad_width)
    wave_im = -np.sin(turns) / math.sqrt(pad_width)
    grid = 2 * BAND
    stride = pad_width // grid
    fold = LANES // BAND
    rows = np.arange(BAND).reshape(BAND // fold, fold).T.reshape(-1)
    row_re, row_im = wave_re[rows], wave_im[rows]
    coarse_re, coarse_im = wave_re[:, ::stride], wave_im[:, ::stride]
    crow_re, crow_im = row_re[:, ::stride], row_im[:, ::stride]
    core = slice(margin, pad_width - margin)
    core_re, core_im = wave_re[:, core], wave_im[:, core]
    steps = (place[:, None] - stride * np.arange(grid)[None, :]) % pad_width
    diffs = np.arange(1, BAND)
    phases = (steps[..., None] * diffs % pad_width) * (2.0 * math.pi / pad_width)
    between = (1.0 + 2.0 * np.cos(phases).sum(-1)) / grid

    def beside(*blocks):
        return np.concatenate(blocks, axis=1)

    def below(*blocks):
        return np.concatenate(blocks, axis=0)

    found = {}
    h, l = split_table(beside(wave_re.T, wave_im.T, -wave_im.T, wave_re.T), 2)
    found["analyse_cols"] = beside(h, l)
    found["analyse_rows"] = below(*split_table(below(row_re, row_im), 3))
    from_re = beside(coarse_re, -coarse_im, -coarse_im, -coarse_re)
    from_im = beside(coarse_im, coarse_re, coarse_re, -coarse_im)
    h, m, l = split_table(below(from_re, from_im, from_re, from_im), 3)
    found["field_cols"] = below(h, m, l)
    h, m, l = split_table(beside(crow_re.T, crow_im.T), 3)
    found["field_rows"] = beside(h, h, h, m, m, l)
    h, m, l = split_table(between, 3)
    found["up_rows"] = beside(h, h, h, m, m, l)
    found["up_cols"] = below(h.T, m.T, l.T)
    found["down_cols"] = beside(h, h, m, m)
    found["down_rows"] = below(h.T, m.T)
    h, l = split_table(below(crow_re, crow_im), 2)
    found["back_rows"] = beside(h, h, l)
    c_re, c_im = coarse_re.T, coarse_im.T
    h, l = split_table(
        below(beside(c_re, c_im, c_im, -c_re), beside(-c_im, c_re, c_re, c_im)), 2
    )
    found["back_cols"] = below(h, l)
    from_re, from_im = beside(core_re, -core_im), beside(core_im, core_re)
    h, l = split_table(below(from_re, from_im, from_re, from_im), 2)
    found["core_cols"] = below(h, l)
    h, l = split_table(2.0 * beside(row_re[:, core].T, row_im[:, core].T), 2)
    found["core_rows"] = beside(h, h, l)

    pieces = []
    for name, table in found.items():
        for first in range(0, table.shape[1], 2 * LANES):
            pieces.append(((name, first // (2 * LANES)), table[:, first : first + 2 * LANES]))
    where, tops, blocks = {}, [0, 0], []
    for key, piece in sorted(pieces, key=lambda p: (p[1].shape[1] <= LANES, -p[1].shape[0])):
        thin = piece.shape[1] <= LANES
        side = int(thin and tops[1] < tops[0])
        where[key] = (tops[side], side * LANES, piece.shape)
        blocks.append((where[key], piece))
        tops[side] += piece.shape[0]
        if not thin:
            tops[1] = tops[0]
    whole = np.zeros((max(tops), 2 * LANES), jnp.bfloat16)
    for (top, left, shape), piece in blocks:
        whole[top : top + shape[0], left : left + shape[1]] = piece
    return jnp.asarray(whole), where


def pack(held_ref, own_ref, a_ref, b_ref, up_ref, down_ref, bank_ref):
    cells, width = own_ref.shape[1:]
    for index in range(3):
        own_ref[index] = held_ref[:cells, index * width : (index + 1) * width]
    shard = held_ref[cells : cells + CONDITIONS, : bank_ref.shape[2]]
    bank_ref[...] = jnp.broadcast_to(shard[None], bank_ref.shape)
    odd_row = lax.rem(lax.axis_index("row"), 2) == 1
    for index in range(3):
        first, second = own_ref[index, :HALO], own_ref[index, HALO:]
        up_ref[index] = jnp.where(odd_row, first, second)
        down_ref[index] = jnp.where(odd_row, second, first)
    half = HALO
    odd = lax.rem(lax.axis_index("col"), 2) == 1
    values = [own_ref[index] for index in range(3)]
    turned = [pltpu.roll(value, half, 1) for value in values]
    low = lax.broadcasted_iota(jnp.int32, values[0].shape, 1) < half
    rows = values[0].shape[0]
    to_right = [
        jnp.where(low, turned[0], values[1]),
        jnp.where(low[: rows // 2], turned[2][: rows // 2], values[2][rows // 2 :]),
    ]
    to_left = [
        jnp.where(low, values[0], turned[1]),
        jnp.where(low[: rows // 2], values[2][: rows // 2], turned[2][rows // 2 :]),
    ]
    a_ref[:rows] = jnp.where(odd, to_left[0], to_right[0])
    a_ref[rows:] = jnp.where(odd, to_left[1], to_right[1])
    b_ref[:rows] = jnp.where(odd, to_right[0], to_left[0])
    b_ref[rows:] = jnp.where(odd, to_right[1], to_left[1])


def widen(
    own_ref, a_ref, b_ref, _, centre_ref, up_ref, down_ref, down_weight_ref
):
    half = HALO
    odd = lax.rem(lax.axis_index("col"), 2) == 1
    odd_row = lax.rem(lax.axis_index("row"), 2) == 1
    values = [own_ref[index] for index in range(3)]
    rows = values[0].shape[0]
    low = lax.broadcasted_iota(jnp.int32, values[0].shape, 1) < half
    got_a, got_b = a_ref[...], b_ref[...]
    col, cols = lax.axis_index("col"), lax.axis_size("col")
    left = jnp.where(col == 0, 0.0, jnp.where(odd, got_a, got_b))
    right = jnp.where(col == cols - 1, 0.0, jnp.where(odd, got_b, got_a))
    left_turned, right_turned = pltpu.roll(left, half, 1), pltpu.roll(right, half, 1)

    def two(first, second):
        return jnp.concatenate([first, second], axis=0)

    lefts = [left[:rows], left_turned[:rows], two(left[rows:], left_turned[rows:])]
    rights = [right_turned[:rows], right[:rows], two(right_turned[rows:], right[rows:])]
    margins = []
    for index, value in enumerate(values):
        turned = pltpu.roll(value, half, 1)
        wide = jnp.concatenate(
            [jnp.where(low, lefts[index], turned), jnp.where(low, turned, rights[index])], axis=1
        )
        centre_ref[index] = wide
        margins.append(jnp.where(low, wide[:, :LANES], wide[:, LANES:]))
    margins[0] = mask_of(margins[0], margins[2])
    for margin, first_ref, second_ref in zip(
        margins,
        (up_ref.at[0], up_ref.at[1], up_ref.at[2]),
        (down_ref.at[0], down_ref.at[1], down_weight_ref),
        strict=True,
    ):
        first_ref[...] = jnp.where(odd_row, margin[:half], margin[half:])
        second_ref[...] = jnp.where(odd_row, margin[half:], margin[:half])


def beside(*blocks):
    return jnp.concatenate(blocks, axis=1)


def below(*blocks):
    return jnp.concatenate(blocks, axis=0)


class Tables:
    def __init__(self, ref, place):
        self.ref, self.place = ref, place

    def __call__(self, name, first=0, count=None, part=0):
        top, left, shape = self.place[name, part]
        top, count = top + first, shape[0] - first if count is None else count
        return self.ref[top : top + count, left : left + shape[1]]

    def three(self, name, h, l):
        th, tl = self(name, 0, LANES), self(name, LANES)
        return dot(beside(h, l), below(th, th)) + dot(h, tl)

    def six(self, name, h, m, l):
        first = dot(self(name), below(h, m, l, h))
        return first + dot(self(name, part=1), below(m, h))


def above_below(first, second):
    row = lax.axis_index("row")
    odd = lax.rem(row, 2) == 1
    above = jnp.where(row == 0, 0.0, jnp.where(odd, first, second))
    last = row == lax.axis_size("row") - 1
    return above, jnp.where(last, 0.0, jnp.where(odd, second, first))


def spectrum_of(mask, cols, rows):
    grid = 2 * BAND
    low = lax.broadcasted_iota(jnp.int32, (1, LANES), 1) < LANES // 2
    h, l = split(mask, 2)
    both = dot(h, cols)
    half = both[:, :LANES] + both[:, LANES:] + dot(l, cols[:, :LANES])
    h, m, l = split(half, 3)
    both = dot(rows[: 2 * grid], beside(h, m))
    rest = dot(rows[2 * grid :], h) + dot(rows[:grid], l)
    middle = both[:grid, LANES:] + both[grid:, :LANES]
    both = both[:grid, :LANES] + middle + (both[grid:, LANES:] + rest)
    turned = pltpu.roll(both[BAND:], LANES // 2, 1)
    return both[:BAND] + jnp.where(low, turned, -turned)


def mask_of(logits, weight):
    return jnp.where(weight > 0.0, jax.nn.sigmoid(logits), 0.0)


def before_margins(
    place, centre_ref, up_ref, down_ref, table_ref, spectrum_ref, cells_ref, factor_ref
):
    table = Tables(table_ref, place)
    low = lax.broadcasted_iota(jnp.int32, (1, LANES), 1) < LANES // 2

    def padded(index):
        ends = []
        for own in above_below(up_ref[index], down_ref[index]):
            turned = pltpu.roll(own, HALO, 1)
            ends.append(beside(jnp.where(low, 0.0, turned), jnp.where(low, turned, 0.0)))
        return below(ends[0], centre_ref[index], ends[1])

    weight = padded(2)
    mask = mask_of(padded(0), weight)
    cells_ref[0] = padded(1)
    cells_ref[1] = weight
    core = slice(HALO, mask.shape[0] - HALO)
    own = mask[core, core]
    factor_ref[...] = own * (1.0 - own)
    spectrum_ref[...] = spectrum_of(mask, table("analyse_cols"), table("analyse_rows"))


def forward_kernel(
    order,
    place,
    bank_ref,
    spectrum_ref,
    up_margin_ref,
    down_margin_ref,
    table_ref,
    spectra_ref,
    fields_ref,
    tall_ref,
    flat_ref,
):
    grid = 2 * BAND
    fold = LANES // BAND
    per = BAND // fold
    table = Tables(table_ref, place)
    low = lax.broadcasted_iota(jnp.int32, (1, LANES), 1) < LANES // 2
    corner_mask = below(*above_below(up_margin_ref[0], down_margin_ref[0]))

    for row, (device, piece) in enumerate(order):
        both = bank_ref[device, :, piece * LANES : (piece + 1) * LANES]
        for condition in range(CONDITIONS):
            flat_ref[condition, row : row + 1, :] = both[condition : condition + 1]

    lane = lax.broadcasted_iota(jnp.int32, (per, LANES), 1)

    def spread(condition, kernel):
        real = flat_ref[condition, pl.ds(kernel * per, per), :]
        imag = flat_ref[condition, pl.ds((KERNELS + kernel) * per, per), :]
        reals = [real] + [pltpu.roll(real, BAND * s, 1) for s in range(1, fold)]
        imags = [imag] + [pltpu.roll(imag, BAND * s, 1) for s in range(1, fold)]
        rows = []
        for j in range(fold):
            first, second = reals[-j % fold], reals[(1 - j) % fold]
            third, fourth = imags[(2 - j) % fold], imags[(3 - j) % fold]
            rows.append(
                jnp.where(
                    lane < 2 * BAND,
                    jnp.where(lane < BAND, first, second),
                    jnp.where(lane < 3 * BAND, third, fourth),
                )
            )
        return jnp.concatenate(rows, axis=0)

    pairs = [(c, k) for c in range(CONDITIONS) for k in range(KERNELS)]
    spectra = [spread(c, k) for c, k in pairs]

    cols = table("analyse_cols")
    cols = below(cols[:HALO], cols[-HALO:])
    rows = table("analyse_rows").astype(jnp.float32)
    rows = jnp.where(low, rows[:, :LANES], rows[:, LANES:]).astype(jnp.bfloat16)
    spectrum = spectrum_ref[...] + spectrum_of(corner_mask, cols, rows)

    products = below(*[s * spectrum for s in spectra])
    h, m, l = split(products, 3)
    th, tm, tl = [table("field_cols", LANES * index, LANES) for index in range(3)]
    halves = (
        dot(beside(h, m), below(th, th))
        + dot(beside(h, m), below(tm, tm))
        + dot(beside(l, h), below(th, tl))
    )
    halves = split(halves, 3)
    fields = []
    square = 0.0
    for kernel in range(KERNELS):
        parts = []
        for part in halves:
            stacked = []
            for condition in range(CONDITIONS):
                first = (condition * KERNELS + kernel) * BAND
                rows = part[first : first + BAND]
                stacked.append(below(rows[:, :LANES], rows[:, LANES:]))
            parts.append(beside(*stacked))
        field = table.six("field_rows", *parts)
        fields.append(field)
        square = square + field * field

    square = below(*[square[:, c * LANES : (c + 1) * LANES] for c in range(CONDITIONS)])
    square = square + pltpu.roll(square, LANES // 2, 1)
    h, m, l = [part.astype(jnp.float32) for part in split(square, 3)]
    mixed = [jnp.where(low, h, m), jnp.where(low, l, h), jnp.where(low, m, h)]
    th, tm, tl = [table("up_cols", grid * index, grid) for index in range(3)]
    mixed = beside(*[part.astype(jnp.bfloat16) for part in mixed])
    tall = dot(mixed, below(th, th, th, tm, tm, tl))
    tall_ref[...] = tall
    for index, value in enumerate(spectra):
        spectra_ref[index] = value
    for index, value in enumerate(fields):
        fields_ref[index] = value


def backward_kernel(
    place,
    spectra_ref,
    fields_ref,
    tall_ref,
    cells_ref,
    factor_ref,
    up_margin_ref,
    down_margin_ref,
    down_weight_ref,
    table_ref,
    grad_ref,
    sums_ref,
):
    grid = 2 * BAND
    table = Tables(table_ref, place)
    low = lax.broadcasted_iota(jnp.int32, (1, LANES), 1) < LANES // 2
    pad_width = cells_ref.shape[1]
    core = slice(HALO, pad_width - HALO)

    def filled(index):
        cells = cells_ref[index]
        other = (down_margin_ref[1], down_weight_ref[...])[index]
        corners = above_below(up_margin_ref[index + 1], other)
        ends = []
        for corner, rows in zip(corners, (cells[:HALO], cells[-HALO:]), strict=True):
            left, right = rows[:, :LANES], rows[:, LANES:]
            ends.append(beside(jnp.where(low, corner, left), jnp.where(low, right, corner)))
        return below(ends[0], cells[core], ends[1])

    target, weight = filled(0), filled(1)
    spectra = [spectra_ref[index] for index in range(CONDITIONS * KERNELS)]
    fields = [fields_ref[index] for index in range(KERNELS)]
    tall = split(tall_ref[...], 3)
    slopes = []
    loss = 0.0
    for condition, dose in enumerate(DOSES):
        parts = [part[condition * grid : (condition + 1) * grid] for part in tall]
        intensity = table.six("up_rows", *parts)
        resist = jax.nn.sigmoid(SHARPNESS * (dose * intensity - THRESHOLD))
        error = resist - target
        scaled = weight * error
        loss = loss + (scaled * error)[core, core]
        slopes.append((2.0 * SHARPNESS * dose) * scaled * (resist * (1.0 - resist)))
    h, l = split(below(*slopes), 2)
    both = dot(h, table("down_cols"))
    narrow = both[:, :LANES] + (both[:, LANES:] + dot(l, table("down_cols")[:, :LANES]))
    narrow = beside(*[narrow[c * pad_width : (c + 1) * pad_width] for c in range(CONDITIONS)])
    h, l = split(narrow, 2)
    both = dot(table("down_rows"), h)
    coarse = both[:grid] + (both[grid:] + dot(table("down_rows", 0, grid), l))

    backs = [[], []]
    for field in fields:
        h, l = split(field * coarse, 2)
        back = dot(table("back_rows"), below(h, l, h))
        for condition in range(CONDITIONS):
            block = back[:, condition * LANES : (condition + 1) * LANES]
            turned = pltpu.roll(block[BAND:], LANES // 2, 1)
            backs[condition].append(block[:BAND] + jnp.where(low, -turned, turned))
    h, l = split(below(*backs[0], *backs[1]), 2)
    backs = table.three("back_cols", h, l)
    total = 0.0
    for index, spectrum in enumerate(spectra):
        total = total + spectrum * backs[index * BAND : (index + 1) * BAND]

    h, l = split(total, 2)
    across = table.three("core_cols", h, l)
    core_width = across.shape[1] // 2
    h, l = split(below(across[:, :core_width], across[:, core_width:]), 2)
    gradient = dot(table("core_rows"), below(h, l, h))
    cells = gradient * factor_ref[...]
    grad_ref[...] = cells
    square = jnp.sum(jnp.sum(cells * cells, axis=0, keepdims=True), axis=1, keepdims=True)
    loss = jnp.sum(jnp.sum(loss, axis=0, keepdims=True), axis=1, keepdims=True)
    sums = jnp.concatenate([square, loss], axis=0)
    sums_ref[...] = jnp.broadcast_to(sums[None], sums_ref.shape)


def small(megabytes):
    return pltpu.CompilerParams(vmem_limit_bytes=megabytes * 1024 * 1024)


def to_all(value):
    return lax.all_to_all(value, ("row", "col"), 0, 0)


def pair_swap(value, axis, first):
    sizes = lax.axis_size("row"), lax.axis_size("col")
    along = ("row", "col").index(axis)
    pairs = []
    for place in np.ndindex(*sizes):
        other = list(place)
        step = 1 if (place[along] - first) % 2 == 0 else -1
        if 0 <= place[along] + step < sizes[along]:
            other[along] += step
        elif 0 <= place[1 - along] ^ 1 < sizes[1 - along]:
            other[1 - along] ^= 1
        else:
            continue
        pairs.append(tuple(int(r) * sizes[1] + int(c) for r, c in (place, other)))
    return lax.ppermute(value, ("row", "col"), pairs)


def finish(cell_count, own_ref, cells_ref, sums_ref, logits_ref, loss_ref):
    total = jnp.sum(sums_ref[...], axis=0) / cell_count
    scale = STEP / jnp.sqrt(total[0:1] + EPSILON)
    logits_ref[...] = own_ref[0] - cells_ref[...] * scale
    loss_ref[...] = total[1:2, 0:1]


def shards(mask_logits, target, weight, kernels):
    core_width = mask_logits.shape[0]
    pad_width = core_width + 2 * HALO
    rows, cols = lax.axis_size("row"), lax.axis_size("col")
    f32 = jnp.float32

    def struct(*shape):
        return jax.ShapeDtypeStruct(shape, f32)

    packed = struct(core_width * 3 // 2, core_width)
    slab = struct(3, HALO, core_width)
    cells = jnp.concatenate([mask_logits, target, weight], axis=1)
    shard = jnp.pad(kernels, ((0, 0), (0, cells.shape[1] - kernels.shape[1])))
    own, slab_a, slab_b, up, down, bank = pl.pallas_call(
        pack,
        out_shape=(struct(3, core_width, core_width), packed, packed, slab, slab)
        + (struct(rows * cols, *kernels.shape),),
        in_specs=[VMEM],
        out_specs=(VMEM,) * 6,
        compiler_params=small(4),
    )(jnp.concatenate([cells, shard], axis=0))
    got_a, got_b = pair_swap(slab_a, "col", 0), pair_swap(slab_b, "col", 1)
    up, down = pair_swap(up, "row", 0), pair_swap(down, "row", 1)
    margin = struct(2, HALO, core_width)
    centre, up_margin, down_margin, down_weight = pl.pallas_call(
        widen,
        out_shape=(struct(3, core_width, pad_width), slab, margin, struct(HALO, core_width)),
        in_specs=[VMEM] * 3 + [pl.BlockSpec(memory_space=pl.ANY)],
        out_specs=(VMEM,) * 4,
        compiler_params=small(8),
    )(own, got_a, got_b, down)
    up_margin = pair_swap(up_margin, "row", 0)
    down_margin = pair_swap(down_margin, "row", 1)
    down_weight = pair_swap(down_weight, "row", 1)
    consts, place = tables(pad_width, HALO)
    spectrum, cells, factor = pl.pallas_call(
        functools.partial(before_margins, place),
        out_shape=(
            struct(BAND, LANES),
            struct(2, pad_width, pad_width),
            struct(core_width, core_width),
        ),
        in_specs=[VMEM] * 4,
        out_specs=(VMEM,) * 3,
        compiler_params=small(16),
    )(centre, up, down, consts)
    bank = to_all(bank)
    pieces = kernels.shape[1] // LANES
    if kernels.shape[1] % LANES:
        bank = jnp.swapaxes(bank, 0, 1).reshape(1, CONDITIONS, -1)
        pieces = bank.shape[2] // LANES
    order = [(device, piece) for device in range(bank.shape[0]) for piece in range(pieces)]

    spectra, fields, tall = pl.pallas_call(
        functools.partial(forward_kernel, order, place),
        out_shape=(
            struct(CONDITIONS * KERNELS, BAND, LANES),
            struct(KERNELS, 2 * BAND, 2 * LANES),
            struct(CONDITIONS * 2 * BAND, pad_width),
        ),
        in_specs=[VMEM] * 5,
        out_specs=(VMEM,) * 3,
        scratch_shapes=[pltpu.VMEM((CONDITIONS, len(order), LANES), f32)],
        compiler_params=small(16),
    )(bank, spectrum, up_margin, down_margin, consts)
    grad_cells, sums = pl.pallas_call(
        functools.partial(backward_kernel, place),
        out_shape=(struct(core_width, core_width), struct(rows * cols, 2, LANES)),
        in_specs=[VMEM] * 9,
        out_specs=(VMEM,) * 2,
        compiler_params=small(16),
    )(spectra, fields, tall, cells, factor, up_margin, down_margin, down_weight, consts)

    sums = to_all(sums)
    cell_count = rows * cols * core_width * core_width
    new_logits, loss = pl.pallas_call(
        functools.partial(finish, cell_count),
        out_shape=(struct(core_width, core_width), struct(1, 1)),
        in_specs=[VMEM] * 3,
        out_specs=(VMEM,) * 2,
        compiler_params=small(4),
    )(own, grad_cells, sums)
    return (new_logits, loss[0, 0])


def solution(mesh):
    placed = (P("row", "col"), P("row", "col"), P("row", "col"), P(None, ("row", "col")))
    return jax.shard_map(
        shards, mesh=mesh, in_specs=placed, out_specs=(P("row", "col"), P()), check_vma=False
    )
```

```python
import functools
import math

import jax
import jax.numpy as jnp
import numpy as np
from jax import lax
from jax.experimental import pallas as pl
from jax.experimental.pallas import tpu as pltpu
from jax.sharding import PartitionSpec as P

HALO = 64
KERNELS = 6
BAND = 32
CONDITIONS = 2

SHARPNESS = 6.0
THRESHOLD = 0.75
STEP = 0.5
EPSILON = 1e-06
DOSES = (1.0, 1.15)

LANES = 128
VMEM = pl.BlockSpec(memory_space=pltpu.VMEM)


def dot(first, second):
    return lax.dot_general(
        first, second, (((1,), (0,)), ((), ())), preferred_element_type=jnp.float32
    )


def split(value, count):
    parts = []
    for index in range(count):
        part = value.astype(jnp.bfloat16)
        parts.append(part)
        if index + 1 < count:
            value = value - part.astype(jnp.float32)
    return parts


def split_table(table, count):
    parts = []
    for _ in range(count):
        part = table.astype(np.float32).astype(jnp.bfloat16)
        parts.append(part)
        table = table - part.astype(np.float64)
    return parts


def tables(pad_width, margin):
    freq = np.arange(BAND) - BAND // 2
    place = np.arange(pad_width)
    turns = (freq[:, None] * place[None, :] % pad_width) * (2.0 * math.pi / pad_width)
    wave_re = np.cos(turns) / math.sqrt(pad_width)
    wave_im = -np.sin(turns) / math.sqrt(pad_width)
    grid = 2 * BAND
    stride = pad_width // grid
    fold = LANES // BAND
    rows = np.arange(BAND).reshape(BAND // fold, fold).T.reshape(-1)
    row_re, row_im = wave_re[rows], wave_im[rows]
    coarse_re, coarse_im = wave_re[:, ::stride], wave_im[:, ::stride]
    crow_re, crow_im = row_re[:, ::stride], row_im[:, ::stride]
    core = slice(margin, pad_width - margin)
    core_re, core_im = wave_re[:, core], wave_im[:, core]
    steps = (place[:, None] - stride * np.arange(grid)[None, :]) % pad_width
    diffs = np.arange(1, BAND)
    phases = (steps[..., None] * diffs % pad_width) * (2.0 * math.pi / pad_width)
    between = (1.0 + 2.0 * np.cos(phases).sum(-1)) / grid

    def beside(*blocks):
        return np.concatenate(blocks, axis=1)

    def below(*blocks):
        return np.concatenate(blocks, axis=0)

    found = {}
    h, l = split_table(beside(wave_re.T, wave_im.T, -wave_im.T, wave_re.T), 2)
    found["analyse_cols"] = beside(h, l)
    found["analyse_rows"] = below(*split_table(below(row_re, row_im), 3))
    from_re = beside(coarse_re, -coarse_im, -coarse_im, -coarse_re)
    from_im = beside(coarse_im, coarse_re, coarse_re, -coarse_im)
    h, m, l = split_table(below(from_re, from_im, from_re, from_im), 3)
    found["field_cols"] = below(h, m, l)
    h, m, l = split_table(beside(crow_re.T, crow_im.T), 3)
    found["field_rows"] = beside(h, h, h, m, m, l)
    h, m, l = split_table(between, 3)
    found["up_rows"] = beside(h, h, h, m, m, l)
    found["up_cols"] = below(h.T, m.T, l.T)
    found["down_cols"] = beside(h, h, m, m)
    found["down_rows"] = below(h.T, m.T)
    h, l = split_table(below(crow_re, crow_im), 2)
    found["back_rows"] = beside(h, h, l)
    c_re, c_im = coarse_re.T, coarse_im.T
    h, l = split_table(
        below(beside(c_re, c_im, c_im, -c_re), beside(-c_im, c_re, c_re, c_im)), 2
    )
    found["back_cols"] = below(h, l)
    from_re, from_im = beside(core_re, -core_im), beside(core_im, core_re)
    h, l = split_table(below(from_re, from_im, from_re, from_im), 2)
    found["core_cols"] = below(h, l)
    h, l = split_table(2.0 * beside(row_re[:, core].T, row_im[:, core].T), 2)
    found["core_rows"] = beside(h, h, l)

    pieces = []
    for name, table in found.items():
        for first in range(0, table.shape[1], 2 * LANES):
            pieces.append(((name, first // (2 * LANES)), table[:, first : first + 2 * LANES]))
    where, tops, blocks = {}, [0, 0], []
    for key, piece in sorted(pieces, key=lambda p: (p[1].shape[1] <= LANES, -p[1].shape[0])):
        thin = piece.shape[1] <= LANES
        side = int(thin and tops[1] < tops[0])
        where[key] = (tops[side], side * LANES, piece.shape)
        blocks.append((where[key], piece))
        tops[side] += piece.shape[0]
        if not thin:
            tops[1] = tops[0]
    whole = np.zeros((max(tops), 2 * LANES), jnp.bfloat16)
    for (top, left, shape), piece in blocks:
        whole[top : top + shape[0], left : left + shape[1]] = piece
    return jnp.asarray(whole), where


def pack(held_ref, own_ref, a_ref, b_ref, up_ref, down_ref, bank_ref):
    cells, width = own_ref.shape[1:]
    for index in range(3):
        own_ref[index] = held_ref[:cells, index * width : (index + 1) * width]
    shard = held_ref[cells : cells + CONDITIONS, : bank_ref.shape[2]]
    bank_ref[...] = jnp.broadcast_to(shard[None], bank_ref.shape)
    odd_row = lax.rem(lax.axis_index("row"), 2) == 1
    for index in range(3):
        first, second = own_ref[index, :HALO], own_ref[index, HALO:]
        up_ref[index] = jnp.where(odd_row, first, second)
        down_ref[index] = jnp.where(odd_row, second, first)
    half = HALO
    odd = lax.rem(lax.axis_index("col"), 2) == 1
    values = [own_ref[index] for index in range(3)]
    turned = [pltpu.roll(value, half, 1) for value in values]
    low = lax.broadcasted_iota(jnp.int32, values[0].shape, 1) < half
    rows = values[0].shape[0]
    to_right = [
        jnp.where(low, turned[0], values[1]),
        jnp.where(low[: rows // 2], turned[2][: rows // 2], values[2][rows // 2 :]),
    ]
    to_left = [
        jnp.where(low, values[0], turned[1]),
        jnp.where(low[: rows // 2], values[2][: rows // 2], turned[2][rows // 2 :]),
    ]
    a_ref[:rows] = jnp.where(odd, to_left[0], to_right[0])
    a_ref[rows:] = jnp.where(odd, to_left[1], to_right[1])
    b_ref[:rows] = jnp.where(odd, to_right[0], to_left[0])
    b_ref[rows:] = jnp.where(odd, to_right[1], to_left[1])


def widen(
    own_ref, a_ref, b_ref, _, centre_ref, up_ref, first_ref, second_ref
):
    half = HALO
    odd = lax.rem(lax.axis_index("col"), 2) == 1
    odd_row = lax.rem(lax.axis_index("row"), 2) == 1
    values = [own_ref[index] for index in range(3)]
    rows = values[0].shape[0]
    low = lax.broadcasted_iota(jnp.int32, values[0].shape, 1) < half
    got_a, got_b = a_ref[...], b_ref[...]
    col, cols = lax.axis_index("col"), lax.axis_size("col")
    left = jnp.where(col == 0, 0.0, jnp.where(odd, got_a, got_b))
    right = jnp.where(col == cols - 1, 0.0, jnp.where(odd, got_b, got_a))
    left_turned, right_turned = pltpu.roll(left, half, 1), pltpu.roll(right, half, 1)

    def two(first, second):
        return jnp.concatenate([first, second], axis=0)

    lefts = [left[:rows], left_turned[:rows], two(left[rows:], left_turned[rows:])]
    rights = [right_turned[:rows], right[:rows], two(right_turned[rows:], right[rows:])]
    margins = []
    for index, value in enumerate(values):
        turned = pltpu.roll(value, half, 1)
        wide = jnp.concatenate(
            [jnp.where(low, lefts[index], turned), jnp.where(low, turned, rights[index])], axis=1
        )
        centre_ref[index] = wide
        margins.append(jnp.where(low, wide[:, :LANES], wide[:, LANES:]))
    margins[0] = mask_of(margins[0], margins[2])
    ups, downs = [], []
    for margin in margins:
        ups.append(jnp.where(odd_row, margin[:half], margin[half:]))
        downs.append(jnp.where(odd_row, margin[half:], margin[:half]))
    for index, value in enumerate(ups):
        up_ref[index] = value
    middle = half // 2
    first_ref[:half] = downs[0]
    first_ref[half:] = downs[1][:middle]
    second_ref[:middle] = downs[1][middle:]
    second_ref[middle:] = downs[2]


def beside(*blocks):
    return jnp.concatenate(blocks, axis=1)


def below(*blocks):
    return jnp.concatenate(blocks, axis=0)


class Tables:
    def __init__(self, ref, place):
        self.ref, self.place = ref, place

    def __call__(self, name, first=0, count=None, part=0):
        top, left, shape = self.place[name, part]
        top, count = top + first, shape[0] - first if count is None else count
        return self.ref[top : top + count, left : left + shape[1]]

    def three(self, name, h, l):
        th, tl = self(name, 0, LANES), self(name, LANES)
        return dot(beside(h, l), below(th, th)) + dot(h, tl)

    def six(self, name, h, m, l):
        first = dot(self(name), below(h, m, l, h))
        return first + dot(self(name, part=1), below(m, h))


def above_below(first, second):
    row = lax.axis_index("row")
    odd = lax.rem(row, 2) == 1
    above = jnp.where(row == 0, 0.0, jnp.where(odd, first, second))
    last = row == lax.axis_size("row") - 1
    return above, jnp.where(last, 0.0, jnp.where(odd, second, first))


def spectrum_of(mask, cols, rows):
    grid = 2 * BAND
    low = lax.broadcasted_iota(jnp.int32, (1, LANES), 1) < LANES // 2
    h, l = split(mask, 2)
    both = dot(h, cols)
    half = both[:, :LANES] + both[:, LANES:] + dot(l, cols[:, :LANES])
    h, m, l = split(half, 3)
    both = dot(rows[: 2 * grid], beside(h, m))
    rest = dot(rows[2 * grid :], h) + dot(rows[:grid], l)
    middle = both[:grid, LANES:] + both[grid:, :LANES]
    both = both[:grid, :LANES] + middle + (both[grid:, LANES:] + rest)
    turned = pltpu.roll(both[BAND:], LANES // 2, 1)
    return both[:BAND] + jnp.where(low, turned, -turned)


def mask_of(logits, weight):
    return jnp.where(weight > 0.0, jax.nn.sigmoid(logits), 0.0)


def before_margins(
    place, centre_ref, up_ref, down_ref, table_ref, spectrum_ref, cells_ref, factor_ref
):
    table = Tables(table_ref, place)
    low = lax.broadcasted_iota(jnp.int32, (1, LANES), 1) < LANES // 2

    def padded(index):
        ends = []
        for own in above_below(up_ref[index], down_ref[index]):
            turned = pltpu.roll(own, HALO, 1)
            ends.append(beside(jnp.where(low, 0.0, turned), jnp.where(low, turned, 0.0)))
        return below(ends[0], centre_ref[index], ends[1])

    weight = padded(2)
    mask = mask_of(padded(0), weight)
    cells_ref[0] = padded(1)
    cells_ref[1] = weight
    core = slice(HALO, mask.shape[0] - HALO)
    own = mask[core, core]
    factor_ref[...] = own * (1.0 - own)
    spectrum_ref[...] = spectrum_of(mask, table("analyse_cols"), table("analyse_rows"))


def forward_kernel(
    order,
    place,
    bank_ref,
    spectrum_ref,
    up_margin_ref,
    first_ref,
    table_ref,
    spectra_ref,
    fields_ref,
    tall_ref,
    flat_ref,
):
    grid = 2 * BAND
    fold = LANES // BAND
    per = BAND // fold
    table = Tables(table_ref, place)
    low = lax.broadcasted_iota(jnp.int32, (1, LANES), 1) < LANES // 2
    corner_mask = below(*above_below(up_margin_ref[0], first_ref[:HALO]))

    for row, (device, piece) in enumerate(order):
        both = bank_ref[device, :, piece * LANES : (piece + 1) * LANES]
        for condition in range(CONDITIONS):
            flat_ref[condition, row : row + 1, :] = both[condition : condition + 1]

    lane = lax.broadcasted_iota(jnp.int32, (per, LANES), 1)

    def spread(condition, kernel):
        real = flat_ref[condition, pl.ds(kernel * per, per), :]
        imag = flat_ref[condition, pl.ds((KERNELS + kernel) * per, per), :]
        reals = [real] + [pltpu.roll(real, BAND * s, 1) for s in range(1, fold)]
        imags = [imag] + [pltpu.roll(imag, BAND * s, 1) for s in range(1, fold)]
        rows = []
        for j in range(fold):
            first, second = reals[-j % fold], reals[(1 - j) % fold]
            third, fourth = imags[(2 - j) % fold], imags[(3 - j) % fold]
            rows.append(
                jnp.where(
                    lane < 2 * BAND,
                    jnp.where(lane < BAND, first, second),
                    jnp.where(lane < 3 * BAND, third, fourth),
                )
            )
        return jnp.concatenate(rows, axis=0)

    pairs = [(c, k) for c in range(CONDITIONS) for k in range(KERNELS)]
    spectra = [spread(c, k) for c, k in pairs]

    cols = table("analyse_cols")
    cols = below(cols[:HALO], cols[-HALO:])
    rows = table("analyse_rows").astype(jnp.float32)
    rows = jnp.where(low, rows[:, :LANES], rows[:, LANES:]).astype(jnp.bfloat16)
    spectrum = spectrum_ref[...] + spectrum_of(corner_mask, cols, rows)

    products = below(*[s * spectrum for s in spectra])
    h, m, l = split(products, 3)
    th, tm, tl = [table("field_cols", LANES * index, LANES) for index in range(3)]
    halves = (
        dot(beside(h, m), below(th, th))
        + dot(beside(h, m), below(tm, tm))
        + dot(beside(l, h), below(th, tl))
    )
    halves = split(halves, 3)
    fields = []
    square = 0.0
    for kernel in range(KERNELS):
        parts = []
        for part in halves:
            stacked = []
            for condition in range(CONDITIONS):
                first = (condition * KERNELS + kernel) * BAND
                rows = part[first : first + BAND]
                stacked.append(below(rows[:, :LANES], rows[:, LANES:]))
            parts.append(beside(*stacked))
        field = table.six("field_rows", *parts)
        fields.append(field)
        square = square + field * field

    square = below(*[square[:, c * LANES : (c + 1) * LANES] for c in range(CONDITIONS)])
    square = square + pltpu.roll(square, LANES // 2, 1)
    h, m, l = [part.astype(jnp.float32) for part in split(square, 3)]
    mixed = [jnp.where(low, h, m), jnp.where(low, l, h), jnp.where(low, m, h)]
    th, tm, tl = [table("up_cols", grid * index, grid) for index in range(3)]
    mixed = beside(*[part.astype(jnp.bfloat16) for part in mixed])
    tall = dot(mixed, below(th, th, th, tm, tm, tl))
    tall_ref[...] = tall
    for index, value in enumerate(spectra):
        spectra_ref[index] = value
    for index, value in enumerate(fields):
        fields_ref[index] = value


def backward_kernel(
    place,
    spectra_ref,
    fields_ref,
    tall_ref,
    cells_ref,
    factor_ref,
    up_margin_ref,
    first_ref,
    second_ref,
    table_ref,
    grad_ref,
    sums_ref,
):
    grid = 2 * BAND
    table = Tables(table_ref, place)
    low = lax.broadcasted_iota(jnp.int32, (1, LANES), 1) < LANES // 2
    pad_width = cells_ref.shape[1]
    core = slice(HALO, pad_width - HALO)

    def filled(index):
        cells = cells_ref[index]
        other = (below(first_ref[HALO:], second_ref[: HALO // 2]), second_ref[HALO // 2 :])[index]
        corners = above_below(up_margin_ref[index + 1], other)
        ends = []
        for corner, rows in zip(corners, (cells[:HALO], cells[-HALO:]), strict=True):
            left, right = rows[:, :LANES], rows[:, LANES:]
            ends.append(beside(jnp.where(low, corner, left), jnp.where(low, right, corner)))
        return below(ends[0], cells[core], ends[1])

    target, weight = filled(0), filled(1)
    spectra = [spectra_ref[index] for index in range(CONDITIONS * KERNELS)]
    fields = [fields_ref[index] for index in range(KERNELS)]
    tall = split(tall_ref[...], 3)
    slopes = []
    loss = 0.0
    for condition, dose in enumerate(DOSES):
        parts = [part[condition * grid : (condition + 1) * grid] for part in tall]
        intensity = table.six("up_rows", *parts)
        resist = jax.nn.sigmoid(SHARPNESS * (dose * intensity - THRESHOLD))
        error = resist - target
        scaled = weight * error
        loss = loss + (scaled * error)[core, core]
        slopes.append((2.0 * SHARPNESS * dose) * scaled * (resist * (1.0 - resist)))
    h, l = split(below(*slopes), 2)
    both = dot(h, table("down_cols"))
    narrow = both[:, :LANES] + (both[:, LANES:] + dot(l, table("down_cols")[:, :LANES]))
    narrow = beside(*[narrow[c * pad_width : (c + 1) * pad_width] for c in range(CONDITIONS)])
    h, l = split(narrow, 2)
    both = dot(table("down_rows"), h)
    coarse = both[:grid] + (both[grid:] + dot(table("down_rows", 0, grid), l))

    backs = [[], []]
    for field in fields:
        h, l = split(field * coarse, 2)
        back = dot(table("back_rows"), below(h, l, h))
        for condition in range(CONDITIONS):
            block = back[:, condition * LANES : (condition + 1) * LANES]
            turned = pltpu.roll(block[BAND:], LANES // 2, 1)
            backs[condition].append(block[:BAND] + jnp.where(low, -turned, turned))
    h, l = split(below(*backs[0], *backs[1]), 2)
    backs = table.three("back_cols", h, l)
    total = 0.0
    for index, spectrum in enumerate(spectra):
        total = total + spectrum * backs[index * BAND : (index + 1) * BAND]

    h, l = split(total, 2)
    across = table.three("core_cols", h, l)
    core_width = across.shape[1] // 2
    h, l = split(below(across[:, :core_width], across[:, core_width:]), 2)
    gradient = dot(table("core_rows"), below(h, l, h))
    cells = gradient * factor_ref[...]
    grad_ref[...] = cells
    square = jnp.sum(jnp.sum(cells * cells, axis=0, keepdims=True), axis=1, keepdims=True)
    loss = jnp.sum(jnp.sum(loss, axis=0, keepdims=True), axis=1, keepdims=True)
    sums = jnp.concatenate([square, loss], axis=0)
    sums_ref[...] = jnp.broadcast_to(sums[None], sums_ref.shape)


def small(megabytes):
    return pltpu.CompilerParams(vmem_limit_bytes=megabytes * 1024 * 1024)


def to_all(value):
    return lax.all_to_all(value, ("row", "col"), 0, 0)


def pair_swap(value, axis, first):
    sizes = lax.axis_size("row"), lax.axis_size("col")
    along = ("row", "col").index(axis)
    pairs = []
    for place in np.ndindex(*sizes):
        other = list(place)
        step = 1 if (place[along] - first) % 2 == 0 else -1
        if 0 <= place[along] + step < sizes[along]:
            other[along] += step
        elif 0 <= place[1 - along] ^ 1 < sizes[1 - along]:
            other[1 - along] ^= 1
        else:
            continue
        pairs.append(tuple(int(r) * sizes[1] + int(c) for r, c in (place, other)))
    return lax.ppermute(value, ("row", "col"), pairs)


def finish(cell_count, own_ref, cells_ref, sums_ref, logits_ref, loss_ref):
    total = jnp.sum(sums_ref[...], axis=0) / cell_count
    scale = STEP / jnp.sqrt(total[0:1] + EPSILON)
    logits_ref[...] = own_ref[0] - cells_ref[...] * scale
    loss_ref[...] = total[1:2, 0:1]


def shards(mask_logits, target, weight, kernels):
    core_width = mask_logits.shape[0]
    pad_width = core_width + 2 * HALO
    rows, cols = lax.axis_size("row"), lax.axis_size("col")
    f32 = jnp.float32

    def struct(*shape):
        return jax.ShapeDtypeStruct(shape, f32)

    packed = struct(core_width * 3 // 2, core_width)
    slab = struct(3, HALO, core_width)
    cells = jnp.concatenate([mask_logits, target, weight], axis=1)
    shard = jnp.pad(kernels, ((0, 0), (0, cells.shape[1] - kernels.shape[1])))
    own, slab_a, slab_b, up, down, bank = pl.pallas_call(
        pack,
        out_shape=(struct(3, core_width, core_width), packed, packed, slab, slab)
        + (struct(rows * cols, *kernels.shape),),
        in_specs=[VMEM],
        out_specs=(VMEM,) * 6,
        compiler_params=small(4),
    )(jnp.concatenate([cells, shard], axis=0))
    got_a, got_b = pair_swap(slab_a, "col", 0), pair_swap(slab_b, "col", 1)
    up, down = pair_swap(up, "row", 0), pair_swap(down, "row", 1)
    margin = struct(HALO * 3 // 2, core_width)
    centre, up_margin, first_margin, second_margin = pl.pallas_call(
        widen,
        out_shape=(struct(3, core_width, pad_width), slab, margin, margin),
        in_specs=[VMEM] * 3 + [pl.BlockSpec(memory_space=pl.ANY)],
        out_specs=(VMEM,) * 4,
        compiler_params=small(8),
    )(own, got_a, got_b, down)
    up_margin = pair_swap(up_margin, "row", 0)
    first_margin = pair_swap(first_margin, "row", 1)
    second_margin = pair_swap(second_margin, "row", 1)
    consts, place = tables(pad_width, HALO)
    spectrum, cells, factor = pl.pallas_call(
        functools.partial(before_margins, place),
        out_shape=(
            struct(BAND, LANES),
            struct(2, pad_width, pad_width),
            struct(core_width, core_width),
        ),
        in_specs=[VMEM] * 4,
        out_specs=(VMEM,) * 3,
        compiler_params=small(16),
    )(centre, up, down, consts)
    bank = to_all(bank)
    pieces = kernels.shape[1] // LANES
    if kernels.shape[1] % LANES:
        bank = jnp.swapaxes(bank, 0, 1).reshape(1, CONDITIONS, -1)
        pieces = bank.shape[2] // LANES
    order = [(device, piece) for device in range(bank.shape[0]) for piece in range(pieces)]

    spectra, fields, tall = pl.pallas_call(
        functools.partial(forward_kernel, order, place),
        out_shape=(
            struct(CONDITIONS * KERNELS, BAND, LANES),
            struct(KERNELS, 2 * BAND, 2 * LANES),
            struct(CONDITIONS * 2 * BAND, pad_width),
        ),
        in_specs=[VMEM] * 5,
        out_specs=(VMEM,) * 3,
        scratch_shapes=[pltpu.VMEM((CONDITIONS, len(order), LANES), f32)],
        compiler_params=small(16),
    )(bank, spectrum, up_margin, first_margin, consts)
    grad_cells, sums = pl.pallas_call(
        functools.partial(backward_kernel, place),
        out_shape=(struct(core_width, core_width), struct(rows * cols, 2, LANES)),
        in_specs=[VMEM] * 9,
        out_specs=(VMEM,) * 2,
        compiler_params=small(16),
    )(spectra, fields, tall, cells, factor, up_margin, first_margin, second_margin, consts)

    sums = to_all(sums)
    cell_count = rows * cols * core_width * core_width
    new_logits, loss = pl.pallas_call(
        functools.partial(finish, cell_count),
        out_shape=(struct(core_width, core_width), struct(1, 1)),
        in_specs=[VMEM] * 3,
        out_specs=(VMEM,) * 2,
        compiler_params=small(4),
    )(own, grad_cells, sums)
    return (new_logits, loss[0, 0])


def solution(mesh):
    placed = (P("row", "col"), P("row", "col"), P("row", "col"), P(None, ("row", "col")))
    return jax.shard_map(
        shards, mesh=mesh, in_specs=placed, out_specs=(P("row", "col"), P()), check_vma=False
    )
```

```python
import functools
import math

import jax
import jax.numpy as jnp
import numpy as np
from jax import lax
from jax.experimental import pallas as pl
from jax.experimental.pallas import tpu as pltpu
from jax.sharding import PartitionSpec as P

HALO = 64
KERNELS = 6
BAND = 32
CONDITIONS = 2

SHARPNESS = 6.0
THRESHOLD = 0.75
STEP = 0.5
EPSILON = 1e-06
DOSES = (1.0, 1.15)

LANES = 128
VMEM = pl.BlockSpec(memory_space=pltpu.VMEM)


def dot(first, second):
    return lax.dot_general(
        first, second, (((1,), (0,)), ((), ())), preferred_element_type=jnp.float32
    )


def split(value, count):
    parts = []
    for index in range(count):
        part = value.astype(jnp.bfloat16)
        parts.append(part)
        if index + 1 < count:
            value = value - part.astype(jnp.float32)
    return parts


def split_table(table, count):
    parts = []
    for _ in range(count):
        part = table.astype(np.float32).astype(jnp.bfloat16)
        parts.append(part)
        table = table - part.astype(np.float64)
    return parts


def tables(pad_width, margin):
    freq = np.arange(BAND) - BAND // 2
    place = np.arange(pad_width)
    turns = (freq[:, None] * place[None, :] % pad_width) * (2.0 * math.pi / pad_width)
    wave_re = np.cos(turns) / math.sqrt(pad_width)
    wave_im = -np.sin(turns) / math.sqrt(pad_width)
    grid = 2 * BAND
    stride = pad_width // grid
    fold = LANES // BAND
    rows = np.arange(BAND).reshape(BAND // fold, fold).T.reshape(-1)
    row_re, row_im = wave_re[rows], wave_im[rows]
    coarse_re, coarse_im = wave_re[:, ::stride], wave_im[:, ::stride]
    crow_re, crow_im = row_re[:, ::stride], row_im[:, ::stride]
    core = slice(margin, pad_width - margin)
    core_re, core_im = wave_re[:, core], wave_im[:, core]
    steps = (place[:, None] - stride * np.arange(grid)[None, :]) % pad_width
    diffs = np.arange(1, BAND)
    phases = (steps[..., None] * diffs % pad_width) * (2.0 * math.pi / pad_width)
    between = (1.0 + 2.0 * np.cos(phases).sum(-1)) / grid

    def beside(*blocks):
        return np.concatenate(blocks, axis=1)

    def below(*blocks):
        return np.concatenate(blocks, axis=0)

    found = {}
    h, l = split_table(beside(wave_re.T, wave_im.T, -wave_im.T, wave_re.T), 2)
    found["analyse_cols"] = beside(h, l)
    found["analyse_rows"] = below(*split_table(below(row_re, row_im), 3))
    from_re = beside(coarse_re, -coarse_im, -coarse_im, -coarse_re)
    from_im = beside(coarse_im, coarse_re, coarse_re, -coarse_im)
    h, m, l = split_table(below(from_re, from_im, from_re, from_im), 3)
    found["field_cols"] = below(h, m, l)
    h, m, l = split_table(beside(crow_re.T, crow_im.T), 3)
    found["field_rows"] = beside(h, h, h, m, m, l)
    h, m, l = split_table(between, 3)
    found["up_rows"] = beside(h, h, h, m, m, l)
    found["up_cols"] = below(h.T, m.T, l.T)
    found["down_cols"] = beside(h, h, m, m)
    found["down_rows"] = below(h.T, m.T)
    h, l = split_table(below(crow_re, crow_im), 2)
    found["back_rows"] = beside(h, h, l)
    c_re, c_im = coarse_re.T, coarse_im.T
    h, l = split_table(
        below(beside(c_re, c_im, c_im, -c_re), beside(-c_im, c_re, c_re, c_im)), 2
    )
    found["back_cols"] = below(h, l)
    from_re, from_im = beside(core_re, -core_im), beside(core_im, core_re)
    h, l = split_table(below(from_re, from_im, from_re, from_im), 2)
    found["core_cols"] = below(h, l)
    h, l = split_table(2.0 * beside(row_re[:, core].T, row_im[:, core].T), 2)
    found["core_rows"] = beside(h, h, l)

    pieces = []
    for name, table in found.items():
        for first in range(0, table.shape[1], 2 * LANES):
            pieces.append(((name, first // (2 * LANES)), table[:, first : first + 2 * LANES]))
    where, tops, blocks = {}, [0, 0], []
    for key, piece in sorted(pieces, key=lambda p: (p[1].shape[1] <= LANES, -p[1].shape[0])):
        thin = piece.shape[1] <= LANES
        side = int(thin and tops[1] < tops[0])
        where[key] = (tops[side], side * LANES, piece.shape)
        blocks.append((where[key], piece))
        tops[side] += piece.shape[0]
        if not thin:
            tops[1] = tops[0]
    whole = np.zeros((max(tops), 2 * LANES), jnp.bfloat16)
    for (top, left, shape), piece in blocks:
        whole[top : top + shape[0], left : left + shape[1]] = piece
    return jnp.asarray(whole), where


def pack(held_ref, own_ref, a_ref, b_ref, up_ref, down_ref, bank_ref):
    cells, width = own_ref.shape[1:]
    for index in range(3):
        own_ref[index] = held_ref[:cells, index * width : (index + 1) * width]
    shard = held_ref[cells : cells + CONDITIONS, : bank_ref.shape[2]]
    bank_ref[...] = jnp.broadcast_to(shard[None], bank_ref.shape)
    odd_row = lax.rem(lax.axis_index("row"), 2) == 1
    for index in range(3):
        first, second = own_ref[index, :HALO], own_ref[index, HALO:]
        up_ref[index] = jnp.where(odd_row, first, second)
        down_ref[index] = jnp.where(odd_row, second, first)
    half = HALO
    odd = lax.rem(lax.axis_index("col"), 2) == 1
    values = [own_ref[index] for index in range(3)]
    turned = [pltpu.roll(value, half, 1) for value in values]
    low = lax.broadcasted_iota(jnp.int32, values[0].shape, 1) < half
    rows = values[0].shape[0]
    to_right = [
        jnp.where(low, turned[0], values[1]),
        jnp.where(low[: rows // 2], turned[2][: rows // 2], values[2][rows // 2 :]),
    ]
    to_left = [
        jnp.where(low, values[0], turned[1]),
        jnp.where(low[: rows // 2], values[2][: rows // 2], turned[2][rows // 2 :]),
    ]
    a_ref[:rows] = jnp.where(odd, to_left[0], to_right[0])
    a_ref[rows:] = jnp.where(odd, to_left[1], to_right[1])
    b_ref[:rows] = jnp.where(odd, to_right[0], to_left[0])
    b_ref[rows:] = jnp.where(odd, to_right[1], to_left[1])


def widen(own_ref, a_ref, b_ref, _, centre_ref, up_ref, first_ref, second_ref):
    half = HALO
    odd = lax.rem(lax.axis_index("col"), 2) == 1
    odd_row = lax.rem(lax.axis_index("row"), 2) == 1
    values = [own_ref[index] for index in range(3)]
    rows = values[0].shape[0]
    low = lax.broadcasted_iota(jnp.int32, values[0].shape, 1) < half
    got_a, got_b = a_ref[...], b_ref[...]
    col, cols = lax.axis_index("col"), lax.axis_size("col")
    left = jnp.where(col == 0, 0.0, jnp.where(odd, got_a, got_b))
    right = jnp.where(col == cols - 1, 0.0, jnp.where(odd, got_b, got_a))
    left_turned, right_turned = pltpu.roll(left, half, 1), pltpu.roll(right, half, 1)

    def two(first, second):
        return jnp.concatenate([first, second], axis=0)

    lefts = [left[:rows], left_turned[:rows], two(left[rows:], left_turned[rows:])]
    rights = [right_turned[:rows], right[:rows], two(right_turned[rows:], right[rows:])]
    margins = []
    for index, value in enumerate(values):
        turned = pltpu.roll(value, half, 1)
        wide = jnp.concatenate(
            [jnp.where(low, lefts[index], turned), jnp.where(low, turned, rights[index])], axis=1
        )
        centre_ref[index] = wide
        margins.append(jnp.where(low, wide[:, :LANES], wide[:, LANES:]))
    margins[0] = mask_of(margins[0], margins[2])
    ups, downs = [], []
    for margin in margins:
        ups.append(jnp.where(odd_row, margin[:half], margin[half:]))
        downs.append(jnp.where(odd_row, margin[half:], margin[:half]))
    for index, value in enumerate(ups):
        up_ref[index] = value
    middle = half // 2
    first_ref[:half] = downs[0]
    first_ref[half:] = downs[1][:middle]
    second_ref[:middle] = downs[1][middle:]
    second_ref[middle:] = downs[2]


def beside(*blocks):
    return jnp.concatenate(blocks, axis=1)


def below(*blocks):
    return jnp.concatenate(blocks, axis=0)


class Tables:
    def __init__(self, ref, place):
        self.ref, self.place = ref, place

    def __call__(self, name, first=0, count=None, part=0):
        top, left, shape = self.place[name, part]
        top, count = top + first, shape[0] - first if count is None else count
        return self.ref[top : top + count, left : left + shape[1]]

    def three(self, name, h, l):
        th, tl = self(name, 0, LANES), self(name, LANES)
        return dot(beside(h, l), below(th, th)) + dot(h, tl)

    def six(self, name, h, m, l):
        first = dot(self(name), below(h, m, l, h))
        return first + dot(self(name, part=1), below(m, h))


def above_below(first, second):
    row = lax.axis_index("row")
    odd = lax.rem(row, 2) == 1
    above = jnp.where(row == 0, 0.0, jnp.where(odd, first, second))
    last = row == lax.axis_size("row") - 1
    return above, jnp.where(last, 0.0, jnp.where(odd, second, first))


def spectrum_of(mask, cols, rows):
    grid = 2 * BAND
    low = lax.broadcasted_iota(jnp.int32, (1, LANES), 1) < LANES // 2
    h, l = split(mask, 2)
    both = dot(h, cols)
    half = both[:, :LANES] + both[:, LANES:] + dot(l, cols[:, :LANES])
    h, m, l = split(half, 3)
    both = dot(rows[: 2 * grid], beside(h, m))
    rest = dot(rows[2 * grid :], h) + dot(rows[:grid], l)
    middle = both[:grid, LANES:] + both[grid:, :LANES]
    both = both[:grid, :LANES] + middle + (both[grid:, LANES:] + rest)
    turned = pltpu.roll(both[BAND:], LANES // 2, 1)
    return both[:BAND] + jnp.where(low, turned, -turned)


def mask_of(logits, weight):
    return jnp.where(weight > 0.0, jax.nn.sigmoid(logits), 0.0)


def before_margins(
    place, centre_ref, up_ref, down_ref, table_ref, spectrum_ref, cells_ref, factor_ref
):
    table = Tables(table_ref, place)
    low = lax.broadcasted_iota(jnp.int32, (1, LANES), 1) < LANES // 2

    def padded(index):
        ends = []
        for own in above_below(up_ref[index], down_ref[index]):
            turned = pltpu.roll(own, HALO, 1)
            ends.append(beside(jnp.where(low, 0.0, turned), jnp.where(low, turned, 0.0)))
        return below(ends[0], centre_ref[index], ends[1])

    weight = padded(2)
    mask = mask_of(padded(0), weight)
    cells_ref[0] = padded(1)
    cells_ref[1] = weight
    core = slice(HALO, mask.shape[0] - HALO)
    own = mask[core, core]
    factor_ref[...] = own * (1.0 - own)
    spectrum_ref[...] = spectrum_of(mask, table("analyse_cols"), table("analyse_rows"))


def forward_kernel(
    order,
    place,
    bank_ref,
    spectrum_ref,
    up_margin_ref,
    first_ref,
    table_ref,
    spectra_ref,
    fields_ref,
    tall_ref,
    flat_ref,
):
    grid = 2 * BAND
    fold = LANES // BAND
    per = BAND // fold
    table = Tables(table_ref, place)
    low = lax.broadcasted_iota(jnp.int32, (1, LANES), 1) < LANES // 2
    corner_mask = below(*above_below(up_margin_ref[0], first_ref[:HALO]))

    for row, (device, piece) in enumerate(order):
        both = bank_ref[device, :, piece * LANES : (piece + 1) * LANES]
        for condition in range(CONDITIONS):
            flat_ref[condition, row : row + 1, :] = both[condition : condition + 1]

    lane = lax.broadcasted_iota(jnp.int32, (per, LANES), 1)

    def spread(condition, kernel):
        real = flat_ref[condition, pl.ds(kernel * per, per), :]
        imag = flat_ref[condition, pl.ds((KERNELS + kernel) * per, per), :]
        reals = [real] + [pltpu.roll(real, BAND * s, 1) for s in range(1, fold)]
        imags = [imag] + [pltpu.roll(imag, BAND * s, 1) for s in range(1, fold)]
        rows = []
        for j in range(fold):
            first, second = reals[-j % fold], reals[(1 - j) % fold]
            third, fourth = imags[(2 - j) % fold], imags[(3 - j) % fold]
            rows.append(
                jnp.where(
                    lane < 2 * BAND,
                    jnp.where(lane < BAND, first, second),
                    jnp.where(lane < 3 * BAND, third, fourth),
                )
            )
        return jnp.concatenate(rows, axis=0)

    pairs = [(c, k) for c in range(CONDITIONS) for k in range(KERNELS)]
    spectra = [spread(c, k) for c, k in pairs]

    cols = table("analyse_cols")
    cols = below(cols[:HALO], cols[-HALO:])
    rows = table("analyse_rows").astype(jnp.float32)
    rows = jnp.where(low, rows[:, :LANES], rows[:, LANES:]).astype(jnp.bfloat16)
    spectrum = spectrum_ref[...] + spectrum_of(corner_mask, cols, rows)

    products = below(*[s * spectrum for s in spectra])
    h, m, l = split(products, 3)
    th, tm, tl = [table("field_cols", LANES * index, LANES) for index in range(3)]
    halves = (
        dot(beside(h, m), below(th, th))
        + dot(beside(h, m), below(tm, tm))
        + dot(beside(l, h), below(th, tl))
    )
    halves = split(halves, 3)
    fields = []
    square = 0.0
    for kernel in range(KERNELS):
        parts = []
        for part in halves:
            stacked = []
            for condition in range(CONDITIONS):
                first = (condition * KERNELS + kernel) * BAND
                rows = part[first : first + BAND]
                stacked.append(below(rows[:, :LANES], rows[:, LANES:]))
            parts.append(beside(*stacked))
        field = table.six("field_rows", *parts)
        fields.append(field)
        square = square + field * field

    square = below(*[square[:, c * LANES : (c + 1) * LANES] for c in range(CONDITIONS)])
    square = square + pltpu.roll(square, LANES // 2, 1)
    h, m, l = [part.astype(jnp.float32) for part in split(square, 3)]
    mixed = [jnp.where(low, h, m), jnp.where(low, l, h), jnp.where(low, m, h)]
    th, tm, tl = [table("up_cols", grid * index, grid) for index in range(3)]
    mixed = beside(*[part.astype(jnp.bfloat16) for part in mixed])
    tall = dot(mixed, below(th, th, th, tm, tm, tl))
    tall_ref[...] = tall
    for index, value in enumerate(spectra):
        spectra_ref[index] = value
    for index, value in enumerate(fields):
        fields_ref[index] = value


def backward_kernel(
    place,
    spectra_ref,
    fields_ref,
    tall_ref,
    cells_ref,
    factor_ref,
    up_margin_ref,
    first_ref,
    second_ref,
    table_ref,
    grad_ref,
    sums_ref,
):
    grid = 2 * BAND
    table = Tables(table_ref, place)
    low = lax.broadcasted_iota(jnp.int32, (1, LANES), 1) < LANES // 2
    pad_width = cells_ref.shape[1]
    core = slice(HALO, pad_width - HALO)

    def filled(index):
        cells = cells_ref[index]
        other = (below(first_ref[HALO:], second_ref[: HALO // 2]), second_ref[HALO // 2 :])[index]
        corners = above_below(up_margin_ref[index + 1], other)
        ends = []
        for corner, rows in zip(corners, (cells[:HALO], cells[-HALO:]), strict=True):
            left, right = rows[:, :LANES], rows[:, LANES:]
            ends.append(beside(jnp.where(low, corner, left), jnp.where(low, right, corner)))
        return below(ends[0], cells[core], ends[1])

    target, weight = filled(0), filled(1)
    spectra = [spectra_ref[index] for index in range(CONDITIONS * KERNELS)]
    fields = [fields_ref[index] for index in range(KERNELS)]
    tall = split(tall_ref[...], 3)
    slopes = []
    loss = 0.0
    for condition, dose in enumerate(DOSES):
        parts = [part[condition * grid : (condition + 1) * grid] for part in tall]
        intensity = table.six("up_rows", *parts)
        resist = jax.nn.sigmoid(SHARPNESS * (dose * intensity - THRESHOLD))
        error = resist - target
        scaled = weight * error
        loss = loss + (scaled * error)[core, core]
        slopes.append((2.0 * SHARPNESS * dose) * scaled * (resist * (1.0 - resist)))
    h, l = split(below(*slopes), 2)
    both = dot(h, table("down_cols"))
    narrow = both[:, :LANES] + (both[:, LANES:] + dot(l, table("down_cols")[:, :LANES]))
    narrow = beside(*[narrow[c * pad_width : (c + 1) * pad_width] for c in range(CONDITIONS)])
    h, l = split(narrow, 2)
    both = dot(table("down_rows"), h)
    coarse = both[:grid] + (both[grid:] + dot(table("down_rows", 0, grid), l))

    backs = [[], []]
    for field in fields:
        h, l = split(field * coarse, 2)
        back = dot(table("back_rows"), below(h, l, h))
        for condition in range(CONDITIONS):
            block = back[:, condition * LANES : (condition + 1) * LANES]
            turned = pltpu.roll(block[BAND:], LANES // 2, 1)
            backs[condition].append(block[:BAND] + jnp.where(low, -turned, turned))
    h, l = split(below(*backs[0], *backs[1]), 2)
    backs = table.three("back_cols", h, l)
    total = 0.0
    for index, spectrum in enumerate(spectra):
        total = total + spectrum * backs[index * BAND : (index + 1) * BAND]

    h, l = split(total, 2)
    across = table.three("core_cols", h, l)
    core_width = across.shape[1] // 2
    h, l = split(below(across[:, :core_width], across[:, core_width:]), 2)
    gradient = dot(table("core_rows"), below(h, l, h))
    cells = gradient * factor_ref[...]
    grad_ref[...] = cells
    square = jnp.sum(jnp.sum(cells * cells, axis=0, keepdims=True), axis=1, keepdims=True)
    loss = jnp.sum(jnp.sum(loss, axis=0, keepdims=True), axis=1, keepdims=True)
    sums = jnp.concatenate([square, loss], axis=0)
    sums_ref[...] = jnp.broadcast_to(sums[None], sums_ref.shape)


def small(megabytes):
    return pltpu.CompilerParams(vmem_limit_bytes=megabytes * 1024 * 1024)


def to_all(value):
    return lax.all_to_all(value, ("row", "col"), 0, 0)


def pair_swap(value, axis, first):
    sizes = lax.axis_size("row"), lax.axis_size("col")
    along = ("row", "col").index(axis)
    pairs = []
    for place in np.ndindex(*sizes):
        other = list(place)
        step = 1 if (place[along] - first) % 2 == 0 else -1
        if 0 <= place[along] + step < sizes[along]:
            other[along] += step
        elif 0 <= place[1 - along] ^ 1 < sizes[1 - along]:
            other[1 - along] ^= 1
        else:
            continue
        pairs.append(tuple(int(r) * sizes[1] + int(c) for r, c in (place, other)))
    return lax.ppermute(value, ("row", "col"), pairs)


def finish(cell_count, own_ref, cells_ref, sums_ref, logits_ref, loss_ref):
    total = jnp.sum(sums_ref[...], axis=0) / cell_count
    scale = STEP / jnp.sqrt(total[0:1] + EPSILON)
    logits_ref[...] = own_ref[0] - cells_ref[...] * scale
    loss_ref[...] = total[1:2, 0:1]


def shards(mask_logits, target, weight, kernels):
    core_width = mask_logits.shape[0]
    pad_width = core_width + 2 * HALO
    rows, cols = lax.axis_size("row"), lax.axis_size("col")
    f32 = jnp.float32

    def struct(*shape):
        return jax.ShapeDtypeStruct(shape, f32)

    packed = struct(core_width * 3 // 2, core_width)
    slab = struct(3, HALO, core_width)
    cells = jnp.concatenate([mask_logits, target, weight], axis=1)
    width = max(cells.shape[1], kernels.shape[1])
    cells, shard = [jnp.pad(a, ((0, 0), (0, width - a.shape[1]))) for a in (cells, kernels)]
    own, slab_a, slab_b, up, down, bank = pl.pallas_call(
        pack,
        out_shape=(struct(3, core_width, core_width), packed, packed, slab, slab)
        + (struct(rows * cols, *kernels.shape),),
        in_specs=[VMEM],
        out_specs=(VMEM,) * 6,
        compiler_params=small(4),
    )(jnp.concatenate([cells, shard], axis=0))
    got_a, got_b = pair_swap(slab_a, "col", 0), pair_swap(slab_b, "col", 1)
    up, down = pair_swap(up, "row", 0), pair_swap(down, "row", 1)
    margin = struct(HALO * 3 // 2, core_width)
    centre, up_margin, first_margin, second_margin = pl.pallas_call(
        widen,
        out_shape=(struct(3, core_width, pad_width), slab, margin, margin),
        in_specs=[VMEM] * 3 + [pl.BlockSpec(memory_space=pl.ANY)],
        out_specs=(VMEM,) * 4,
        compiler_params=small(8),
    )(own, got_a, got_b, down)
    up_margin = pair_swap(up_margin, "row", 0)
    first_margin = pair_swap(first_margin, "row", 1)
    second_margin = pair_swap(second_margin, "row", 1)
    consts, place = tables(pad_width, HALO)
    spectrum, cells, factor = pl.pallas_call(
        functools.partial(before_margins, place),
        out_shape=(
            struct(BAND, LANES),
            struct(2, pad_width, pad_width),
            struct(core_width, core_width),
        ),
        in_specs=[VMEM] * 4,
        out_specs=(VMEM,) * 3,
        compiler_params=small(16),
    )(centre, up, down, consts)
    bank = to_all(bank)
    pieces = kernels.shape[1] // LANES
    if kernels.shape[1] % LANES:
        bank = jnp.swapaxes(bank, 0, 1).reshape(1, CONDITIONS, -1)
        pieces = bank.shape[2] // LANES
    order = [(device, piece) for device in range(bank.shape[0]) for piece in range(pieces)]

    spectra, fields, tall = pl.pallas_call(
        functools.partial(forward_kernel, order, place),
        out_shape=(
            struct(CONDITIONS * KERNELS, BAND, LANES),
            struct(KERNELS, 2 * BAND, 2 * LANES),
            struct(CONDITIONS * 2 * BAND, pad_width),
        ),
        in_specs=[VMEM] * 5,
        out_specs=(VMEM,) * 3,
        scratch_shapes=[pltpu.VMEM((CONDITIONS, len(order), LANES), f32)],
        compiler_params=small(16),
    )(bank, spectrum, up_margin, first_margin, consts)
    grad_cells, sums = pl.pallas_call(
        functools.partial(backward_kernel, place),
        out_shape=(struct(core_width, core_width), struct(rows * cols, 2, LANES)),
        in_specs=[VMEM] * 9,
        out_specs=(VMEM,) * 2,
        compiler_params=small(16),
    )(spectra, fields, tall, cells, factor, up_margin, first_margin, second_margin, consts)

    sums = to_all(sums)
    cell_count = rows * cols * core_width * core_width
    new_logits, loss = pl.pallas_call(
        functools.partial(finish, cell_count),
        out_shape=(struct(core_width, core_width), struct(1, 1)),
        in_specs=[VMEM] * 3,
        out_specs=(VMEM,) * 2,
        compiler_params=small(4),
    )(own, grad_cells, sums)
    return (new_logits, loss[0, 0])


def solution(mesh):
    placed = (P("row", "col"), P("row", "col"), P("row", "col"), P(None, ("row", "col")))
    return jax.shard_map(
        shards, mesh=mesh, in_specs=placed, out_specs=(P("row", "col"), P()), check_vma=False
    )
```

```python
import functools
import math

import jax
import jax.numpy as jnp
import numpy as np
from jax import lax
from jax.experimental import pallas as pl
from jax.experimental.pallas import tpu as pltpu
from jax.sharding import PartitionSpec as P

HALO = 64
KERNELS = 6
BAND = 32
CONDITIONS = 2

SHARPNESS = 6.0
THRESHOLD = 0.75
STEP = 0.5
EPSILON = 1e-06
DOSES = (1.0, 1.15)

LANES = 128
VMEM = pl.BlockSpec(memory_space=pltpu.VMEM)


def dot(first, second):
    return lax.dot_general(
        first, second, (((1,), (0,)), ((), ())), preferred_element_type=jnp.float32
    )


def split(value, count):
    parts = []
    for index in range(count):
        part = value.astype(jnp.bfloat16)
        parts.append(part)
        if index + 1 < count:
            value = value - part.astype(jnp.float32)
    return parts


def split_table(table, count):
    parts = []
    for _ in range(count):
        part = table.astype(np.float32).astype(jnp.bfloat16)
        parts.append(part)
        table = table - part.astype(np.float64)
    return parts


def tables(pad_width, margin):
    freq = np.arange(BAND) - BAND // 2
    place = np.arange(pad_width)
    turns = (freq[:, None] * place[None, :] % pad_width) * (2.0 * math.pi / pad_width)
    wave_re = np.cos(turns) / math.sqrt(pad_width)
    wave_im = -np.sin(turns) / math.sqrt(pad_width)
    grid = 2 * BAND
    stride = pad_width // grid
    fold = LANES // BAND
    rows = np.arange(BAND).reshape(BAND // fold, fold).T.reshape(-1)
    row_re, row_im = wave_re[rows], wave_im[rows]
    coarse_re, coarse_im = wave_re[:, ::stride], wave_im[:, ::stride]
    crow_re, crow_im = row_re[:, ::stride], row_im[:, ::stride]
    core = slice(margin, pad_width - margin)
    core_re, core_im = wave_re[:, core], wave_im[:, core]
    steps = (place[:, None] - stride * np.arange(grid)[None, :]) % pad_width
    diffs = np.arange(1, BAND)
    phases = (steps[..., None] * diffs % pad_width) * (2.0 * math.pi / pad_width)
    between = (1.0 + 2.0 * np.cos(phases).sum(-1)) / grid

    def beside(*blocks):
        return np.concatenate(blocks, axis=1)

    def below(*blocks):
        return np.concatenate(blocks, axis=0)

    found = {}
    h, l = split_table(beside(wave_re.T, wave_im.T, -wave_im.T, wave_re.T), 2)
    found["analyse_cols"] = beside(h, l)
    found["analyse_rows"] = below(*split_table(below(row_re, row_im), 3))
    from_re = beside(coarse_re, -coarse_im, -coarse_im, -coarse_re)
    from_im = beside(coarse_im, coarse_re, coarse_re, -coarse_im)
    h, m, l = split_table(below(from_re, from_im, from_re, from_im), 3)
    found["field_cols"] = below(h, m, l)
    h, m, l = split_table(beside(crow_re.T, crow_im.T), 3)
    found["field_rows"] = beside(h, h, h, m, m, l)
    h, m, l = split_table(between, 3)
    found["up_rows"] = beside(h, h, h, m, m, l)
    found["up_cols"] = below(h.T, m.T, l.T)
    found["down_cols"] = beside(h, h, m, m)
    found["down_rows"] = below(h.T, m.T)
    h, l = split_table(below(crow_re, crow_im), 2)
    found["back_rows"] = beside(h, h, l)
    c_re, c_im = coarse_re.T, coarse_im.T
    h, l = split_table(
        below(beside(c_re, c_im, c_im, -c_re), beside(-c_im, c_re, c_re, c_im)), 2
    )
    found["back_cols"] = below(h, l)
    from_re, from_im = beside(core_re, -core_im), beside(core_im, core_re)
    h, l = split_table(below(from_re, from_im, from_re, from_im), 2)
    found["core_cols"] = below(h, l)
    h, l = split_table(2.0 * beside(row_re[:, core].T, row_im[:, core].T), 2)
    found["core_rows"] = beside(h, h, l)

    pieces = []
    for name, table in found.items():
        for first in range(0, table.shape[1], 2 * LANES):
            pieces.append(((name, first // (2 * LANES)), table[:, first : first + 2 * LANES]))
    where, tops, blocks = {}, [0, 0], []
    for key, piece in sorted(pieces, key=lambda p: (p[1].shape[1] <= LANES, -p[1].shape[0])):
        thin = piece.shape[1] <= LANES
        side = int(thin and tops[1] < tops[0])
        where[key] = (tops[side], side * LANES, piece.shape)
        blocks.append((where[key], piece))
        tops[side] += piece.shape[0]
        if not thin:
            tops[1] = tops[0]
    whole = np.zeros((max(tops), 2 * LANES), jnp.bfloat16)
    for (top, left, shape), piece in blocks:
        whole[top : top + shape[0], left : left + shape[1]] = piece
    return jnp.asarray(whole), where


def pack(held_ref, own_ref, a_ref, b_ref, up_ref, down_ref, bank_ref):
    cells, width = own_ref.shape[1:]
    for index in range(3):
        own_ref[index] = held_ref[:cells, index * width : (index + 1) * width]
    shard = held_ref[cells : cells + CONDITIONS, : bank_ref.shape[2]]
    bank_ref[...] = jnp.broadcast_to(shard[None], bank_ref.shape)
    odd_row = lax.rem(lax.axis_index("row"), 2) == 1
    for index in range(3):
        first, second = own_ref[index, :HALO], own_ref[index, HALO:]
        up_ref[index] = jnp.where(odd_row, first, second)
        down_ref[index] = jnp.where(odd_row, second, first)
    half = HALO
    odd = lax.rem(lax.axis_index("col"), 2) == 1
    values = [own_ref[index] for index in range(3)]
    turned = [pltpu.roll(value, half, 1) for value in values]
    low = lax.broadcasted_iota(jnp.int32, values[0].shape, 1) < half
    rows = values[0].shape[0]
    to_right = [
        jnp.where(low, turned[0], values[1]),
        jnp.where(low[: rows // 2], turned[2][: rows // 2], values[2][rows // 2 :]),
    ]
    to_left = [
        jnp.where(low, values[0], turned[1]),
        jnp.where(low[: rows // 2], values[2][: rows // 2], turned[2][rows // 2 :]),
    ]
    a_ref[:rows] = jnp.where(odd, to_left[0], to_right[0])
    a_ref[rows:] = jnp.where(odd, to_left[1], to_right[1])
    b_ref[:rows] = jnp.where(odd, to_right[0], to_left[0])
    b_ref[rows:] = jnp.where(odd, to_right[1], to_left[1])


def widen(own_ref, a_ref, b_ref, _, centre_ref, up_ref, first_ref, second_ref):
    half = HALO
    odd = lax.rem(lax.axis_index("col"), 2) == 1
    odd_row = lax.rem(lax.axis_index("row"), 2) == 1
    values = [own_ref[index] for index in range(3)]
    rows = values[0].shape[0]
    low = lax.broadcasted_iota(jnp.int32, values[0].shape, 1) < half
    got_a, got_b = a_ref[...], b_ref[...]
    col, cols = lax.axis_index("col"), lax.axis_size("col")
    left = jnp.where(col == 0, 0.0, jnp.where(odd, got_a, got_b))
    right = jnp.where(col == cols - 1, 0.0, jnp.where(odd, got_b, got_a))
    left_turned, right_turned = pltpu.roll(left, half, 1), pltpu.roll(right, half, 1)

    def two(first, second):
        return jnp.concatenate([first, second], axis=0)

    lefts = [left[:rows], left_turned[:rows], two(left[rows:], left_turned[rows:])]
    rights = [right_turned[:rows], right[:rows], two(right_turned[rows:], right[rows:])]
    margins = []
    for index, value in enumerate(values):
        turned = pltpu.roll(value, half, 1)
        wide = jnp.concatenate(
            [jnp.where(low, lefts[index], turned), jnp.where(low, turned, rights[index])], axis=1
        )
        centre_ref[index] = wide
        margins.append(jnp.where(low, wide[:, :LANES], wide[:, LANES:]))
    margins[0] = mask_of(margins[0], margins[2])
    ups, downs = [], []
    for margin in margins:
        ups.append(jnp.where(odd_row, margin[:half], margin[half:]))
        downs.append(jnp.where(odd_row, margin[half:], margin[:half]))
    for index, value in enumerate(ups):
        up_ref[index] = value
    middle = half // 2
    first_ref[:half] = downs[0]
    first_ref[half:] = downs[1][:middle]
    second_ref[:middle] = downs[1][middle:]
    second_ref[middle:] = downs[2]


def beside(*blocks):
    return jnp.concatenate(blocks, axis=1)


def below(*blocks):
    return jnp.concatenate(blocks, axis=0)


class Tables:
    def __init__(self, ref, place):
        self.ref, self.place = ref, place

    def __call__(self, name, first=0, count=None, part=0):
        top, left, shape = self.place[name, part]
        top, count = top + first, shape[0] - first if count is None else count
        return self.ref[top : top + count, left : left + shape[1]]

    def three(self, name, h, l):
        th, tl = self(name, 0, LANES), self(name, LANES)
        return dot(beside(h, l), below(th, th)) + dot(h, tl)

    def six(self, name, h, m, l):
        first = dot(self(name), below(h, m, l, h))
        return first + dot(self(name, part=1), below(m, h))


def above_below(first, second):
    row = lax.axis_index("row")
    odd = lax.rem(row, 2) == 1
    above = jnp.where(row == 0, 0.0, jnp.where(odd, first, second))
    last = row == lax.axis_size("row") - 1
    return above, jnp.where(last, 0.0, jnp.where(odd, second, first))


def spectrum_of(mask, cols, rows):
    grid = 2 * BAND
    low = lax.broadcasted_iota(jnp.int32, (1, LANES), 1) < LANES // 2
    h, l = split(mask, 2)
    both = dot(h, cols)
    half = both[:, :LANES] + both[:, LANES:] + dot(l, cols[:, :LANES])
    h, m, l = split(half, 3)
    both = dot(rows[: 2 * grid], beside(h, m))
    rest = dot(rows[2 * grid :], h) + dot(rows[:grid], l)
    middle = both[:grid, LANES:] + both[grid:, :LANES]
    both = both[:grid, :LANES] + middle + (both[grid:, LANES:] + rest)
    turned = pltpu.roll(both[BAND:], LANES // 2, 1)
    return both[:BAND] + jnp.where(low, turned, -turned)


def mask_of(logits, weight):
    return jnp.where(weight > 0.0, jax.nn.sigmoid(logits), 0.0)


def before_margins(
    place, centre_ref, up_ref, down_ref, table_ref, spectrum_ref, cells_ref, factor_ref
):
    table = Tables(table_ref, place)
    low = lax.broadcasted_iota(jnp.int32, (1, LANES), 1) < LANES // 2

    def padded(index):
        ends = []
        for own in above_below(up_ref[index], down_ref[index]):
            turned = pltpu.roll(own, HALO, 1)
            ends.append(beside(jnp.where(low, 0.0, turned), jnp.where(low, turned, 0.0)))
        return below(ends[0], centre_ref[index], ends[1])

    weight = padded(2)
    mask = mask_of(padded(0), weight)
    cells_ref[0] = padded(1)
    cells_ref[1] = weight
    core = slice(HALO, mask.shape[0] - HALO)
    own = mask[core, core]
    factor_ref[...] = own * (1.0 - own)
    spectrum_ref[...] = spectrum_of(mask, table("analyse_cols"), table("analyse_rows"))


def forward_kernel(
    order,
    place,
    bank_ref,
    spectrum_ref,
    up_margin_ref,
    first_ref,
    table_ref,
    spectra_ref,
    fields_ref,
    tall_ref,
    flat_ref,
):
    grid = 2 * BAND
    fold = LANES // BAND
    per = BAND // fold
    table = Tables(table_ref, place)
    low = lax.broadcasted_iota(jnp.int32, (1, LANES), 1) < LANES // 2
    corner_mask = below(*above_below(up_margin_ref[0], first_ref[:HALO]))

    for row, (device, piece) in enumerate(order):
        both = bank_ref[device, :, piece * LANES : (piece + 1) * LANES]
        for condition in range(CONDITIONS):
            flat_ref[condition, row : row + 1, :] = both[condition : condition + 1]

    lane = lax.broadcasted_iota(jnp.int32, (per, LANES), 1)

    def spread(condition, kernel):
        real = flat_ref[condition, pl.ds(kernel * per, per), :]
        imag = flat_ref[condition, pl.ds((KERNELS + kernel) * per, per), :]
        reals = [real] + [pltpu.roll(real, BAND * s, 1) for s in range(1, fold)]
        imags = [imag] + [pltpu.roll(imag, BAND * s, 1) for s in range(1, fold)]
        rows = []
        for j in range(fold):
            first, second = reals[-j % fold], reals[(1 - j) % fold]
            third, fourth = imags[(2 - j) % fold], imags[(3 - j) % fold]
            rows.append(
                jnp.where(
                    lane < 2 * BAND,
                    jnp.where(lane < BAND, first, second),
                    jnp.where(lane < 3 * BAND, third, fourth),
                )
            )
        return jnp.concatenate(rows, axis=0)

    pairs = [(c, k) for c in range(CONDITIONS) for k in range(KERNELS)]
    spectra = [spread(c, k) for c, k in pairs]

    cols = table("analyse_cols")
    cols = below(cols[:HALO], cols[-HALO:])
    rows = table("analyse_rows").astype(jnp.float32)
    rows = jnp.where(low, rows[:, :LANES], rows[:, LANES:]).astype(jnp.bfloat16)
    spectrum = spectrum_ref[...] + spectrum_of(corner_mask, cols, rows)

    products = below(*[s * spectrum for s in spectra])
    h, m, l = split(products, 3)
    th, tm, tl = [table("field_cols", LANES * index, LANES) for index in range(3)]
    halves = (
        dot(beside(h, m), below(th, th))
        + dot(beside(h, m), below(tm, tm))
        + dot(beside(l, h), below(th, tl))
    )
    halves = split(halves, 3)
    fields = []
    square = 0.0
    for kernel in range(KERNELS):
        parts = []
        for part in halves:
            stacked = []
            for condition in range(CONDITIONS):
                first = (condition * KERNELS + kernel) * BAND
                rows = part[first : first + BAND]
                stacked.append(below(rows[:, :LANES], rows[:, LANES:]))
            parts.append(beside(*stacked))
        field = table.six("field_rows", *parts)
        fields.append(field)
        square = square + field * field

    square = below(*[square[:, c * LANES : (c + 1) * LANES] for c in range(CONDITIONS)])
    square = square + pltpu.roll(square, LANES // 2, 1)
    h, m, l = [part.astype(jnp.float32) for part in split(square, 3)]
    mixed = [jnp.where(low, h, m), jnp.where(low, l, h), jnp.where(low, m, h)]
    th, tm, tl = [table("up_cols", grid * index, grid) for index in range(3)]
    mixed = beside(*[part.astype(jnp.bfloat16) for part in mixed])
    tall = dot(mixed, below(th, th, th, tm, tm, tl))
    tall_ref[...] = tall
    for index, value in enumerate(spectra):
        spectra_ref[index] = value
    for index, value in enumerate(fields):
        fields_ref[index] = value


def backward_kernel(
    place,
    spectra_ref,
    fields_ref,
    tall_ref,
    cells_ref,
    factor_ref,
    up_margin_ref,
    first_ref,
    second_ref,
    table_ref,
    grad_ref,
    sums_ref,
):
    grid = 2 * BAND
    table = Tables(table_ref, place)
    low = lax.broadcasted_iota(jnp.int32, (1, LANES), 1) < LANES // 2
    pad_width = cells_ref.shape[1]
    core = slice(HALO, pad_width - HALO)

    def filled(index):
        cells = cells_ref[index]
        other = (below(first_ref[HALO:], second_ref[: HALO // 2]), second_ref[HALO // 2 :])[index]
        corners = above_below(up_margin_ref[index + 1], other)
        ends = []
        for corner, rows in zip(corners, (cells[:HALO], cells[-HALO:]), strict=True):
            left, right = rows[:, :LANES], rows[:, LANES:]
            ends.append(beside(jnp.where(low, corner, left), jnp.where(low, right, corner)))
        return below(ends[0], cells[core], ends[1])

    target, weight = filled(0), filled(1)
    spectra = [spectra_ref[index] for index in range(CONDITIONS * KERNELS)]
    fields = [fields_ref[index] for index in range(KERNELS)]
    tall = split(tall_ref[...], 3)
    slopes = []
    loss = 0.0
    for condition, dose in enumerate(DOSES):
        parts = [part[condition * grid : (condition + 1) * grid] for part in tall]
        intensity = table.six("up_rows", *parts)
        resist = jax.nn.sigmoid(SHARPNESS * (dose * intensity - THRESHOLD))
        error = resist - target
        scaled = weight * error
        loss = loss + (scaled * error)[core, core]
        slopes.append((2.0 * SHARPNESS * dose) * scaled * (resist * (1.0 - resist)))
    h, l = split(beside(*slopes), 2)
    both = dot(table("down_rows"), h)
    narrow = both[:grid] + (both[grid:] + dot(table("down_rows", 0, grid), l))
    narrow = below(*[narrow[:, c * pad_width : (c + 1) * pad_width] for c in range(CONDITIONS)])
    h, l = split(narrow, 2)
    both = dot(h, table("down_cols"))
    coarse = both[:, :LANES] + (both[:, LANES:] + dot(l, table("down_cols")[:, :LANES]))
    coarse = beside(*[coarse[c * grid : (c + 1) * grid] for c in range(CONDITIONS)])

    backs = [[], []]
    for field in fields:
        h, l = split(field * coarse, 2)
        back = dot(table("back_rows"), below(h, l, h))
        for condition in range(CONDITIONS):
            block = back[:, condition * LANES : (condition + 1) * LANES]
            turned = pltpu.roll(block[BAND:], LANES // 2, 1)
            backs[condition].append(block[:BAND] + jnp.where(low, -turned, turned))
    h, l = split(below(*backs[0], *backs[1]), 2)
    backs = table.three("back_cols", h, l)
    total = 0.0
    for index, spectrum in enumerate(spectra):
        total = total + spectrum * backs[index * BAND : (index + 1) * BAND]

    h, l = split(total, 2)
    across = table.three("core_cols", h, l)
    core_width = across.shape[1] // 2
    h, l = split(below(across[:, :core_width], across[:, core_width:]), 2)
    gradient = dot(table("core_rows"), below(h, l, h))
    cells = gradient * factor_ref[...]
    grad_ref[...] = cells
    square = jnp.sum(jnp.sum(cells * cells, axis=0, keepdims=True), axis=1, keepdims=True)
    loss = jnp.sum(jnp.sum(loss, axis=0, keepdims=True), axis=1, keepdims=True)
    sums = jnp.concatenate([square, loss], axis=0)
    sums_ref[...] = jnp.broadcast_to(sums[None], sums_ref.shape)


def small(megabytes):
    return pltpu.CompilerParams(vmem_limit_bytes=megabytes * 1024 * 1024)


def to_all(value):
    return lax.all_to_all(value, ("row", "col"), 0, 0)


def pair_swap(value, axis, first):
    sizes = lax.axis_size("row"), lax.axis_size("col")
    along = ("row", "col").index(axis)
    pairs = []
    for place in np.ndindex(*sizes):
        other = list(place)
        step = 1 if (place[along] - first) % 2 == 0 else -1
        if 0 <= place[along] + step < sizes[along]:
            other[along] += step
        elif 0 <= place[1 - along] ^ 1 < sizes[1 - along]:
            other[1 - along] ^= 1
        else:
            continue
        pairs.append(tuple(int(r) * sizes[1] + int(c) for r, c in (place, other)))
    return lax.ppermute(value, ("row", "col"), pairs)


def finish(cell_count, own_ref, cells_ref, sums_ref, logits_ref, loss_ref):
    total = jnp.sum(sums_ref[...], axis=0) / cell_count
    scale = STEP / jnp.sqrt(total[0:1] + EPSILON)
    logits_ref[...] = own_ref[0] - cells_ref[...] * scale
    loss_ref[...] = total[1:2, 0:1]


def shards(mask_logits, target, weight, kernels):
    core_width = mask_logits.shape[0]
    pad_width = core_width + 2 * HALO
    rows, cols = lax.axis_size("row"), lax.axis_size("col")
    f32 = jnp.float32

    def struct(*shape):
        return jax.ShapeDtypeStruct(shape, f32)

    packed = struct(core_width * 3 // 2, core_width)
    slab = struct(3, HALO, core_width)
    cells = jnp.concatenate([mask_logits, target, weight], axis=1)
    width = max(cells.shape[1], kernels.shape[1])
    cells, shard = [jnp.pad(a, ((0, 0), (0, width - a.shape[1]))) for a in (cells, kernels)]
    own, slab_a, slab_b, up, down, bank = pl.pallas_call(
        pack,
        out_shape=(struct(3, core_width, core_width), packed, packed, slab, slab)
        + (struct(rows * cols, *kernels.shape),),
        in_specs=[VMEM],
        out_specs=(VMEM,) * 6,
        compiler_params=small(4),
    )(jnp.concatenate([cells, shard], axis=0))
    got_a, got_b = pair_swap(slab_a, "col", 0), pair_swap(slab_b, "col", 1)
    up, down = pair_swap(up, "row", 0), pair_swap(down, "row", 1)
    margin = struct(HALO * 3 // 2, core_width)
    centre, up_margin, first_margin, second_margin = pl.pallas_call(
        widen,
        out_shape=(struct(3, core_width, pad_width), slab, margin, margin),
        in_specs=[VMEM] * 3 + [pl.BlockSpec(memory_space=pl.ANY)],
        out_specs=(VMEM,) * 4,
        compiler_params=small(8),
    )(own, got_a, got_b, down)
    up_margin = pair_swap(up_margin, "row", 0)
    first_margin = pair_swap(first_margin, "row", 1)
    second_margin = pair_swap(second_margin, "row", 1)
    consts, place = tables(pad_width, HALO)
    spectrum, cells, factor = pl.pallas_call(
        functools.partial(before_margins, place),
        out_shape=(
            struct(BAND, LANES),
            struct(2, pad_width, pad_width),
            struct(core_width, core_width),
        ),
        in_specs=[VMEM] * 4,
        out_specs=(VMEM,) * 3,
        compiler_params=small(16),
    )(centre, up, down, consts)
    bank = to_all(bank)
    pieces = kernels.shape[1] // LANES
    if kernels.shape[1] % LANES:
        bank = jnp.swapaxes(bank, 0, 1).reshape(1, CONDITIONS, -1)
        pieces = bank.shape[2] // LANES
    order = [(device, piece) for device in range(bank.shape[0]) for piece in range(pieces)]

    spectra, fields, tall = pl.pallas_call(
        functools.partial(forward_kernel, order, place),
        out_shape=(
            struct(CONDITIONS * KERNELS, BAND, LANES),
            struct(KERNELS, 2 * BAND, 2 * LANES),
            struct(CONDITIONS * 2 * BAND, pad_width),
        ),
        in_specs=[VMEM] * 5,
        out_specs=(VMEM,) * 3,
        scratch_shapes=[pltpu.VMEM((CONDITIONS, len(order), LANES), f32)],
        compiler_params=small(16),
    )(bank, spectrum, up_margin, first_margin, consts)
    grad_cells, sums = pl.pallas_call(
        functools.partial(backward_kernel, place),
        out_shape=(struct(core_width, core_width), struct(rows * cols, 2, LANES)),
        in_specs=[VMEM] * 9,
        out_specs=(VMEM,) * 2,
        compiler_params=small(16),
    )(spectra, fields, tall, cells, factor, up_margin, first_margin, second_margin, consts)

    sums = to_all(sums)
    cell_count = rows * cols * core_width * core_width
    new_logits, loss = pl.pallas_call(
        functools.partial(finish, cell_count),
        out_shape=(struct(core_width, core_width), struct(1, 1)),
        in_specs=[VMEM] * 3,
        out_specs=(VMEM,) * 2,
        compiler_params=small(4),
    )(own, grad_cells, sums)
    return (new_logits, loss[0, 0])


def solution(mesh):
    placed = (P("row", "col"), P("row", "col"), P("row", "col"), P(None, ("row", "col")))
    return jax.shard_map(
        shards, mesh=mesh, in_specs=placed, out_specs=(P("row", "col"), P()), check_vma=False
    )
```

```python
import functools
import math

import jax
import jax.numpy as jnp
import numpy as np
from jax import lax
from jax.experimental import pallas as pl
from jax.experimental.pallas import tpu as pltpu
from jax.sharding import PartitionSpec as P

HALO = 64
KERNELS = 6
BAND = 32
CONDITIONS = 2

SHARPNESS = 6.0
THRESHOLD = 0.75
STEP = 0.5
EPSILON = 1e-06
DOSES = (1.0, 1.15)

LANES = 128
VMEM = pl.BlockSpec(memory_space=pltpu.VMEM)


def dot(first, second):
    return lax.dot_general(
        first, second, (((1,), (0,)), ((), ())), preferred_element_type=jnp.float32
    )


def split(value, count):
    parts = []
    for index in range(count):
        part = value.astype(jnp.bfloat16)
        parts.append(part)
        if index + 1 < count:
            value = value - part.astype(jnp.float32)
    return parts


def split_table(table, count):
    parts = []
    for _ in range(count):
        part = table.astype(np.float32).astype(jnp.bfloat16)
        parts.append(part)
        table = table - part.astype(np.float64)
    return parts


def tables(pad_width, margin):
    freq = np.arange(BAND) - BAND // 2
    place = np.arange(pad_width)
    turns = (freq[:, None] * place[None, :] % pad_width) * (2.0 * math.pi / pad_width)
    wave_re = np.cos(turns) / math.sqrt(pad_width)
    wave_im = -np.sin(turns) / math.sqrt(pad_width)
    grid = 2 * BAND
    stride = pad_width // grid
    fold = LANES // BAND
    rows = np.arange(BAND).reshape(BAND // fold, fold).T.reshape(-1)
    row_re, row_im = wave_re[rows], wave_im[rows]
    coarse_re, coarse_im = wave_re[:, ::stride], wave_im[:, ::stride]
    crow_re, crow_im = row_re[:, ::stride], row_im[:, ::stride]
    core = slice(margin, pad_width - margin)
    core_re, core_im = wave_re[:, core], wave_im[:, core]
    steps = (place[:, None] - stride * np.arange(grid)[None, :]) % pad_width
    diffs = np.arange(1, BAND)
    phases = (steps[..., None] * diffs % pad_width) * (2.0 * math.pi / pad_width)
    between = (1.0 + 2.0 * np.cos(phases).sum(-1)) / grid

    def beside(*blocks):
        return np.concatenate(blocks, axis=1)

    def below(*blocks):
        return np.concatenate(blocks, axis=0)

    found = {}
    h, l = split_table(beside(wave_re.T, wave_im.T, -wave_im.T, wave_re.T), 2)
    found["analyse_cols"] = beside(h, l)
    found["analyse_rows"] = below(*split_table(below(row_re, row_im), 3))
    from_re = beside(coarse_re, -coarse_im, -coarse_im, -coarse_re)
    from_im = beside(coarse_im, coarse_re, coarse_re, -coarse_im)
    h, m, l = split_table(below(from_re, from_im, from_re, from_im), 3)
    found["field_cols"] = below(h, m, l)
    h, m, l = split_table(beside(crow_re.T, crow_im.T), 3)
    found["field_rows"] = beside(h, h, h, m, m, l)
    h, m, l = split_table(between, 3)
    found["up_rows"] = beside(h, h, h, m, m, l)
    found["up_cols"] = below(h.T, m.T, l.T)
    found["down_cols"] = beside(h, h, m, m)
    found["down_rows"] = below(h.T, m.T)
    h, l = split_table(below(crow_re, crow_im), 2)
    found["back_rows"] = beside(h, h, l)
    c_re, c_im = coarse_re.T, coarse_im.T
    h, l = split_table(
        below(beside(c_re, c_im, c_im, -c_re), beside(-c_im, c_re, c_re, c_im)), 2
    )
    found["back_cols"] = below(h, l)
    from_re, from_im = beside(core_re, -core_im), beside(core_im, core_re)
    h, l = split_table(below(from_re, from_im, from_re, from_im), 2)
    found["core_cols"] = below(h, l)
    h, l = split_table(2.0 * beside(row_re[:, core].T, row_im[:, core].T), 2)
    found["core_rows"] = beside(h, h, l)

    pieces = []
    for name, table in found.items():
        for first in range(0, table.shape[1], 2 * LANES):
            pieces.append(((name, first // (2 * LANES)), table[:, first : first + 2 * LANES]))
    where, tops, blocks = {}, [0, 0], []
    for key, piece in sorted(pieces, key=lambda p: (p[1].shape[1] <= LANES, -p[1].shape[0])):
        thin = piece.shape[1] <= LANES
        side = int(thin and tops[1] < tops[0])
        where[key] = (tops[side], side * LANES, piece.shape)
        blocks.append((where[key], piece))
        tops[side] += piece.shape[0]
        if not thin:
            tops[1] = tops[0]
    whole = np.zeros((max(tops), 2 * LANES), jnp.bfloat16)
    for (top, left, shape), piece in blocks:
        whole[top : top + shape[0], left : left + shape[1]] = piece
    return jnp.asarray(whole), where


def pack(held_ref, own_ref, a_ref, b_ref, up_ref, down_ref, bank_ref):
    cells, width = own_ref.shape[1:]
    for index in range(3):
        own_ref[index] = held_ref[:cells, index * width : (index + 1) * width]
    shard = held_ref[cells : cells + CONDITIONS, : bank_ref.shape[2]]
    bank_ref[...] = jnp.broadcast_to(shard[None], bank_ref.shape)
    odd_row = lax.rem(lax.axis_index("row"), 2) == 1
    for index in range(3):
        first, second = own_ref[index, :HALO], own_ref[index, HALO:]
        up_ref[index] = jnp.where(odd_row, first, second)
        down_ref[index] = jnp.where(odd_row, second, first)
    half = HALO
    odd = lax.rem(lax.axis_index("col"), 2) == 1
    values = [own_ref[index] for index in range(3)]
    turned = [pltpu.roll(value, half, 1) for value in values]
    low = lax.broadcasted_iota(jnp.int32, values[0].shape, 1) < half
    rows = values[0].shape[0]
    to_right = [
        jnp.where(low, turned[0], values[1]),
        jnp.where(low[: rows // 2], turned[2][: rows // 2], values[2][rows // 2 :]),
    ]
    to_left = [
        jnp.where(low, values[0], turned[1]),
        jnp.where(low[: rows // 2], values[2][: rows // 2], turned[2][rows // 2 :]),
    ]
    a_ref[:rows] = jnp.where(odd, to_left[0], to_right[0])
    a_ref[rows:] = jnp.where(odd, to_left[1], to_right[1])
    b_ref[:rows] = jnp.where(odd, to_right[0], to_left[0])
    b_ref[rows:] = jnp.where(odd, to_right[1], to_left[1])


def widen(own_ref, a_ref, b_ref, _, centre_ref, up_ref, first_ref, second_ref):
    half = HALO
    odd = lax.rem(lax.axis_index("col"), 2) == 1
    odd_row = lax.rem(lax.axis_index("row"), 2) == 1
    values = [own_ref[index] for index in range(3)]
    rows = values[0].shape[0]
    low = lax.broadcasted_iota(jnp.int32, values[0].shape, 1) < half
    got_a, got_b = a_ref[...], b_ref[...]
    col, cols = lax.axis_index("col"), lax.axis_size("col")
    left = jnp.where(col == 0, 0.0, jnp.where(odd, got_a, got_b))
    right = jnp.where(col == cols - 1, 0.0, jnp.where(odd, got_b, got_a))
    left_turned, right_turned = pltpu.roll(left, half, 1), pltpu.roll(right, half, 1)

    def two(first, second):
        return jnp.concatenate([first, second], axis=0)

    lefts = [left[:rows], left_turned[:rows], two(left[rows:], left_turned[rows:])]
    rights = [right_turned[:rows], right[:rows], two(right_turned[rows:], right[rows:])]
    margins = []
    for index, value in enumerate(values):
        turned = pltpu.roll(value, half, 1)
        wide = jnp.concatenate(
            [jnp.where(low, lefts[index], turned), jnp.where(low, turned, rights[index])], axis=1
        )
        centre_ref[index] = wide
        margins.append(jnp.where(low, wide[:, :LANES], wide[:, LANES:]))
    margins[0] = mask_of(margins[0], margins[2])
    ups, downs = [], []
    for margin in margins:
        ups.append(jnp.where(odd_row, margin[:half], margin[half:]))
        downs.append(jnp.where(odd_row, margin[half:], margin[:half]))
    for index, value in enumerate(ups):
        up_ref[index] = value
    middle = half // 2
    first_ref[:half] = downs[0]
    first_ref[half:] = downs[1][:middle]
    second_ref[:middle] = downs[1][middle:]
    second_ref[middle:] = downs[2]


def beside(*blocks):
    return jnp.concatenate(blocks, axis=1)


def below(*blocks):
    return jnp.concatenate(blocks, axis=0)


class Tables:
    def __init__(self, ref, place):
        self.ref, self.place = ref, place

    def __call__(self, name, first=0, count=None, part=0):
        top, left, shape = self.place[name, part]
        top, count = top + first, shape[0] - first if count is None else count
        return self.ref[top : top + count, left : left + shape[1]]

    def three(self, name, h, l):
        th, tl = self(name, 0, LANES), self(name, LANES)
        return dot(beside(h, l), below(th, th)) + dot(h, tl)

    def six(self, name, h, m, l):
        first = dot(self(name), below(h, m, l, h))
        return first + dot(self(name, part=1), below(m, h))


def above_below(first, second):
    row = lax.axis_index("row")
    odd = lax.rem(row, 2) == 1
    above = jnp.where(row == 0, 0.0, jnp.where(odd, first, second))
    last = row == lax.axis_size("row") - 1
    return above, jnp.where(last, 0.0, jnp.where(odd, second, first))


def spectrum_of(mask, cols, rows):
    grid = 2 * BAND
    low = lax.broadcasted_iota(jnp.int32, (1, LANES), 1) < LANES // 2
    h, l = split(mask, 2)
    both = dot(h, cols)
    half = both[:, :LANES] + both[:, LANES:] + dot(l, cols[:, :LANES])
    h, m, l = split(half, 3)
    both = dot(rows[: 2 * grid], beside(h, m))
    rest = dot(rows[2 * grid :], h) + dot(rows[:grid], l)
    middle = both[:grid, LANES:] + both[grid:, :LANES]
    both = both[:grid, :LANES] + middle + (both[grid:, LANES:] + rest)
    turned = pltpu.roll(both[BAND:], LANES // 2, 1)
    return both[:BAND] + jnp.where(low, turned, -turned)


def mask_of(logits, weight):
    return jnp.where(weight > 0.0, jax.nn.sigmoid(logits), 0.0)


def before_margins(
    place, centre_ref, up_ref, down_ref, table_ref, spectrum_ref, cells_ref, factor_ref
):
    table = Tables(table_ref, place)
    low = lax.broadcasted_iota(jnp.int32, (1, LANES), 1) < LANES // 2

    def padded(index):
        ends = []
        for own in above_below(up_ref[index], down_ref[index]):
            turned = pltpu.roll(own, HALO, 1)
            ends.append(beside(jnp.where(low, 0.0, turned), jnp.where(low, turned, 0.0)))
        return below(ends[0], centre_ref[index], ends[1])

    weight = padded(2)
    mask = mask_of(padded(0), weight)
    cells_ref[0] = padded(1)
    cells_ref[1] = weight
    core = slice(HALO, mask.shape[0] - HALO)
    own = mask[core, core]
    factor_ref[...] = own * (1.0 - own)
    spectrum_ref[...] = spectrum_of(mask, table("analyse_cols"), table("analyse_rows"))


def forward_kernel(
    order,
    place,
    bank_ref,
    spectrum_ref,
    up_margin_ref,
    first_ref,
    table_ref,
    spectra_ref,
    fields_ref,
    tall_ref,
    flat_ref,
):
    grid = 2 * BAND
    fold = LANES // BAND
    per = BAND // fold
    table = Tables(table_ref, place)
    low = lax.broadcasted_iota(jnp.int32, (1, LANES), 1) < LANES // 2
    corner_mask = below(*above_below(up_margin_ref[0], first_ref[:HALO]))

    for row, (device, piece) in enumerate(order):
        both = bank_ref[device, :, piece * LANES : (piece + 1) * LANES]
        for condition in range(CONDITIONS):
            flat_ref[condition, row : row + 1, :] = both[condition : condition + 1]

    lane = lax.broadcasted_iota(jnp.int32, (per, LANES), 1)

    def spread(condition, kernel):
        real = flat_ref[condition, pl.ds(kernel * per, per), :]
        imag = flat_ref[condition, pl.ds((KERNELS + kernel) * per, per), :]
        reals = [real] + [pltpu.roll(real, BAND * s, 1) for s in range(1, fold)]
        imags = [imag] + [pltpu.roll(imag, BAND * s, 1) for s in range(1, fold)]
        rows = []
        for j in range(fold):
            first, second = reals[-j % fold], reals[(1 - j) % fold]
            third, fourth = imags[(2 - j) % fold], imags[(3 - j) % fold]
            rows.append(
                jnp.where(
                    lane < 2 * BAND,
                    jnp.where(lane < BAND, first, second),
                    jnp.where(lane < 3 * BAND, third, fourth),
                )
            )
        return jnp.concatenate(rows, axis=0)

    pairs = [(c, k) for c in range(CONDITIONS) for k in range(KERNELS)]
    spectra = [spread(c, k) for c, k in pairs]

    cols = table("analyse_cols")
    cols = below(cols[:HALO], cols[-HALO:])
    rows = table("analyse_rows").astype(jnp.float32)
    rows = jnp.where(low, rows[:, :LANES], rows[:, LANES:]).astype(jnp.bfloat16)
    spectrum = spectrum_ref[...] + spectrum_of(corner_mask, cols, rows)

    products = below(*[s * spectrum for s in spectra])
    h, m, l = split(products, 3)
    th, tm, tl = [table("field_cols", LANES * index, LANES) for index in range(3)]
    halves = (
        dot(beside(h, m), below(th, th))
        + dot(beside(h, m), below(tm, tm))
        + dot(beside(l, h), below(th, tl))
    )
    halves = split(halves, 3)
    fields = []
    square = 0.0
    for kernel in range(KERNELS):
        parts = []
        for part in halves:
            stacked = []
            for condition in range(CONDITIONS):
                first = (condition * KERNELS + kernel) * BAND
                rows = part[first : first + BAND]
                stacked.append(below(rows[:, :LANES], rows[:, LANES:]))
            parts.append(beside(*stacked))
        field = table.six("field_rows", *parts)
        fields.append(field)
        square = square + field * field

    square = below(*[square[:, c * LANES : (c + 1) * LANES] for c in range(CONDITIONS)])
    square = square + pltpu.roll(square, LANES // 2, 1)
    h, m, l = [part.astype(jnp.float32) for part in split(square, 3)]
    mixed = [jnp.where(low, h, m), jnp.where(low, l, h), jnp.where(low, m, h)]
    th, tm, tl = [table("up_cols", grid * index, grid) for index in range(3)]
    mixed = beside(*[part.astype(jnp.bfloat16) for part in mixed])
    tall = dot(mixed, below(th, th, th, tm, tm, tl))
    tall_ref[...] = tall
    for index, value in enumerate(spectra):
        spectra_ref[index] = value
    for index, value in enumerate(fields):
        fields_ref[index] = value


def backward_kernel(
    place,
    spectra_ref,
    fields_ref,
    tall_ref,
    cells_ref,
    factor_ref,
    up_margin_ref,
    first_ref,
    second_ref,
    table_ref,
    grad_ref,
    sums_ref,
):
    grid = 2 * BAND
    table = Tables(table_ref, place)
    low = lax.broadcasted_iota(jnp.int32, (1, LANES), 1) < LANES // 2
    pad_width = cells_ref.shape[1]
    core = slice(HALO, pad_width - HALO)

    def filled(index):
        cells = cells_ref[index]
        other = (below(first_ref[HALO:], second_ref[: HALO // 2]), second_ref[HALO // 2 :])[index]
        corners = above_below(up_margin_ref[index + 1], other)
        ends = []
        for corner, rows in zip(corners, (cells[:HALO], cells[-HALO:]), strict=True):
            left, right = rows[:, :LANES], rows[:, LANES:]
            ends.append(beside(jnp.where(low, corner, left), jnp.where(low, right, corner)))
        return below(ends[0], cells[core], ends[1])

    target, weight = filled(0), filled(1)
    spectra = [spectra_ref[index] for index in range(CONDITIONS * KERNELS)]
    fields = [fields_ref[index] for index in range(KERNELS)]
    tall = split(tall_ref[...], 3)
    slopes = []
    loss = 0.0
    for condition, dose in enumerate(DOSES):
        parts = [part[condition * grid : (condition + 1) * grid] for part in tall]
        intensity = table.six("up_rows", *parts)
        resist = jax.nn.sigmoid(SHARPNESS * (dose * intensity - THRESHOLD))
        error = resist - target
        scaled = weight * error
        loss = loss + (scaled * error)[core, core]
        slopes.append((2.0 * SHARPNESS * dose) * scaled * (resist * (1.0 - resist)))
    h, l = split(beside(*slopes), 2)
    both = dot(table("down_rows"), h)
    narrow = both[:grid] + (both[grid:] + dot(table("down_rows", 0, grid), l))
    narrow = below(*[narrow[:, c * pad_width : (c + 1) * pad_width] for c in range(CONDITIONS)])
    h, l = split(narrow, 2)
    both = dot(h, table("down_cols"))
    coarse = both[:, :LANES] + (both[:, LANES:] + dot(l, table("down_cols")[:, :LANES]))
    coarse = beside(*[coarse[c * grid : (c + 1) * grid] for c in range(CONDITIONS)])

    backs = [[], []]
    for field in fields:
        h, l = split(field * coarse, 2)
        back = dot(table("back_rows"), below(h, l, h))
        for condition in range(CONDITIONS):
            block = back[:, condition * LANES : (condition + 1) * LANES]
            turned = pltpu.roll(block[BAND:], LANES // 2, 1)
            backs[condition].append(block[:BAND] + jnp.where(low, -turned, turned))
    h, l = split(below(*backs[0], *backs[1]), 2)
    backs = table.three("back_cols", h, l)
    total = 0.0
    for index, spectrum in enumerate(spectra):
        total = total + spectrum * backs[index * BAND : (index + 1) * BAND]

    h, l = split(total, 2)
    across = table.three("core_cols", h, l)
    core_width = across.shape[1] // 2
    h, l = split(below(across[:, :core_width], across[:, core_width:]), 2)
    gradient = dot(table("core_rows"), below(h, l, h))
    cells = gradient * factor_ref[...]
    grad_ref[...] = cells
    square = jnp.sum(jnp.sum(cells * cells, axis=0, keepdims=True), axis=1, keepdims=True)
    loss = jnp.sum(jnp.sum(loss, axis=0, keepdims=True), axis=1, keepdims=True)
    sums_ref[...] = jnp.broadcast_to(jnp.where(low, square, loss)[None], sums_ref.shape)


def small(megabytes):
    return pltpu.CompilerParams(vmem_limit_bytes=megabytes * 1024 * 1024)


def to_all(value):
    return lax.all_to_all(value, ("row", "col"), 0, 0)


def pair_swap(value, axis, first):
    sizes = lax.axis_size("row"), lax.axis_size("col")
    along = ("row", "col").index(axis)
    pairs = []
    for place in np.ndindex(*sizes):
        other = list(place)
        step = 1 if (place[along] - first) % 2 == 0 else -1
        if 0 <= place[along] + step < sizes[along]:
            other[along] += step
        elif 0 <= place[1 - along] ^ 1 < sizes[1 - along]:
            other[1 - along] ^= 1
        else:
            continue
        pairs.append(tuple(int(r) * sizes[1] + int(c) for r, c in (place, other)))
    return lax.ppermute(value, ("row", "col"), pairs)


def finish(cell_count, own_ref, cells_ref, sums_ref, logits_ref, loss_ref):
    total = jnp.sum(sums_ref[...], axis=0) / cell_count
    low = lax.broadcasted_iota(jnp.int32, total.shape, 1) < LANES // 2
    turned = pltpu.roll(total, LANES // 2, 1)
    scale = STEP / jnp.sqrt(jnp.where(low, total, turned) + EPSILON)
    logits_ref[...] = own_ref[0] - cells_ref[...] * scale
    loss_ref[...] = turned[:, 0:1]


def shards(mask_logits, target, weight, kernels):
    core_width = mask_logits.shape[0]
    pad_width = core_width + 2 * HALO
    rows, cols = lax.axis_size("row"), lax.axis_size("col")
    f32 = jnp.float32

    def struct(*shape):
        return jax.ShapeDtypeStruct(shape, f32)

    packed = struct(core_width * 3 // 2, core_width)
    slab = struct(3, HALO, core_width)
    cells = jnp.concatenate([mask_logits, target, weight], axis=1)
    width = max(cells.shape[1], kernels.shape[1])
    cells, shard = [jnp.pad(a, ((0, 0), (0, width - a.shape[1]))) for a in (cells, kernels)]
    own, slab_a, slab_b, up, down, bank = pl.pallas_call(
        pack,
        out_shape=(struct(3, core_width, core_width), packed, packed, slab, slab)
        + (struct(rows * cols, *kernels.shape),),
        in_specs=[VMEM],
        out_specs=(VMEM,) * 6,
        compiler_params=small(4),
    )(jnp.concatenate([cells, shard], axis=0))
    got_a, got_b = pair_swap(slab_a, "col", 0), pair_swap(slab_b, "col", 1)
    up, down = pair_swap(up, "row", 0), pair_swap(down, "row", 1)
    margin = struct(HALO * 3 // 2, core_width)
    centre, up_margin, first_margin, second_margin = pl.pallas_call(
        widen,
        out_shape=(struct(3, core_width, pad_width), slab, margin, margin),
        in_specs=[VMEM] * 3 + [pl.BlockSpec(memory_space=pl.ANY)],
        out_specs=(VMEM,) * 4,
        compiler_params=small(8),
    )(own, got_a, got_b, down)
    up_margin = pair_swap(up_margin, "row", 0)
    first_margin = pair_swap(first_margin, "row", 1)
    second_margin = pair_swap(second_margin, "row", 1)
    consts, place = tables(pad_width, HALO)
    spectrum, cells, factor = pl.pallas_call(
        functools.partial(before_margins, place),
        out_shape=(
            struct(BAND, LANES),
            struct(2, pad_width, pad_width),
            struct(core_width, core_width),
        ),
        in_specs=[VMEM] * 4,
        out_specs=(VMEM,) * 3,
        compiler_params=small(16),
    )(centre, up, down, consts)
    bank = to_all(bank)
    pieces = kernels.shape[1] // LANES
    if kernels.shape[1] % LANES:
        bank = jnp.swapaxes(bank, 0, 1).reshape(1, CONDITIONS, -1)
        pieces = bank.shape[2] // LANES
    order = [(device, piece) for device in range(bank.shape[0]) for piece in range(pieces)]

    spectra, fields, tall = pl.pallas_call(
        functools.partial(forward_kernel, order, place),
        out_shape=(
            struct(CONDITIONS * KERNELS, BAND, LANES),
            struct(KERNELS, 2 * BAND, 2 * LANES),
            struct(CONDITIONS * 2 * BAND, pad_width),
        ),
        in_specs=[VMEM] * 5,
        out_specs=(VMEM,) * 3,
        scratch_shapes=[pltpu.VMEM((CONDITIONS, len(order), LANES), f32)],
        compiler_params=small(16),
    )(bank, spectrum, up_margin, first_margin, consts)
    grad_cells, sums = pl.pallas_call(
        functools.partial(backward_kernel, place),
        out_shape=(struct(core_width, core_width), struct(rows * cols, 1, LANES)),
        in_specs=[VMEM] * 9,
        out_specs=(VMEM,) * 2,
        compiler_params=small(16),
    )(spectra, fields, tall, cells, factor, up_margin, first_margin, second_margin, consts)

    sums = to_all(sums)
    cell_count = rows * cols * core_width * core_width
    new_logits, loss = pl.pallas_call(
        functools.partial(finish, cell_count),
        out_shape=(struct(core_width, core_width), struct(1, 1)),
        in_specs=[VMEM] * 3,
        out_specs=(VMEM,) * 2,
        compiler_params=small(4),
    )(own, grad_cells, sums)
    return (new_logits, loss[0, 0])


def solution(mesh):
    placed = (P("row", "col"), P("row", "col"), P("row", "col"), P(None, ("row", "col")))
    return jax.shard_map(
        shards, mesh=mesh, in_specs=placed, out_specs=(P("row", "col"), P()), check_vma=False
    )
```
